32 devices in a mesh: fsdp: 4 (over y, x), tok: 8 (over z, core).
Axes of the slice: x: 2, y: 2, z: 4, core: 2. Of those that a mesh axis runs over, the one named last changes fastest.
Arguments:
- tokens: bfloat16 [8192, 8192], P(('fsdp', 'tok')), may hold values from -6 to 6
- frozen_value_weight: bfloat16 [8192, 1024], P(None, 'fsdp'), may hold values from -0.0625 to 0.0625
- adapter_down_maps: bfloat16 [8192, 4096], P('tok', 'fsdp'), may hold values from -0.0625 to 0.0625
- adapter_up_maps: bfloat16 [1024, 4096], P('tok', 'fsdp'), may hold values from -1.5 to 1.5
- cotangent: bfloat16 [8192, 1024], P(('fsdp', 'tok')), may hold values from -6 to 6
- packing_block_tenant: int32 [64], replicated, may hold values from 0 to 255
- packing_block_fill: int32 [64], replicated, may hold values from 1 to 128
Outputs:
- values: bfloat16 [8192, 1024], P(('fsdp', 'tok'))
- token_gradient: bfloat16 [8192, 8192], P(('fsdp', 'tok'))
- grad_down: float32 [8192, 4096], P('tok', 'fsdp')
- grad_up: float32 [1024, 4096], P('tok', 'fsdp')
The draws below stay inside these ranges and needn't reach their ends.
All inputs are finite; a program needn't handle non-finite values.
Results may differ from the reference program's by a relative error of at most 0.0055.
Values may be sent and summed in bfloat16 or wider, within the bound.
No kernel may reach another device: no remote copies, remote signals or barrier semaphores. Data moves between devices by JAX's collectives and lax.ppermute only.
A program may use at most 128 MiB of HBM per device.

```python
import math
import jax
import jax.numpy as jnp
import numpy as np
from jax import lax

MODEL_WIDTH = 8192
VALUE_WIDTH = 1024
ADAPTER_RANK = 16
TENANT_COUNT = 256
BLOCK = 128
TOKENS = 8192
BLOCKS = 64


def draw_packing_block_fill(key, part):
    key = jax.random.fold_in(key, 7)
    fill_key, chosen_key = jax.random.split(key)
    fill_values = jax.random.randint(fill_key, (BLOCKS,), 1, BLOCK + 1)
    chosen = jax.random.randint(chosen_key, (), 0, BLOCKS)
    positions = jnp.arange(BLOCKS)
    fill_values = jnp.where(positions == chosen, BLOCK, fill_values)
    fill_values = jnp.where(positions == (chosen + BLOCKS // 2) % BLOCKS, 1, fill_values)
    return fill_values.astype(jnp.int32)


def plant(drawn, own_key, least, high):
    shape = drawn.shape
    place = [jax.random.randint(jax.random.fold_in(own_key, axis), (), 0, shape[axis]) for axis in range(len(shape))]
    drawn = drawn.at[tuple(place)].set(least)
    longest = shape.index(max(shape))
    place[longest] = (place[longest] + 1) % shape[longest]
    return drawn.at[tuple(place)].set(high)


def block_levels(own_key, dims, cuts, smallest, largest):
    def one(position, parts):
        heights = jax.random.uniform(jax.random.fold_in(jax.random.fold_in(own_key, 6), position), (parts,), jnp.float32, smallest / len(cuts), largest / len(cuts))
        return jnp.repeat(jnp.exp(heights), dims[position] // parts).reshape((-1,) + (1,) * (len(dims) - position - 1))

    loudness = one(*cuts[0])
    for cut in cuts[1:]:
        loudness = loudness * one(*cut)
    return loudness


def rank_bounds(count, lean):
    loads = [(1 << 20) // math.isqrt(rank ** lean) + 1 for rank in range(1, count + 1)]
    spread = 1 + sum(loads) // (1 << 30)
    return np.cumsum(np.array([max(1, weight // spread) for weight in loads]))


def skewed_ids(rng, extent, number_of, skew):
    grid = rank_bounds(number_of, skew)
    lot = jax.random.randint(jax.random.fold_in(rng, 1), extent, 0, int(grid[number_of - 1]))
    rank = jnp.searchsorted(jnp.asarray(grid, jnp.int32), lot, side="right")
    return jax.random.permutation(jax.random.fold_in(rng, 2), number_of)[rank].astype(jnp.int32)


def scatter_about(stream_key, shape, width, bound, shards=(), kind=jnp.bfloat16):
    entries = jax.random.normal(stream_key, shape, jnp.float32) * width
    if len(shards) > 0:
        entries = block_levels(stream_key, shape, shards, -0.22, 0.18) * entries
    return jnp.clip(entries, min=-bound, max=bound).astype(kind)


def setup_inputs(seed: int = 0) -> dict:
    streams_of = jax.random.split(jax.random.key(seed), 8)
    return {
        "tokens": scatter_about(streams_of[0], (TOKENS, MODEL_WIDTH), 1.0, 6.0, ((0, 32),)),
        "frozen_value_weight": scatter_about(streams_of[1], (MODEL_WIDTH, VALUE_WIDTH), MODEL_WIDTH ** -0.5, 0.0625, ((1, 4),)),
        "adapter_down_maps": scatter_about(streams_of[2], (MODEL_WIDTH, TENANT_COUNT * ADAPTER_RANK), MODEL_WIDTH ** -0.5, 0.0625, ((0, 8), (1, 4))),
        "adapter_up_maps": scatter_about(streams_of[3], (VALUE_WIDTH, TENANT_COUNT * ADAPTER_RANK), ADAPTER_RANK ** -0.5, 1.5, ((0, 8), (1, 4))),
        "cotangent": scatter_about(streams_of[4], (TOKENS, VALUE_WIDTH), 1.0, 6.0, ((0, 32),)),
        "packing_block_tenant": plant(skewed_ids(streams_of[5], (BLOCKS,), TENANT_COUNT, 2), jax.random.fold_in(streams_of[5], 3), 0, TENANT_COUNT - 1).astype(jnp.int32),
        "packing_block_fill": draw_packing_block_fill(jax.random.fold_in(streams_of[7], 71), 0),
    }


ADAPTER_SCALE = 2.0


def reference(tokens, frozen_value_weight, adapter_down_maps, adapter_up_maps, cotangent, packing_block_tenant, packing_block_fill):
    filled_row_count = tokens.shape[0]
    blocks = filled_row_count // BLOCK
    used_rows = (jnp.arange(BLOCK, dtype=jnp.int32)[None, :] < packing_block_fill[:, None]).reshape(filled_row_count, 1)
    grad_out = cotangent * used_rows.astype(cotangent.dtype)
    feature_blocks = tokens.reshape(blocks, BLOCK, MODEL_WIDTH)
    gradient_blocks = grad_out.reshape(blocks, BLOCK, VALUE_WIDTH)

    def per_block_step(totals, inputs_now):
        down_gradient_total, up_gradient_total = totals
        feat_rows, grad_rows, tenant = inputs_now
        column_offset = (tenant * ADAPTER_RANK).astype(jnp.int32)
        down_map_columns = lax.dynamic_slice_in_dim(adapter_down_maps, column_offset, ADAPTER_RANK, 1)
        up_map_columns = lax.dynamic_slice_in_dim(adapter_up_maps, column_offset, ADAPTER_RANK, 1)
        rank_space_input = jnp.dot(feat_rows, down_map_columns, preferred_element_type=jnp.float32).astype(jnp.bfloat16)
        rank_space_gradient = (ADAPTER_SCALE * jnp.dot(grad_rows, up_map_columns, preferred_element_type=jnp.float32)).astype(jnp.bfloat16)
        adapter_output = (ADAPTER_SCALE * jnp.dot(rank_space_input, up_map_columns.T, preferred_element_type=jnp.float32)).astype(jnp.bfloat16)
        adapter_backward = jnp.dot(rank_space_gradient, down_map_columns.T, preferred_element_type=jnp.float32).astype(jnp.bfloat16)
        down_term = jnp.dot(feat_rows.T, rank_space_gradient, preferred_element_type=jnp.float32)
        up_term = ADAPTER_SCALE * jnp.dot(grad_rows.T, rank_space_input, preferred_element_type=jnp.float32)
        old_down = lax.dynamic_slice_in_dim(down_gradient_total, column_offset, ADAPTER_RANK, 1)
        down_gradient_total = lax.dynamic_update_slice_in_dim(down_gradient_total, old_down + down_term, column_offset, 1)
        old_up = lax.dynamic_slice_in_dim(up_gradient_total, column_offset, ADAPTER_RANK, 1)
        up_gradient_total = lax.dynamic_update_slice_in_dim(up_gradient_total, old_up + up_term, column_offset, 1)
        return (down_gradient_total, up_gradient_total), (adapter_output, adapter_backward)

    initial_totals = (jnp.zeros((MODEL_WIDTH, TENANT_COUNT * ADAPTER_RANK), jnp.float32), jnp.zeros((VALUE_WIDTH, TENANT_COUNT * ADAPTER_RANK), jnp.float32))
    (down_gradient_total, up_gradient_total), (adapter_output, adapter_backward) = lax.scan(per_block_step, initial_totals, (feature_blocks, gradient_blocks, packing_block_tenant))
    masked_token_rows = used_rows.astype(jnp.float32)
    frozen_output = jnp.dot(tokens, frozen_value_weight, preferred_element_type=jnp.float32)
    values = (masked_token_rows * (frozen_output + adapter_output.reshape(filled_row_count, VALUE_WIDTH).astype(jnp.float32))).astype(jnp.bfloat16)
    frozen_backward = jnp.dot(grad_out, frozen_value_weight.T, preferred_element_type=jnp.float32)
    token_gradient = (frozen_backward + adapter_backward.reshape(filled_row_count, MODEL_WIDTH).astype(jnp.float32)).astype(jnp.bfloat16)
    counts = jax.ops.segment_sum(packing_block_fill.astype(jnp.float32), packing_block_tenant, num_segments=TENANT_COUNT)
    denominator = jnp.repeat(jnp.maximum(counts, 1.0), ADAPTER_RANK)
    return values, token_gradient, down_gradient_total / denominator, up_gradient_total / denominator
```

```python
import functools

import jax
import jax.numpy as jnp
from jax import lax
from jax.experimental import pallas as pl
from jax.experimental.pallas import tpu as pltpu
from jax.sharding import PartitionSpec as P

ADAPTER_RANK = 16
TENANT_COUNT = 256
BLOCK = 128
ADAPTER_SCALE = 2.0
CHUNKS = 4
VMEM_LIMIT = 48 * 1024 * 1024

F32 = jnp.float32
BF16 = jnp.bfloat16
NT = (((1,), (1,)), ((), ()))
TN = (((0,), (0,)), ((), ()))
SMEM = pl.BlockSpec(memory_space=pltpu.SMEM)
VMEM = pl.BlockSpec(memory_space=pltpu.VMEM)


def dot(a, b, dims=(((1,), (0,)), ((), ()))):
    return lax.dot_general(a, b, dims, preferred_element_type=F32)


def block_rows(tenant_ref, block, shard, columns):
    base = tenant_ref[block] * ADAPTER_RANK - shard * columns
    lane = lax.broadcasted_iota(jnp.int32, (ADAPTER_RANK, columns), 1)
    row = lax.broadcasted_iota(jnp.int32, (ADAPTER_RANK, columns), 0)
    return jnp.where(lane - row == base, 1.0, 0.0)


def fill_pick(tenant_ref, pick_ref, row, first_block, count, shard):
    columns = pick_ref.shape[1]

    @pl.loop(0, count)
    def _(n):
        start = pl.multiple_of(row + n * ADAPTER_RANK, ADAPTER_RANK)
        rows = block_rows(tenant_ref, first_block + n, shard, columns)
        pick_ref[pl.ds(start, ADAPTER_RANK), :] = rows.astype(BF16)


def picked(pick_ref, down_ref, up_ref, out_ref):
    cut = down_ref.shape[0]
    out_ref[:, :cut] = dot(pick_ref[...], down_ref[...], NT).astype(BF16)
    out_ref[:, cut:] = dot(pick_ref[...], up_ref[...], NT).astype(BF16)


def send_select_kernel(group, where_ref, tenant_ref, down_ref, up_ref, x_ref, y_ref, pick_ref):
    here = where_ref[0]
    half = group // 2
    rows = half * ADAPTER_RANK
    for out_ref, part, others in ((x_ref, 0, (1, 3)), (y_ref, half, (2, 3))):
        for place, other in enumerate(others):
            first = (here ^ other) * group + part
            fill_pick(tenant_ref, pick_ref, place * rows, first, half, here)
        picked(pick_ref, down_ref, up_ref, out_ref)


def keep_select_kernel(
    group, where_ref, tenant_ref, down_ref, up_ref, x_ref, y_ref, keep_ref, on_y_ref, on_x_ref, pick_ref, part_ref
):
    here = where_ref[0]
    half = group // 2
    rows = half * ADAPTER_RANK
    for n, (came_ref, part, others, on_ref) in enumerate(
        ((x_ref, 0, (0, 2), on_y_ref), (y_ref, half, (0, 1), on_x_ref))
    ):
        for place, other in enumerate(others):
            first = (here ^ other) * group + part
            fill_pick(tenant_ref, pick_ref, place * rows, first, half, here)
        picked(pick_ref, down_ref, up_ref, part_ref)
        keep_ref[n * rows : (n + 1) * rows, :] = part_ref[:rows, :] + came_ref[:rows, :]
        on_ref[...] = part_ref[rows:, :] + came_ref[rows:, :]


def rank_kernel(
    where_ref, fill_ref, tokens_ref, cot_ref, maps_ref, grad_ref, at_ref, rg_ref, lora_ref, terms_ref, up_ref
):
    rows, width = cot_ref.shape
    shards, rank, both = maps_ref.shape
    cut = tokens_ref.shape[1] // shards
    blocks = rows // BLOCK
    first = where_ref[2]
    for n in range(blocks):
        row = lax.broadcasted_iota(jnp.int32, (BLOCK, width), 0)
        part = cot_ref[n * BLOCK : (n + 1) * BLOCK, :]
        grad_ref[n * BLOCK : (n + 1) * BLOCK, :] = jnp.where(
            row < fill_ref[first + n], part, jnp.zeros_like(part)
        )
    for s in range(shards):
        up_ref[:, s * (both - cut) : (s + 1) * (both - cut)] = maps_ref[s, :, cut:]
        at_ref[:, s * cut : (s + 1) * cut] = maps_ref[s, :, :cut]
    own = (
        lax.broadcasted_iota(jnp.int32, (rows, rank), 0) // BLOCK
        == lax.broadcasted_iota(jnp.int32, (rows, rank), 1) // ADAPTER_RANK
    )
    grad = grad_ref[...]
    rank_grad = jnp.where(own, ADAPTER_SCALE * dot(grad, up_ref[...], NT), 0.0).astype(BF16)
    rg_ref[...] = rank_grad
    rank_in = jnp.where(own, dot(tokens_ref[...], at_ref[...], NT), 0.0).astype(BF16)
    lora_ref[...] = (ADAPTER_SCALE * dot(rank_in, up_ref[...])).astype(BF16).astype(F32)
    up_terms = (ADAPTER_SCALE * dot(rank_in, grad, TN)).astype(BF16)
    for s in range(shards):
        terms_ref[s, :, :cut] = dot(rank_grad, tokens_ref[:, s * cut : (s + 1) * cut], TN).astype(BF16)
        terms_ref[s, :, cut:] = up_terms[:, s * (both - cut) : (s + 1) * (both - cut)]


def chunk_kernel(
    steps, final, where_ref, fill_ref, tokens_ref, own_ref, near_ref, far_ref, mine_ref, theirs_ref,
    at_ref, grad_ref, rg_ref, sum_ref, *refs
):
    out_ref, total_ref = refs[-3:-1] if final else refs[-2:]
    acc_ref = refs[-1]
    i = pl.program_id(0)
    here, core = where_ref[0], where_ref[1]
    wide = own_ref.shape[1]

    @pl.when(i == 0)
    def _():
        acc_ref[...] = sum_ref[...]

    last = jnp.where(i < steps // 2, mine_ref[...], theirs_ref[...])
    tokens = tokens_ref[...]
    back = dot(rg_ref[...], at_ref[...]).astype(BF16).astype(F32)
    for other, weight in (
        (here, own_ref[...]),
        (here ^ (1 + core), near_ref[...]),
        (here ^ (2 - core), far_ref[...]),
        (here ^ 3, last),
    ):
        place = pl.ds(pl.multiple_of(other * wide, wide), wide)
        back += dot(grad_ref[:, place], weight, NT)
        acc_ref[:, place] += dot(tokens, weight)
    out_ref[...] = back.astype(BF16)

    if final:
        first = where_ref[2]

        @pl.when(i == steps - 1)
        def _():
            for n in range(total_ref.shape[0] // BLOCK):
                part = acc_ref[n * BLOCK : (n + 1) * BLOCK, :]
                row = lax.broadcasted_iota(jnp.int32, part.shape, 0)
                total_ref[n * BLOCK : (n + 1) * BLOCK, :] = jnp.where(
                    row < fill_ref[first + n], part, 0.0
                ).astype(BF16)


def expand_kernel(
    group, where_ref, tenant_ref, fill_ref, r0_ref, r1_ref, r2_ref, r3a_ref, r3b_ref,
    down_ref, up_ref, pick_ref, scale_ref
):
    here = where_ref[0]
    columns = down_ref.shape[1]
    rows = group * ADAPTER_RANK
    scale_ref[...] = jnp.zeros_like(scale_ref)
    for place in range(4):
        first = (here ^ place) * group

        @pl.loop(0, group)
        def _(n):
            start = pl.multiple_of(place * rows + n * ADAPTER_RANK, ADAPTER_RANK)
            part = block_rows(tenant_ref, first + n, here, columns)
            pick_ref[pl.ds(start, ADAPTER_RANK), :] = part.astype(BF16)
            scale_ref[...] += part * fill_ref[first + n].astype(F32)

    scale = 1.0 / jnp.maximum(jnp.sum(scale_ref[...], axis=0, keepdims=True), 1.0)
    cut = down_ref.shape[0]
    both = r0_ref.shape[1]

    def sums(lo, hi):
        total = dot(r0_ref[:, lo:hi], pick_ref[:rows, :], TN)
        total += dot(r1_ref[:, lo:hi], pick_ref[rows : 2 * rows, :], TN)
        total += dot(r2_ref[:, lo:hi], pick_ref[2 * rows : 3 * rows, :], TN)
        total += dot(r3a_ref[:, lo:hi], pick_ref[3 * rows : 3 * rows + rows // 2, :], TN)
        total += dot(r3b_ref[:, lo:hi], pick_ref[3 * rows + rows // 2 :, :], TN)
        return total * scale

    step = min(cut, 256)
    for lo in range(0, cut, step):
        down_ref[lo : lo + step, :] = sums(lo, lo + step)
    up_ref[...] = sums(cut, both)


def params(**extra):
    return pltpu.CompilerParams(vmem_limit_bytes=VMEM_LIMIT, **extra)


def shape(*dims, dtype=BF16):
    return jax.ShapeDtypeStruct(dims, dtype)


def local(tokens, weight, down_maps, up_maps, cotangent, tenants, fills):
    shards = lax.axis_size("tok")
    groups = lax.axis_size("fsdp")
    rows, model = tokens.shape
    value = cotangent.shape[1]
    wide = weight.shape[1]
    cut, columns = down_maps.shape
    both = cut + up_maps.shape[0]
    dev_blocks = rows // BLOCK
    group = dev_blocks * shards
    rank = dev_blocks * ADAPTER_RANK
    group_rank = group * ADAPTER_RANK
    here = lax.axis_index("fsdp")
    tok_here = lax.axis_index("tok")
    core = tok_here % 2
    where = jnp.stack([here, core, (here * shards + tok_here) * dev_blocks]).astype(jnp.int32)

    def over(axis, flip):
        return lambda a: lax.ppermute(a, axis, [(i, i ^ flip) for i in range(lax.axis_size(axis))])

    on_x, on_y, on_core = over("fsdp", 1), over("fsdp", 2), over("tok", 1)

    def split(first, second):
        pairs = [
            (f * shards + t, (f ^ (second if t % 2 else first)) * shards + t)
            for f in range(groups)
            for t in range(shards)
        ]
        return lambda a: lax.ppermute(a, ("fsdp", "tok"), pairs)

    to_x, to_y = pl.pallas_call(
        functools.partial(send_select_kernel, group),
        out_shape=[shape(group_rank, both)] * 2,
        in_specs=[SMEM, SMEM, VMEM, VMEM],
        out_specs=[VMEM, VMEM],
        scratch_shapes=[pltpu.VMEM((group_rank, columns), BF16)],
        compiler_params=params(),
        name="select_sent",
    )(where, tenants, down_maps, up_maps)
    came_x, came_y = on_x(to_x), on_y(to_y)
    keep, on_y_next, on_x_next = pl.pallas_call(
        functools.partial(keep_select_kernel, group),
        out_shape=[shape(group_rank, both)] + [shape(group_rank // 2, both)] * 2,
        in_specs=[SMEM, SMEM, VMEM, VMEM, VMEM, VMEM],
        out_specs=[VMEM] * 3,
        scratch_shapes=[pltpu.VMEM((group_rank, columns), BF16), pltpu.VMEM((group_rank, both), BF16)],
        compiler_params=params(),
        name="select_kept",
    )(where, tenants, down_maps, up_maps, came_x, came_y)
    maps = keep + jnp.concatenate([on_y(on_y_next), on_x(on_x_next)], axis=0)
    maps = lax.all_to_all(maps.reshape(shards, rank, both), "tok", split_axis=0, concat_axis=0)

    chunk_rows = model // CHUNKS
    arrived = []
    for k in range(CHUNKS):
        own = lax.slice_in_dim(weight, k * chunk_rows, (k + 1) * chunk_rows, axis=0)
        near = split(1, 2)(own)
        far = on_core(near)
        half = chunk_rows // 2
        mine = split(2, 1)(lax.dynamic_slice_in_dim(near, core * half, half, axis=0))
        arrived.append((near, far, mine, on_core(mine)))

    grad, at, rank_grad, lora, terms = pl.pallas_call(
        rank_kernel,
        out_shape=[
            shape(rows, value),
            shape(rank, model),
            shape(rows, rank),
            shape(rows, value, dtype=F32),
            shape(shards, rank, both),
        ],
        in_specs=[SMEM, SMEM, VMEM, VMEM, VMEM],
        out_specs=[VMEM] * 5,
        scratch_shapes=[pltpu.VMEM((rank, value), BF16)],
        compiler_params=params(),
        name="rank_space",
    )(where, fills, tokens, cotangent, maps)

    r0 = lax.all_to_all(terms, "tok", split_axis=0, concat_axis=0).reshape(group_rank, both)
    r1, r2 = on_x(r0), on_y(r0)
    r3a, r3b = on_y(r1[: group_rank // 2]), on_x(r2[group_rank // 2 :])

    tile = 512
    steps = chunk_rows // tile
    total, token_gradient = lora, None
    for k, (near, far, mine, theirs) in enumerate(arrived):
        final = k == CHUNKS - 1

        def turned(i, where_ref):
            return (i + where_ref[1] * (steps // 2)) % steps

        def spot(i, w, f, k=k):
            return k * steps + turned(i, w)

        whole = lambda i, w, f: (0, 0)
        in_specs = [
            pl.BlockSpec((rows, tile), lambda i, w, f, spot=spot: (0, spot(i, w, f))),
            pl.BlockSpec((tile, wide), lambda i, w, f, spot=spot: (spot(i, w, f), 0)),
            pl.BlockSpec((tile, wide), lambda i, w, f: (turned(i, w), 0)),
            pl.BlockSpec((tile, wide), lambda i, w, f: (turned(i, w), 0)),
            pl.BlockSpec((tile, wide), lambda i, w, f: (jnp.minimum(i, steps // 2 - 1), 0)),
            pl.BlockSpec((tile, wide), lambda i, w, f: (jnp.maximum(i - steps // 2, 0), 0)),
            pl.BlockSpec((rank, tile), lambda i, w, f, spot=spot: (0, spot(i, w, f))),
            pl.BlockSpec((rows, value), whole),
            pl.BlockSpec((rows, rank), whole),
            pl.BlockSpec((rows, value), whole),
        ]
        operands = [where, fills, tokens, weight, near, far, mine, theirs, at, grad, rank_grad, total]
        aliases = {}
        if token_gradient is not None:
            in_specs.append(pl.BlockSpec(memory_space=pl.ANY))
            aliases = {len(operands): 0}
            operands.append(token_gradient)
        token_gradient, total = pl.pallas_call(
            functools.partial(chunk_kernel, steps, final),
            out_shape=[shape(rows, model), shape(rows, value, dtype=BF16 if final else F32)],
            grid_spec=pltpu.PrefetchScalarGridSpec(
                num_scalar_prefetch=2,
                grid=(steps,),
                in_specs=in_specs,
                out_specs=[
                    pl.BlockSpec((rows, tile), lambda i, w, f, spot=spot: (0, spot(i, w, f))),
                    pl.BlockSpec((rows, value), whole),
                ],
                scratch_shapes=[pltpu.VMEM((rows, value), F32)] if final else [],
            ),
            input_output_aliases=aliases,
            compiler_params=params(dimension_semantics=("arbitrary",)),
            cost_estimate=pl.CostEstimate(
                flops=4 * rows * chunk_rows * value,
                bytes_accessed=2 * chunk_rows * (2 * rows + value) + 8 * rows * value,
                transcendentals=0,
            ),
            name="base_chunk",
        )(*operands)

    grad_down, grad_up = pl.pallas_call(
        functools.partial(expand_kernel, group),
        out_shape=[shape(cut, columns, dtype=F32), shape(both - cut, columns, dtype=F32)],
        in_specs=[SMEM, SMEM, SMEM] + [VMEM] * 5,
        out_specs=[VMEM, VMEM],
        scratch_shapes=[
            pltpu.VMEM((groups * group_rank, columns), BF16),
            pltpu.VMEM((ADAPTER_RANK, columns), F32),
        ],
        compiler_params=params(),
        name="expand",
    )(where, tenants, fills, r0, r1, r2, r3a, r3b)
    return total, token_gradient, grad_down, grad_up


def solution(mesh):
    placed = (
        P(("fsdp", "tok"), None),
        P(None, "fsdp"),
        P("tok", "fsdp"),
        P("tok", "fsdp"),
        P(("fsdp", "tok"), None),
        P(),
        P(),
    )
    return jax.shard_map(
        local,
        mesh=mesh,
        in_specs=placed,
        out_specs=(
            P(("fsdp", "tok"), None),
            P(("fsdp", "tok"), None),
            P("tok", "fsdp"),
            P("tok", "fsdp"),
        ),
        check_vma=False,
    )
```

```python
import functools

import jax
import jax.numpy as jnp
from jax import lax
from jax.experimental import pallas as pl
from jax.experimental.pallas import tpu as pltpu
from jax.sharding import PartitionSpec as P

ADAPTER_RANK = 16
TENANT_COUNT = 256
BLOCK = 128
ADAPTER_SCALE = 2.0
CHUNKS = (2, 2, 2, 2)
VMEM_LIMIT = 48 * 1024 * 1024

F32 = jnp.float32
BF16 = jnp.bfloat16
NT = (((1,), (1,)), ((), ()))
TN = (((0,), (0,)), ((), ()))
SMEM = pl.BlockSpec(memory_space=pltpu.SMEM)
VMEM = pl.BlockSpec(memory_space=pltpu.VMEM)
ANY = pl.BlockSpec(memory_space=pl.ANY)


def dot(a, b, dims=(((1,), (0,)), ((), ()))):
    return lax.dot_general(a, b, dims, preferred_element_type=F32)


def block_rows(tenant_ref, block, shard, columns):
    base = tenant_ref[block] * ADAPTER_RANK - shard * columns
    lane = lax.broadcasted_iota(jnp.int32, (ADAPTER_RANK, columns), 1)
    row = lax.broadcasted_iota(jnp.int32, (ADAPTER_RANK, columns), 0)
    return jnp.where(lane - row == base, 1.0, 0.0)


def fill_pick(tenant_ref, pick_ref, row, first_block, count, shard):
    columns = pick_ref.shape[1]

    @pl.loop(0, count)
    def _(n):
        start = pl.multiple_of(row + n * ADAPTER_RANK, ADAPTER_RANK)
        rows = block_rows(tenant_ref, first_block + n, shard, columns)
        pick_ref[pl.ds(start, ADAPTER_RANK), :] = rows.astype(BF16)


def picked(pick_ref, down_ref, up_ref, out_ref):
    cut = down_ref.shape[0]
    out_ref[:, :cut] = dot(pick_ref[...], down_ref[...], NT).astype(BF16)
    out_ref[:, cut:] = dot(pick_ref[...], up_ref[...], NT).astype(BF16)


def pick_two(group, tenant_ref, pick_ref, here, others):
    for place, other in enumerate(others):
        fill_pick(tenant_ref, pick_ref, place * group * ADAPTER_RANK, (here ^ other) * group, group, here)


def send_select_kernel(group, size, where_ref, tenant_ref, weight_ref, down_ref, up_ref, out_ref, piece_ref, pick_ref, sem):
    copy = pltpu.make_async_copy(weight_ref.at[pl.ds(0, size), :], piece_ref, sem)
    copy.start()
    here, core = where_ref[0], where_ref[1]
    pick_two(group, tenant_ref, pick_ref, here, (1 + core, 3))
    picked(pick_ref, down_ref, up_ref, out_ref)
    copy.wait()


def keep_select_kernel(group, where_ref, tenant_ref, down_ref, up_ref, out_ref, pick_ref):
    here, core = where_ref[0], where_ref[1]
    pick_two(group, tenant_ref, pick_ref, here, (0, 2 - core))
    picked(pick_ref, down_ref, up_ref, out_ref)


def cut_kernel(start, where_ref, near_ref, weight_ref, half_ref, piece_ref, sems):
    half = half_ref.shape[0]
    at = pl.multiple_of(where_ref[1] * half, half)
    copies = [
        pltpu.make_async_copy(near_ref.at[pl.ds(at, half), :], half_ref, sems.at[0]),
        pltpu.make_async_copy(weight_ref.at[pl.ds(start, piece_ref.shape[0]), :], piece_ref, sems.at[1]),
    ]
    for copy in copies:
        copy.start()
    for copy in copies:
        copy.wait()


def rank_kernel(
    where_ref, fill_ref, tokens_ref, cot_ref, maps_ref, grad_ref, at_ref, rg_ref, lora_ref, terms_ref, up_ref
):
    rows, width = cot_ref.shape
    shards, rank, both = maps_ref.shape
    cut = tokens_ref.shape[1] // shards
    blocks = rows // BLOCK
    first = where_ref[2]
    for n in range(blocks):
        row = lax.broadcasted_iota(jnp.int32, (BLOCK, width), 0)
        part = cot_ref[n * BLOCK : (n + 1) * BLOCK, :]
        grad_ref[n * BLOCK : (n + 1) * BLOCK, :] = jnp.where(
            row < fill_ref[first + n], part, jnp.zeros_like(part)
        )
    for s in range(shards):
        up_ref[:, s * (both - cut) : (s + 1) * (both - cut)] = maps_ref[s, :, cut:]
        at_ref[:, s * cut : (s + 1) * cut] = maps_ref[s, :, :cut]
    own = (
        lax.broadcasted_iota(jnp.int32, (rows, rank), 0) // BLOCK
        == lax.broadcasted_iota(jnp.int32, (rows, rank), 1) // ADAPTER_RANK
    )
    grad = grad_ref[...]
    rank_grad = jnp.where(own, ADAPTER_SCALE * dot(grad, up_ref[...], NT), 0.0).astype(BF16)
    rg_ref[...] = rank_grad
    rank_in = jnp.where(own, dot(tokens_ref[...], at_ref[...], NT), 0.0).astype(BF16)
    lora_ref[...] = (ADAPTER_SCALE * dot(rank_in, up_ref[...])).astype(BF16).astype(F32)
    up_terms = (ADAPTER_SCALE * dot(rank_in, grad, TN)).astype(BF16)
    for s in range(shards):
        terms_ref[s, :, :cut] = dot(rank_grad, tokens_ref[:, s * cut : (s + 1) * cut], TN).astype(BF16)
        terms_ref[s, :, cut:] = up_terms[:, s * (both - cut) : (s + 1) * (both - cut)]


def chunk_kernel(
    steps, final, where_ref, fill_ref, tokens_ref, own_ref, near_ref, far_ref, mine_ref, theirs_ref,
    at_ref, grad_ref, rg_ref, sum_ref, *refs
):
    out_ref, total_ref = refs[-3:-1] if final else refs[-2:]
    acc_ref = refs[-1]
    i = pl.program_id(0)
    here, core = where_ref[0], where_ref[1]
    wide = own_ref.shape[1]

    @pl.when(i == 0)
    def _():
        acc_ref[...] = sum_ref[...]

    last = jnp.where(i < steps // 2, mine_ref[...], theirs_ref[...])
    tokens = tokens_ref[...]
    back = dot(rg_ref[...], at_ref[...]).astype(BF16).astype(F32)
    for other, weight in (
        (here, own_ref[...]),
        (here ^ (1 + core), near_ref[...]),
        (here ^ (2 - core), far_ref[...]),
        (here ^ 3, last),
    ):
        place = pl.ds(pl.multiple_of(other * wide, wide), wide)
        back += dot(grad_ref[:, place], weight, NT)
        acc_ref[:, place] += dot(tokens, weight)
    out_ref[...] = back.astype(BF16)

    if final:
        first = where_ref[2]

        @pl.when(i == steps - 1)
        def _():
            for n in range(total_ref.shape[0] // BLOCK):
                part = acc_ref[n * BLOCK : (n + 1) * BLOCK, :]
                row = lax.broadcasted_iota(jnp.int32, part.shape, 0)
                total_ref[n * BLOCK : (n + 1) * BLOCK, :] = jnp.where(
                    row < fill_ref[first + n], part, 0.0
                ).astype(BF16)


def expand_kernel(
    group, where_ref, tenant_ref, fill_ref, r0_ref, r1_ref, r2_ref, r3_ref, _, down_ref, up_ref, pick_ref, scale_ref
):
    here, core = where_ref[0], where_ref[1]
    columns = down_ref.shape[1]
    rows = group * ADAPTER_RANK
    scale_ref[...] = jnp.zeros_like(scale_ref)
    for place, other in enumerate((0, 1 + core, 2 - core, 3)):
        first = (here ^ other) * group

        @pl.loop(0, group)
        def _(n):
            start = pl.multiple_of(place * rows + n * ADAPTER_RANK, ADAPTER_RANK)
            part = block_rows(tenant_ref, first + n, here, columns)
            pick_ref[pl.ds(start, ADAPTER_RANK), :] = part.astype(BF16)
            scale_ref[...] += part * fill_ref[first + n].astype(F32)

    scale = 1.0 / jnp.maximum(jnp.sum(scale_ref[...], axis=0, keepdims=True), 1.0)
    cut = down_ref.shape[0]
    both = r0_ref.shape[1]

    def sums(lo, hi):
        total = dot(r0_ref[:, lo:hi], pick_ref[:rows, :], TN)
        for n, ref in enumerate((r1_ref, r2_ref, r3_ref)):
            total += dot(ref[:, lo:hi], pick_ref[(n + 1) * rows : (n + 2) * rows, :], TN)
        return total * scale

    step = min(cut, 256)
    for lo in range(0, cut, step):
        down_ref[lo : lo + step, :] = sums(lo, lo + step)
    up_ref[...] = sums(cut, both)


def params(**extra):
    return pltpu.CompilerParams(vmem_limit_bytes=VMEM_LIMIT, **extra)


def shape(*dims, dtype=BF16):
    return jax.ShapeDtypeStruct(dims, dtype)


def local(tokens, weight, down_maps, up_maps, cotangent, tenants, fills):
    shards = lax.axis_size("tok")
    groups = lax.axis_size("fsdp")
    rows, model = tokens.shape
    value = cotangent.shape[1]
    wide = weight.shape[1]
    cut, columns = down_maps.shape
    both = cut + up_maps.shape[0]
    dev_blocks = rows // BLOCK
    group = dev_blocks * shards
    rank = dev_blocks * ADAPTER_RANK
    group_rank = group * ADAPTER_RANK
    here = lax.axis_index("fsdp")
    tok_here = lax.axis_index("tok")
    core = tok_here % 2
    where = jnp.stack([here, core, (here * shards + tok_here) * dev_blocks]).astype(jnp.int32)

    def on_core(a):
        return lax.ppermute(a, "tok", [(t, t ^ 1) for t in range(shards)])

    def split(first, second):
        pairs = [
            (f * shards + t, (f ^ (second if t % 2 else first)) * shards + t)
            for f in range(groups)
            for t in range(shards)
        ]
        return lambda a: lax.ppermute(a, ("fsdp", "tok"), pairs)

    first_way, second_way = split(1, 2), split(2, 1)

    parts = [(model // 8 * sum(CHUNKS[:k]), model // 8 * size) for k, size in enumerate(CHUNKS)]
    sent, piece = pl.pallas_call(
        functools.partial(send_select_kernel, group, parts[0][1]),
        out_shape=[shape(2 * group_rank, both), shape(parts[0][1], wide)],
        in_specs=[SMEM, SMEM, ANY, VMEM, VMEM],
        out_specs=[VMEM, ANY],
        scratch_shapes=[pltpu.VMEM((2 * group_rank, columns), BF16), pltpu.SemaphoreType.DMA],
        compiler_params=params(),
        name="select_sent",
    )(where, tenants, weight, down_maps, up_maps)
    came = first_way(sent)
    kept = pl.pallas_call(
        functools.partial(keep_select_kernel, group),
        out_shape=shape(2 * group_rank, both),
        in_specs=[SMEM, SMEM, VMEM, VMEM],
        out_specs=VMEM,
        scratch_shapes=[pltpu.VMEM((2 * group_rank, columns), BF16)],
        compiler_params=params(),
        name="select_kept",
    )(where, tenants, down_maps, up_maps)
    sent = kept[group_rank:] + came[group_rank:]
    maps = kept[:group_rank] + came[:group_rank] + second_way(sent)
    maps = lax.all_to_all(maps.reshape(shards, rank, both), "tok", split_axis=0, concat_axis=0)

    arrived = []
    for k, (_, size) in enumerate(parts):
        near = first_way(piece)
        far = on_core(near)
        half = size // 2
        if k + 1 < len(parts):
            after, after_size = parts[k + 1]
            part, piece = pl.pallas_call(
                functools.partial(cut_kernel, after),
                out_shape=[shape(half, wide), shape(after_size, wide)],
                in_specs=[SMEM, ANY, ANY],
                out_specs=[ANY, ANY],
                scratch_shapes=[pltpu.SemaphoreType.DMA((2,))],
                compiler_params=params(),
                name="cut_chunk",
            )(where, near, weight)
        else:
            part = lax.dynamic_slice_in_dim(near, core * half, half, axis=0)
        mine = second_way(part)
        arrived.append((near, far, mine, on_core(mine)))

    grad, at, rank_grad, lora, terms = pl.pallas_call(
        rank_kernel,
        out_shape=[
            shape(rows, value),
            shape(rank, model),
            shape(rows, rank),
            shape(rows, value, dtype=F32),
            shape(shards, rank, both),
        ],
        in_specs=[SMEM, SMEM, VMEM, VMEM, VMEM],
        out_specs=[VMEM] * 5,
        scratch_shapes=[pltpu.VMEM((rank, value), BF16)],
        compiler_params=params(),
        name="rank_space",
    )(where, fills, tokens, cotangent, maps)

    r0 = lax.all_to_all(terms, "tok", split_axis=0, concat_axis=0).reshape(group_rank, both)
    r1, r2 = first_way(r0), second_way(r0)
    r3 = second_way(r1)

    tile = 512
    total, token_gradient = lora, None
    totals = []
    for k, (near, far, mine, theirs) in enumerate(arrived):
        final = k == len(parts) - 1
        start, chunk_rows = parts[k]
        steps = chunk_rows // tile

        def turned(i, where_ref, steps=steps):
            return (i + where_ref[1] * (steps // 2)) % steps

        def spot(i, w, f, start=start // tile, turned=turned):
            return start + turned(i, w)

        whole = lambda i, w, f: (0, 0)
        in_specs = [
            pl.BlockSpec((rows, tile), lambda i, w, f, spot=spot: (0, spot(i, w, f))),
            pl.BlockSpec((tile, wide), lambda i, w, f, spot=spot: (spot(i, w, f), 0)),
            pl.BlockSpec((tile, wide), lambda i, w, f, turned=turned: (turned(i, w), 0)),
            pl.BlockSpec((tile, wide), lambda i, w, f, turned=turned: (turned(i, w), 0)),
            pl.BlockSpec((tile, wide), lambda i, w, f, half=steps // 2: (jnp.minimum(i, half - 1), 0)),
            pl.BlockSpec((tile, wide), lambda i, w, f, half=steps // 2: (jnp.maximum(i - half, 0), 0)),
            pl.BlockSpec((rank, tile), lambda i, w, f, spot=spot: (0, spot(i, w, f))),
            pl.BlockSpec((rows, value), whole),
            pl.BlockSpec((rows, rank), whole),
            pl.BlockSpec((rows, value), whole),
        ]
        operands = [where, fills, tokens, weight, near, far, mine, theirs, at, grad, rank_grad, total]
        aliases = {}
        if token_gradient is not None:
            in_specs.append(pl.BlockSpec(memory_space=pl.ANY))
            aliases = {len(operands): 0}
            operands.append(token_gradient)
        token_gradient, total = pl.pallas_call(
            functools.partial(chunk_kernel, steps, final),
            out_shape=[shape(rows, model), shape(rows, value, dtype=BF16 if final else F32)],
            grid_spec=pltpu.PrefetchScalarGridSpec(
                num_scalar_prefetch=2,
                grid=(steps,),
                in_specs=in_specs,
                out_specs=[
                    pl.BlockSpec((rows, tile), lambda i, w, f, spot=spot: (0, spot(i, w, f))),
                    pl.BlockSpec((rows, value), whole),
                ],
                scratch_shapes=[pltpu.VMEM((rows, value), F32)] if final else [],
            ),
            input_output_aliases=aliases,
            compiler_params=params(dimension_semantics=("arbitrary",)),
            cost_estimate=pl.CostEstimate(
                flops=4 * rows * chunk_rows * value,
                bytes_accessed=2 * chunk_rows * (2 * rows + value) + 8 * rows * value,
                transcendentals=0,
            ),
            name="base_chunk",
        )(*operands)
        totals.append(total)

    grad_down, grad_up = pl.pallas_call(
        functools.partial(expand_kernel, group),
        out_shape=[shape(cut, columns, dtype=F32), shape(both - cut, columns, dtype=F32)],
        in_specs=[SMEM, SMEM, SMEM] + [VMEM] * 4 + [ANY],
        out_specs=[VMEM, VMEM],
        scratch_shapes=[
            pltpu.VMEM((groups * group_rank, columns), BF16),
            pltpu.VMEM((ADAPTER_RANK, columns), F32),
        ],
        compiler_params=params(),
        name="expand",
    )(where, tenants, fills, r0, r1, r2, r3, totals[-2])
    return total, token_gradient, grad_down, grad_up


def solution(mesh):
    placed = (
        P(("fsdp", "tok"), None),
        P(None, "fsdp"),
        P("tok", "fsdp"),
        P("tok", "fsdp"),
        P(("fsdp", "tok"), None),
        P(),
        P(),
    )
    return jax.shard_map(
        local,
        mesh=mesh,
        in_specs=placed,
        out_specs=(
            P(("fsdp", "tok"), None),
            P(("fsdp", "tok"), None),
            P("tok", "fsdp"),
            P("tok", "fsdp"),
        ),
        check_vma=False,
    )
```

```python
import functools

import jax
import jax.numpy as jnp
from jax import lax
from jax.experimental import pallas as pl
from jax.experimental.pallas import tpu as pltpu
from jax.sharding import PartitionSpec as P

ADAPTER_RANK = 16
TENANT_COUNT = 256
BLOCK = 128
ADAPTER_SCALE = 2.0
CHUNKS = (2, 2, 2, 2)
VMEM_LIMIT = 48 * 1024 * 1024

F32 = jnp.float32
BF16 = jnp.bfloat16
NT = (((1,), (1,)), ((), ()))
TN = (((0,), (0,)), ((), ()))
SMEM = pl.BlockSpec(memory_space=pltpu.SMEM)
VMEM = pl.BlockSpec(memory_space=pltpu.VMEM)
ANY = pl.BlockSpec(memory_space=pl.ANY)


def dot(a, b, dims=(((1,), (0,)), ((), ()))):
    return lax.dot_general(a, b, dims, preferred_element_type=F32)


def block_rows(tenant_ref, block, shard, columns):
    base = tenant_ref[block] * ADAPTER_RANK - shard * columns
    lane = lax.broadcasted_iota(jnp.int32, (ADAPTER_RANK, columns), 1)
    row = lax.broadcasted_iota(jnp.int32, (ADAPTER_RANK, columns), 0)
    return jnp.where(lane - row == base, 1.0, 0.0)


def fill_pick(tenant_ref, pick_ref, row, first_block, count, shard):
    columns = pick_ref.shape[1]

    @pl.loop(0, count)
    def _(n):
        start = pl.multiple_of(row + n * ADAPTER_RANK, ADAPTER_RANK)
        rows = block_rows(tenant_ref, first_block + n, shard, columns)
        pick_ref[pl.ds(start, ADAPTER_RANK), :] = rows.astype(BF16)


def picked(pick_ref, down_ref, up_ref, out_ref):
    cut = down_ref.shape[0]
    out_ref[:, :cut] = dot(pick_ref[...], down_ref[...], NT).astype(BF16)
    out_ref[:, cut:] = dot(pick_ref[...], up_ref[...], NT).astype(BF16)


def pick_two(group, tenant_ref, pick_ref, here, others):
    for place, other in enumerate(others):
        fill_pick(tenant_ref, pick_ref, place * group * ADAPTER_RANK, (here ^ other) * group, group, here)


def send_select_kernel(group, size, where_ref, tenant_ref, weight_ref, down_ref, up_ref, out_ref, piece_ref, pick_ref, sem):
    copy = pltpu.make_async_copy(weight_ref.at[pl.ds(0, size), :], piece_ref, sem)
    copy.start()
    here, core = where_ref[0], where_ref[1]
    pick_two(group, tenant_ref, pick_ref, here, (1 + core, 3))
    picked(pick_ref, down_ref, up_ref, out_ref)
    copy.wait()


def keep_select_kernel(group, where_ref, tenant_ref, down_ref, up_ref, out_ref, pick_ref):
    here, core = where_ref[0], where_ref[1]
    pick_two(group, tenant_ref, pick_ref, here, (0, 2 - core))
    picked(pick_ref, down_ref, up_ref, out_ref)


def cut_kernel(start, where_ref, near_ref, weight_ref, half_ref, piece_ref, sems):
    half = half_ref.shape[0]
    at = pl.multiple_of(where_ref[1] * half, half)
    copies = [
        pltpu.make_async_copy(near_ref.at[pl.ds(at, half), :], half_ref, sems.at[0]),
        pltpu.make_async_copy(weight_ref.at[pl.ds(start, piece_ref.shape[0]), :], piece_ref, sems.at[1]),
    ]
    for copy in copies:
        copy.start()
    for copy in copies:
        copy.wait()


def rank_kernel(
    where_ref, fill_ref, tokens_ref, cot_ref, maps_ref, grad_ref, at_ref, rg_ref, lora_ref, terms_ref, up_ref
):
    rows, width = cot_ref.shape
    shards, rank, both = maps_ref.shape
    cut = tokens_ref.shape[1] // shards
    blocks = rows // BLOCK
    first = where_ref[2]
    for n in range(blocks):
        row = lax.broadcasted_iota(jnp.int32, (BLOCK, width), 0)
        part = cot_ref[n * BLOCK : (n + 1) * BLOCK, :]
        grad_ref[n * BLOCK : (n + 1) * BLOCK, :] = jnp.where(
            row < fill_ref[first + n], part, jnp.zeros_like(part)
        )
    for s in range(shards):
        up_ref[:, s * (both - cut) : (s + 1) * (both - cut)] = maps_ref[s, :, cut:]
        at_ref[:, s * cut : (s + 1) * cut] = maps_ref[s, :, :cut]
    own = (
        lax.broadcasted_iota(jnp.int32, (rows, rank), 0) // BLOCK
        == lax.broadcasted_iota(jnp.int32, (rows, rank), 1) // ADAPTER_RANK
    )
    grad = grad_ref[...]
    rank_grad = jnp.where(own, ADAPTER_SCALE * dot(grad, up_ref[...], NT), 0.0).astype(BF16)
    rg_ref[...] = rank_grad
    rank_in = jnp.where(own, dot(tokens_ref[...], at_ref[...], NT), 0.0).astype(BF16)
    lora_ref[...] = (ADAPTER_SCALE * dot(rank_in, up_ref[...])).astype(BF16).astype(F32)
    up_terms = (ADAPTER_SCALE * dot(rank_in, grad, TN)).astype(BF16)
    for s in range(shards):
        terms_ref[s, :, :cut] = dot(rank_grad, tokens_ref[:, s * cut : (s + 1) * cut], TN).astype(BF16)
        terms_ref[s, :, cut:] = up_terms[:, s * (both - cut) : (s + 1) * (both - cut)]


def chunk_kernel(
    steps, final, where_ref, fill_ref, tokens_ref, own_ref, near_ref, far_ref, mine_ref, theirs_ref,
    at_ref, grad_ref, rg_ref, sum_ref, *refs
):
    out_ref, total_ref = refs[-3:-1] if final else refs[-2:]
    acc_ref = refs[-1]
    i = pl.program_id(0)
    here, core = where_ref[0], where_ref[1]
    wide = own_ref.shape[1]

    @pl.when(i == 0)
    def _():
        acc_ref[...] = sum_ref[...]

    last = jnp.where(i < steps // 2, mine_ref[...], theirs_ref[...])
    tokens = tokens_ref[...]
    back = dot(rg_ref[...], at_ref[...]).astype(BF16).astype(F32)
    for other, weight in (
        (here, own_ref[...]),
        (here ^ (1 + core), near_ref[...]),
        (here ^ (2 - core), far_ref[...]),
        (here ^ 3, last),
    ):
        place = pl.ds(pl.multiple_of(other * wide, wide), wide)
        back += dot(grad_ref[:, place], weight, NT)
        acc_ref[:, place] += dot(tokens, weight)
    out_ref[...] = back.astype(BF16)

    if final:
        first = where_ref[2]

        @pl.when(i == steps - 1)
        def _():
            for n in range(total_ref.shape[0] // BLOCK):
                part = acc_ref[n * BLOCK : (n + 1) * BLOCK, :]
                row = lax.broadcasted_iota(jnp.int32, part.shape, 0)
                total_ref[n * BLOCK : (n + 1) * BLOCK, :] = jnp.where(
                    row < fill_ref[first + n], part, 0.0
                ).astype(BF16)


def expand_kernel(
    group, where_ref, tenant_ref, fill_ref, r0_ref, r1_ref, r2_ref, r3_ref, _, down_ref, up_ref, pick_ref, scale_ref
):
    here, core = where_ref[0], where_ref[1]
    columns = down_ref.shape[1]
    rows = group * ADAPTER_RANK
    scale_ref[...] = jnp.zeros_like(scale_ref)
    for place, other in enumerate((0, 1 + core, 2 - core, 3)):
        first = (here ^ other) * group

        @pl.loop(0, group)
        def _(n):
            start = pl.multiple_of(place * rows + n * ADAPTER_RANK, ADAPTER_RANK)
            part = block_rows(tenant_ref, first + n, here, columns)
            pick_ref[pl.ds(start, ADAPTER_RANK), :] = part.astype(BF16)
            scale_ref[...] += part * fill_ref[first + n].astype(F32)

    scale = 1.0 / jnp.maximum(jnp.sum(scale_ref[...], axis=0, keepdims=True), 1.0)
    cut = down_ref.shape[0]
    both = r0_ref.shape[1]

    def sums(lo, hi):
        total = dot(r0_ref[:, lo:hi], pick_ref[:rows, :], TN)
        for n, ref in enumerate((r1_ref, r2_ref, r3_ref)):
            total += dot(ref[:, lo:hi], pick_ref[(n + 1) * rows : (n + 2) * rows, :], TN)
        return total * scale

    step = min(cut, 256)
    for lo in range(0, cut, step):
        down_ref[lo : lo + step, :] = sums(lo, lo + step)
    up_ref[...] = sums(cut, both)


def params(**extra):
    return pltpu.CompilerParams(vmem_limit_bytes=VMEM_LIMIT, **extra)


def shape(*dims, dtype=BF16):
    return jax.ShapeDtypeStruct(dims, dtype)


def local(tokens, weight, down_maps, up_maps, cotangent, tenants, fills):
    shards = lax.axis_size("tok")
    groups = lax.axis_size("fsdp")
    rows, model = tokens.shape
    value = cotangent.shape[1]
    wide = weight.shape[1]
    cut, columns = down_maps.shape
    both = cut + up_maps.shape[0]
    dev_blocks = rows // BLOCK
    group = dev_blocks * shards
    rank = dev_blocks * ADAPTER_RANK
    group_rank = group * ADAPTER_RANK
    here = lax.axis_index("fsdp")
    tok_here = lax.axis_index("tok")
    core = tok_here % 2
    where = jnp.stack([here, core, (here * shards + tok_here) * dev_blocks]).astype(jnp.int32)

    def on_core(a):
        return lax.ppermute(a, "tok", [(t, t ^ 1) for t in range(shards)])

    def split(first, second):
        pairs = [
            (f * shards + t, (f ^ (second if t % 2 else first)) * shards + t)
            for f in range(groups)
            for t in range(shards)
        ]
        return lambda a: lax.ppermute(a, ("fsdp", "tok"), pairs)

    first_way, second_way = split(1, 2), split(2, 1)

    parts = [(model // 8 * sum(CHUNKS[:k]), model // 8 * size) for k, size in enumerate(CHUNKS)]
    sent, piece = pl.pallas_call(
        functools.partial(send_select_kernel, group, parts[0][1]),
        out_shape=[shape(2 * group_rank, both), shape(parts[0][1], wide)],
        in_specs=[SMEM, SMEM, ANY, VMEM, VMEM],
        out_specs=[VMEM, VMEM],
        scratch_shapes=[pltpu.VMEM((2 * group_rank, columns), BF16), pltpu.SemaphoreType.DMA],
        compiler_params=params(),
        name="select_sent",
    )(where, tenants, weight, down_maps, up_maps)
    came = first_way(sent)
    kept = pl.pallas_call(
        functools.partial(keep_select_kernel, group),
        out_shape=shape(2 * group_rank, both),
        in_specs=[SMEM, SMEM, VMEM, VMEM],
        out_specs=VMEM,
        scratch_shapes=[pltpu.VMEM((2 * group_rank, columns), BF16)],
        compiler_params=params(),
        name="select_kept",
    )(where, tenants, down_maps, up_maps)
    sent = kept[group_rank:] + came[group_rank:]
    maps = kept[:group_rank] + came[:group_rank] + second_way(sent)
    maps = lax.all_to_all(maps.reshape(shards, rank, both), "tok", split_axis=0, concat_axis=0)

    arrived = []
    for k, (_, size) in enumerate(parts):
        near = first_way(piece)
        far = on_core(near)
        half = size // 2
        if k + 1 < len(parts):
            after, after_size = parts[k + 1]
            part, piece = pl.pallas_call(
                functools.partial(cut_kernel, after),
                out_shape=[shape(half, wide), shape(after_size, wide)],
                in_specs=[SMEM, ANY, ANY],
                out_specs=[VMEM, VMEM],
                scratch_shapes=[pltpu.SemaphoreType.DMA((2,))],
                compiler_params=params(),
                name="cut_chunk",
            )(where, near, weight)
        else:
            part = lax.dynamic_slice_in_dim(near, core * half, half, axis=0)
        mine = second_way(part)
        arrived.append((near, far, mine, on_core(mine)))

    grad, at, rank_grad, lora, terms = pl.pallas_call(
        rank_kernel,
        out_shape=[
            shape(rows, value),
            shape(rank, model),
            shape(rows, rank),
            shape(rows, value, dtype=F32),
            shape(shards, rank, both),
        ],
        in_specs=[SMEM, SMEM, VMEM, VMEM, VMEM],
        out_specs=[VMEM] * 5,
        scratch_shapes=[pltpu.VMEM((rank, value), BF16)],
        compiler_params=params(),
        name="rank_space",
    )(where, fills, tokens, cotangent, maps)

    r0 = lax.all_to_all(terms, "tok", split_axis=0, concat_axis=0).reshape(group_rank, both)
    r1, r2 = first_way(r0), second_way(r0)
    r3 = second_way(r1)

    tile = 512
    total, token_gradient = lora, None
    totals = []
    for k, (near, far, mine, theirs) in enumerate(arrived):
        final = k == len(parts) - 1
        start, chunk_rows = parts[k]
        steps = chunk_rows // tile

        def turned(i, where_ref, steps=steps):
            return (i + where_ref[1] * (steps // 2)) % steps

        def spot(i, w, f, start=start // tile, turned=turned):
            return start + turned(i, w)

        whole = lambda i, w, f: (0, 0)
        in_specs = [
            pl.BlockSpec((rows, tile), lambda i, w, f, spot=spot: (0, spot(i, w, f))),
            pl.BlockSpec((tile, wide), lambda i, w, f, spot=spot: (spot(i, w, f), 0)),
            pl.BlockSpec((tile, wide), lambda i, w, f, turned=turned: (turned(i, w), 0)),
            pl.BlockSpec((tile, wide), lambda i, w, f, turned=turned: (turned(i, w), 0)),
            pl.BlockSpec((tile, wide), lambda i, w, f, half=steps // 2: (jnp.minimum(i, half - 1), 0)),
            pl.BlockSpec((tile, wide), lambda i, w, f, half=steps // 2: (jnp.maximum(i - half, 0), 0)),
            pl.BlockSpec((rank, tile), lambda i, w, f, spot=spot: (0, spot(i, w, f))),
            pl.BlockSpec((rows, value), whole),
            pl.BlockSpec((rows, rank), whole),
            pl.BlockSpec((rows, value), whole),
        ]
        operands = [where, fills, tokens, weight, near, far, mine, theirs, at, grad, rank_grad, total]
        aliases = {}
        if token_gradient is not None:
            in_specs.append(pl.BlockSpec(memory_space=pl.ANY))
            aliases = {len(operands): 0}
            operands.append(token_gradient)
        token_gradient, total = pl.pallas_call(
            functools.partial(chunk_kernel, steps, final),
            out_shape=[shape(rows, model), shape(rows, value, dtype=BF16 if final else F32)],
            grid_spec=pltpu.PrefetchScalarGridSpec(
                num_scalar_prefetch=2,
                grid=(steps,),
                in_specs=in_specs,
                out_specs=[
                    pl.BlockSpec((rows, tile), lambda i, w, f, spot=spot: (0, spot(i, w, f))),
                    pl.BlockSpec((rows, value), whole),
                ],
                scratch_shapes=[pltpu.VMEM((rows, value), F32)] if final else [],
            ),
            input_output_aliases=aliases,
            compiler_params=params(dimension_semantics=("arbitrary",)),
            cost_estimate=pl.CostEstimate(
                flops=4 * rows * chunk_rows * value,
                bytes_accessed=2 * chunk_rows * (2 * rows + value) + 8 * rows * value,
                transcendentals=0,
            ),
            name="base_chunk",
        )(*operands)
        totals.append(total)

    grad_down, grad_up = pl.pallas_call(
        functools.partial(expand_kernel, group),
        out_shape=[shape(cut, columns, dtype=F32), shape(both - cut, columns, dtype=F32)],
        in_specs=[SMEM, SMEM, SMEM] + [VMEM] * 4 + [ANY],
        out_specs=[VMEM, VMEM],
        scratch_shapes=[
            pltpu.VMEM((groups * group_rank, columns), BF16),
            pltpu.VMEM((ADAPTER_RANK, columns), F32),
        ],
        compiler_params=params(),
        name="expand",
    )(where, tenants, fills, r0, r1, r2, r3, totals[-2])
    return total, token_gradient, grad_down, grad_up


def solution(mesh):
    placed = (
        P(("fsdp", "tok"), None),
        P(None, "fsdp"),
        P("tok", "fsdp"),
        P("tok", "fsdp"),
        P(("fsdp", "tok"), None),
        P(),
        P(),
    )
    return jax.shard_map(
        local,
        mesh=mesh,
        in_specs=placed,
        out_specs=(
            P(("fsdp", "tok"), None),
            P(("fsdp", "tok"), None),
            P("tok", "fsdp"),
            P("tok", "fsdp"),
        ),
        check_vma=False,
    )
```

```python
import functools

import jax
import jax.numpy as jnp
from jax import lax
from jax.experimental import pallas as pl
from jax.experimental.pallas import tpu as pltpu
from jax.sharding import PartitionSpec as P

ADAPTER_RANK = 16
TENANT_COUNT = 256
BLOCK = 128
ADAPTER_SCALE = 2.0
SPREAD = 4
VMEM_LIMIT = 48 * 1024 * 1024

F32 = jnp.float32
BF16 = jnp.bfloat16
NT = (((1,), (1,)), ((), ()))
TN = (((0,), (0,)), ((), ()))
SMEM = pl.BlockSpec(memory_space=pltpu.SMEM)
VMEM = pl.BlockSpec(memory_space=pltpu.VMEM)
ANY = pl.BlockSpec(memory_space=pl.ANY)


def dot(a, b, dims=(((1,), (0,)), ((), ()))):
    return lax.dot_general(a, b, dims, preferred_element_type=F32)


def block_rows(tenant_ref, block, shard, columns):
    base = tenant_ref[block] * ADAPTER_RANK - shard * columns
    lane = lax.broadcasted_iota(jnp.int32, (ADAPTER_RANK, columns), 1)
    row = lax.broadcasted_iota(jnp.int32, (ADAPTER_RANK, columns), 0)
    return jnp.where(lane - row == base, 1.0, 0.0)


def fill_pick(tenant_ref, pick_ref, row, first_block, count, shard):
    columns = pick_ref.shape[1]

    @pl.loop(0, count)
    def _(n):
        start = pl.multiple_of(row + n * ADAPTER_RANK, ADAPTER_RANK)
        rows = block_rows(tenant_ref, first_block + n, shard, columns)
        pick_ref[pl.ds(start, ADAPTER_RANK), :] = rows.astype(BF16)


def picked(pick_ref, down_ref, up_ref, out_ref):
    cut = down_ref.shape[0]
    out_ref[:, :cut] = dot(pick_ref[...], down_ref[...], NT).astype(BF16)
    out_ref[:, cut:] = dot(pick_ref[...], up_ref[...], NT).astype(BF16)


def pick_two(group, tenant_ref, pick_ref, here, others):
    for place, other in enumerate(others):
        fill_pick(tenant_ref, pick_ref, place * group * ADAPTER_RANK, (here ^ other) * group, group, here)


def send_select_kernel(group, where_ref, tenant_ref, weight_ref, down_ref, up_ref, out_ref, piece_ref, pick_ref, sem):
    size = piece_ref.shape[0]
    start = pl.multiple_of(where_ref[3] * size, size)
    copy = pltpu.make_async_copy(weight_ref.at[pl.ds(start, size), :], piece_ref, sem)
    copy.start()
    here, core = where_ref[0], where_ref[1]
    pick_two(group, tenant_ref, pick_ref, here, (1 + core, 3))
    picked(pick_ref, down_ref, up_ref, out_ref)
    copy.wait()


def keep_select_kernel(group, where_ref, tenant_ref, down_ref, up_ref, out_ref, pick_ref):
    here, core = where_ref[0], where_ref[1]
    pick_two(group, tenant_ref, pick_ref, here, (0, 2 - core))
    picked(pick_ref, down_ref, up_ref, out_ref)


def sum_kernel(start, keep_ref, came_ref, weight_ref, out_ref, piece_ref, sem):
    copy = pltpu.make_async_copy(weight_ref.at[pl.ds(start, piece_ref.shape[0]), :], piece_ref, sem)
    copy.start()
    out_ref[...] = keep_ref[...] + came_ref[...]
    copy.wait()


def rank_kernel(
    where_ref, fill_ref, tokens_ref, cot_ref, maps_ref, grad_ref, at_ref, rg_ref, lora_ref, terms_ref, up_ref
):
    rows, width = cot_ref.shape
    shards, rank, both = maps_ref.shape
    cut = tokens_ref.shape[1] // shards
    blocks = rows // BLOCK
    first = where_ref[2]
    for n in range(blocks):
        row = lax.broadcasted_iota(jnp.int32, (BLOCK, width), 0)
        part = cot_ref[n * BLOCK : (n + 1) * BLOCK, :]
        grad_ref[n * BLOCK : (n + 1) * BLOCK, :] = jnp.where(
            row < fill_ref[first + n], part, jnp.zeros_like(part)
        )
    for s in range(shards):
        up_ref[:, s * (both - cut) : (s + 1) * (both - cut)] = maps_ref[s, :, cut:]
        at_ref[:, s * cut : (s + 1) * cut] = maps_ref[s, :, :cut]
    own = (
        lax.broadcasted_iota(jnp.int32, (rows, rank), 0) // BLOCK
        == lax.broadcasted_iota(jnp.int32, (rows, rank), 1) // ADAPTER_RANK
    )
    grad = grad_ref[...]
    rank_grad = jnp.where(own, ADAPTER_SCALE * dot(grad, up_ref[...], NT), 0.0).astype(BF16)
    rg_ref[...] = rank_grad
    rank_in = jnp.where(own, dot(tokens_ref[...], at_ref[...], NT), 0.0).astype(BF16)
    lora_ref[...] = (ADAPTER_SCALE * dot(rank_in, up_ref[...])).astype(BF16).astype(F32)
    up_terms = (ADAPTER_SCALE * dot(rank_in, grad, TN)).astype(BF16)
    for s in range(shards):
        terms_ref[s, :, :cut] = dot(rank_grad, tokens_ref[:, s * cut : (s + 1) * cut], TN).astype(BF16)
        terms_ref[s, :, cut:] = up_terms[:, s * (both - cut) : (s + 1) * (both - cut)]


def base_tile(tokens, pieces, at_ref, grad_ref, rg_ref, out_ref, acc_ref):
    back = dot(rg_ref[...], at_ref[...]).astype(BF16).astype(F32)
    wide = pieces[0][1].shape[1]
    for other, weight in pieces:
        place = pl.ds(pl.multiple_of(other * wide, wide), wide)
        back += dot(grad_ref[:, place], weight, NT)
        acc_ref[:, place] += dot(tokens, weight)
    out_ref[...] = back.astype(BF16)


def spread_kernel(
    where_ref, tokens_ref, own_ref, others_ref, at_ref, grad_ref, rg_ref, sum_ref, out_ref, total_ref
):
    i = pl.program_id(0)
    here, core = where_ref[0], i % 2

    @pl.when(i == 0)
    def _():
        total_ref[...] = sum_ref[...]

    pieces = (
        (here, own_ref[...]),
        (here ^ (1 + core), others_ref[0, 0]),
        (here ^ (2 - core), others_ref[0, 1]),
        (here ^ 3, others_ref[0, 2]),
    )
    base_tile(tokens_ref[...], pieces, at_ref, grad_ref, rg_ref, out_ref, total_ref)


def swap_kernel(
    steps, where_ref, fill_ref, tokens_ref, own_ref, near_ref, far_ref, mine_ref, theirs_ref,
    at_ref, grad_ref, rg_ref, sum_ref, _, out_ref, total_ref, acc_ref
):
    i = pl.program_id(0)
    here, core, first = where_ref[0], where_ref[1], where_ref[2]

    @pl.when(i == 0)
    def _():
        acc_ref[...] = sum_ref[...]

    pieces = (
        (here, own_ref[...]),
        (here ^ (1 + core), near_ref[...]),
        (here ^ (2 - core), far_ref[...]),
        (here ^ 3, jnp.where(i < steps // 2, mine_ref[...], theirs_ref[...])),
    )
    base_tile(tokens_ref[...], pieces, at_ref, grad_ref, rg_ref, out_ref, acc_ref)

    @pl.when(i == steps - 1)
    def _():
        for n in range(total_ref.shape[0] // BLOCK):
            part = acc_ref[n * BLOCK : (n + 1) * BLOCK, :]
            row = lax.broadcasted_iota(jnp.int32, part.shape, 0)
            total_ref[n * BLOCK : (n + 1) * BLOCK, :] = jnp.where(row < fill_ref[first + n], part, 0.0).astype(BF16)


def expand_kernel(
    group, where_ref, tenant_ref, fill_ref, r0_ref, r1_ref, r2_ref, r3_ref, _, down_ref, up_ref, pick_ref, scale_ref
):
    here, core = where_ref[0], where_ref[1]
    columns = down_ref.shape[1]
    rows = group * ADAPTER_RANK
    scale_ref[...] = jnp.zeros_like(scale_ref)
    for place, other in enumerate((0, 1 + core, 2 - core, 3)):
        first = (here ^ other) * group

        @pl.loop(0, group)
        def _(n):
            start = pl.multiple_of(place * rows + n * ADAPTER_RANK, ADAPTER_RANK)
            part = block_rows(tenant_ref, first + n, here, columns)
            pick_ref[pl.ds(start, ADAPTER_RANK), :] = part.astype(BF16)
            scale_ref[...] += part * fill_ref[first + n].astype(F32)

    scale = 1.0 / jnp.maximum(jnp.sum(scale_ref[...], axis=0, keepdims=True), 1.0)
    cut = down_ref.shape[0]
    both = r0_ref.shape[1]

    def sums(lo, hi):
        total = dot(r0_ref[:, lo:hi], pick_ref[:rows, :], TN)
        for n, ref in enumerate((r1_ref, r2_ref, r3_ref)):
            total += dot(ref[:, lo:hi], pick_ref[(n + 1) * rows : (n + 2) * rows, :], TN)
        return total * scale

    step = min(cut, 256)
    for lo in range(0, cut, step):
        down_ref[lo : lo + step, :] = sums(lo, lo + step)
    up_ref[...] = sums(cut, both)


def params(**extra):
    return pltpu.CompilerParams(vmem_limit_bytes=VMEM_LIMIT, **extra)


def shape(*dims, dtype=BF16):
    return jax.ShapeDtypeStruct(dims, dtype)


def local(tokens, weight, down_maps, up_maps, cotangent, tenants, fills):
    shards = lax.axis_size("tok")
    groups = lax.axis_size("fsdp")
    rows, model = tokens.shape
    value = cotangent.shape[1]
    wide = weight.shape[1]
    cut, columns = down_maps.shape
    both = cut + up_maps.shape[0]
    dev_blocks = rows // BLOCK
    group = dev_blocks * shards
    rank = dev_blocks * ADAPTER_RANK
    group_rank = group * ADAPTER_RANK
    here = lax.axis_index("fsdp")
    tok_here = lax.axis_index("tok")
    core = tok_here % 2
    where = jnp.stack([here, core, (here * shards + tok_here) * dev_blocks, tok_here]).astype(jnp.int32)

    def on_core(a):
        return lax.ppermute(a, "tok", [(t, t ^ 1) for t in range(shards)])

    def split(first, second):
        pairs = [
            (f * shards + t, (f ^ (second if t % 2 else first)) * shards + t)
            for f in range(groups)
            for t in range(shards)
        ]
        return lambda a: lax.ppermute(a, ("fsdp", "tok"), pairs)

    first_way, second_way = split(1, 2), split(2, 1)

    spread = model // 8 * SPREAD
    swapped = model - spread
    sent, piece = pl.pallas_call(
        functools.partial(send_select_kernel, group),
        out_shape=[shape(2 * group_rank, both), shape(spread // shards, wide)],
        in_specs=[SMEM, SMEM, ANY, VMEM, VMEM],
        out_specs=[VMEM, VMEM],
        scratch_shapes=[pltpu.VMEM((2 * group_rank, columns), BF16), pltpu.SemaphoreType.DMA],
        compiler_params=params(),
        name="select_sent",
    )(where, tenants, weight, down_maps, up_maps)
    came = first_way(sent)
    kept = pl.pallas_call(
        functools.partial(keep_select_kernel, group),
        out_shape=shape(2 * group_rank, both),
        in_specs=[SMEM, SMEM, VMEM, VMEM],
        out_specs=VMEM,
        scratch_shapes=[pltpu.VMEM((2 * group_rank, columns), BF16)],
        compiler_params=params(),
        name="select_kept",
    )(where, tenants, down_maps, up_maps)
    sent = kept[group_rank:] + came[group_rank:]
    keep = kept[:group_rank] + came[:group_rank]

    first = first_way(piece)
    others = lax.all_gather(jnp.stack([first, second_way(piece), second_way(first)]), "tok")

    maps, piece = pl.pallas_call(
        functools.partial(sum_kernel, spread),
        out_shape=[shape(group_rank, both), shape(swapped, wide)],
        in_specs=[VMEM, VMEM, ANY],
        out_specs=[VMEM, VMEM],
        scratch_shapes=[pltpu.SemaphoreType.DMA],
        compiler_params=params(),
        name="sum_and_cut",
    )(keep, second_way(sent), weight)
    maps = lax.all_to_all(maps.reshape(shards, rank, both), "tok", split_axis=0, concat_axis=0)

    near = first_way(piece)
    far = on_core(near)
    mine = second_way(lax.dynamic_slice_in_dim(near, core * (swapped // 2), swapped // 2, axis=0))
    theirs = on_core(mine)

    grad, at, rank_grad, lora, terms = pl.pallas_call(
        rank_kernel,
        out_shape=[
            shape(rows, value),
            shape(rank, model),
            shape(rows, rank),
            shape(rows, value, dtype=F32),
            shape(shards, rank, both),
        ],
        in_specs=[SMEM, SMEM, VMEM, VMEM, VMEM],
        out_specs=[VMEM] * 5,
        scratch_shapes=[pltpu.VMEM((rank, value), BF16)],
        compiler_params=params(),
        name="rank_space",
    )(where, fills, tokens, cotangent, maps)

    r0 = lax.all_to_all(terms, "tok", split_axis=0, concat_axis=0).reshape(group_rank, both)
    r1, r2 = first_way(r0), second_way(r0)
    r3 = second_way(r1)

    whole = lambda i, *refs: (0, 0)
    along = lambda spot: pl.BlockSpec((rows, tile), lambda i, *refs: (0, spot(i, *refs)))
    down = lambda spot: pl.BlockSpec((tile, wide), lambda i, *refs: (spot(i, *refs), 0))

    def cost(count):
        return pl.CostEstimate(
            flops=4 * rows * count * value,
            bytes_accessed=2 * count * (2 * rows + value) + 8 * rows * value,
            transcendentals=0,
        )

    tile = spread // shards
    token_gradient, total = pl.pallas_call(
        spread_kernel,
        out_shape=[shape(rows, model), shape(rows, value, dtype=F32)],
        grid_spec=pltpu.PrefetchScalarGridSpec(
            num_scalar_prefetch=1,
            grid=(shards,),
            in_specs=[
                along(lambda i, w: i),
                down(lambda i, w: i),
                pl.BlockSpec((1, 3, tile, wide), lambda i, w: (i, 0, 0, 0)),
                pl.BlockSpec((rank, tile), lambda i, w: (0, i)),
                pl.BlockSpec((rows, value), whole),
                pl.BlockSpec((rows, rank), whole),
                pl.BlockSpec((rows, value), whole),
            ],
            out_specs=[along(lambda i, w: i), pl.BlockSpec((rows, value), whole)],
        ),
        compiler_params=params(dimension_semantics=("arbitrary",)),
        cost_estimate=cost(spread),
        name="base_spread",
    )(where, tokens, weight, others, at, grad, rank_grad, lora)

    tile = 512
    steps = swapped // tile
    turned = lambda i, w, f: (i + w[1] * (steps // 2)) % steps
    spot = lambda i, w, f: spread // tile + turned(i, w, f)
    values, token_gradient = pl.pallas_call(
        functools.partial(swap_kernel, steps),
        out_shape=[shape(rows, model), shape(rows, value)],
        grid_spec=pltpu.PrefetchScalarGridSpec(
            num_scalar_prefetch=2,
            grid=(steps,),
            in_specs=[
                along(spot),
                down(spot),
                down(turned),
                down(turned),
                down(lambda i, w, f: jnp.minimum(i, steps // 2 - 1)),
                down(lambda i, w, f: jnp.maximum(i - steps // 2, 0)),
                pl.BlockSpec((rank, tile), lambda i, w, f: (0, spot(i, w, f))),
                pl.BlockSpec((rows, value), whole),
                pl.BlockSpec((rows, rank), whole),
                pl.BlockSpec((rows, value), whole),
                ANY,
            ],
            out_specs=[along(spot), pl.BlockSpec((rows, value), whole)],
            scratch_shapes=[pltpu.VMEM((rows, value), F32)],
        ),
        input_output_aliases={12: 0},
        compiler_params=params(dimension_semantics=("arbitrary",)),
        cost_estimate=cost(swapped),
        name="base_swapped",
    )(where, fills, tokens, weight, near, far, mine, theirs, at, grad, rank_grad, total, token_gradient)[::-1]

    grad_down, grad_up = pl.pallas_call(
        functools.partial(expand_kernel, group),
        out_shape=[shape(cut, columns, dtype=F32), shape(both - cut, columns, dtype=F32)],
        in_specs=[SMEM, SMEM, SMEM] + [VMEM] * 4 + [ANY],
        out_specs=[VMEM, VMEM],
        scratch_shapes=[
            pltpu.VMEM((groups * group_rank, columns), BF16),
            pltpu.VMEM((ADAPTER_RANK, columns), F32),
        ],
        compiler_params=params(),
        name="expand",
    )(where, tenants, fills, r0, r1, r2, r3, total)
    return values, token_gradient, grad_down, grad_up


def solution(mesh):
    placed = (
        P(("fsdp", "tok"), None),
        P(None, "fsdp"),
        P("tok", "fsdp"),
        P("tok", "fsdp"),
        P(("fsdp", "tok"), None),
        P(),
        P(),
    )
    return jax.shard_map(
        local,
        mesh=mesh,
        in_specs=placed,
        out_specs=(
            P(("fsdp", "tok"), None),
            P(("fsdp", "tok"), None),
            P("tok", "fsdp"),
            P("tok", "fsdp"),
        ),
        check_vma=False,
    )
```

```python
import functools

import jax
import jax.numpy as jnp
from jax import lax
from jax.experimental import pallas as pl
from jax.experimental.pallas import tpu as pltpu
from jax.sharding import PartitionSpec as P

ADAPTER_RANK = 16
BLOCK = 128
ADAPTER_SCALE = 2.0
SPREAD = 3
VMEM_LIMIT = 48 * 1024 * 1024

F32 = jnp.float32
BF16 = jnp.bfloat16
NT = (((1,), (1,)), ((), ()))
TN = (((0,), (0,)), ((), ()))
SMEM = pl.BlockSpec(memory_space=pltpu.SMEM)
VMEM = pl.BlockSpec(memory_space=pltpu.VMEM)
ANY = pl.BlockSpec(memory_space=pl.ANY)


def dot(a, b, dims=(((1,), (0,)), ((), ()))):
    return lax.dot_general(a, b, dims, preferred_element_type=F32)


def block_rows(tenant_ref, block, shard, columns):
    base = tenant_ref[block] * ADAPTER_RANK - shard * columns
    lane = lax.broadcasted_iota(jnp.int32, (ADAPTER_RANK, columns), 1)
    row = lax.broadcasted_iota(jnp.int32, (ADAPTER_RANK, columns), 0)
    return jnp.where(lane - row == base, 1.0, 0.0)


def fill_pick(tenant_ref, pick_ref, row, first_block, count, shard):
    columns = pick_ref.shape[1]

    @pl.loop(0, count)
    def _(n):
        start = pl.multiple_of(row + n * ADAPTER_RANK, ADAPTER_RANK)
        rows = block_rows(tenant_ref, first_block + n, shard, columns)
        pick_ref[pl.ds(start, ADAPTER_RANK), :] = rows.astype(BF16)


def pick_two(group, tenant_ref, pick_ref, here, others):
    for place, other in enumerate(others):
        fill_pick(tenant_ref, pick_ref, place * group * ADAPTER_RANK, (here ^ other) * group, group, here)


def up_select_kernel(where_ref, tenant_ref, up_ref, out_ref, pick_ref):
    fill_pick(tenant_ref, pick_ref, 0, 0, tenant_ref.shape[0], where_ref[0])
    out_ref[...] = dot(pick_ref[...], up_ref[...], NT).astype(BF16)


def send_select_kernel(group, where_ref, tenant_ref, weight_ref, down_ref, out_ref, piece_ref, pick_ref, sem):
    size = piece_ref.shape[0]
    start = pl.multiple_of(where_ref[3] * size, size)
    copy = pltpu.make_async_copy(weight_ref.at[pl.ds(start, size), :], piece_ref, sem)
    copy.start()
    here, core = where_ref[0], where_ref[1]
    pick_two(group, tenant_ref, pick_ref, here, (1 + core, 3))
    out_ref[...] = dot(pick_ref[...], down_ref[...], NT).astype(BF16)
    copy.wait()


def keep_select_kernel(group, where_ref, tenant_ref, down_ref, out_ref, pick_ref):
    here, core = where_ref[0], where_ref[1]
    pick_two(group, tenant_ref, pick_ref, here, (0, 2 - core))
    out_ref[...] = dot(pick_ref[...], down_ref[...], NT).astype(BF16)


def sum_kernel(start, keep_ref, came_ref, weight_ref, keep_out_ref, send_out_ref, piece_ref, sem):
    copy = pltpu.make_async_copy(weight_ref.at[pl.ds(start, piece_ref.shape[0]), :], piece_ref, sem)
    copy.start()
    rows = keep_out_ref.shape[0]
    send_out_ref[...] = keep_ref[rows:, :] + came_ref[rows:, :]
    keep_out_ref[...] = keep_ref[:rows, :] + came_ref[:rows, :]
    copy.wait()


def block_diagonal(a):
    own = (
        lax.broadcasted_iota(jnp.int32, a.shape, 0) // BLOCK
        == lax.broadcasted_iota(jnp.int32, a.shape, 1) // ADAPTER_RANK
    )
    return jnp.where(own, a, 0.0).astype(BF16)


def down_terms_kernel(
    where_ref, fill_ref, tokens_ref, cot_ref, maps_ref, grad_ref, rg_ref, up_ref, terms_ref, full_ref
):
    rows, value = cot_ref.shape
    devices, _, width = maps_ref.shape
    shards = value // width
    here, first = where_ref[0], where_ref[2]
    wide = value * shards // devices
    for s in range(shards):
        total = maps_ref[s]
        for f in range(1, devices // shards):
            total += maps_ref[f * shards + s]
        full_ref[:, s * width : (s + 1) * width] = total
    for n in range(rows // BLOCK):
        span = slice(n * BLOCK, (n + 1) * BLOCK)
        row = lax.broadcasted_iota(jnp.int32, (BLOCK, wide), 0)
        for other in range(value // wide):
            part = cot_ref[span, pl.ds(pl.multiple_of((here ^ other) * wide, wide), wide)]
            grad_ref[span, other * wide : (other + 1) * wide] = jnp.where(
                row < fill_ref[first + n], part, jnp.zeros_like(part)
            )
    for other in range(value // wide):
        up_ref[:, other * wide : (other + 1) * wide] = full_ref[
            :, pl.ds(pl.multiple_of((here ^ other) * wide, wide), wide)
        ]
    rank_grad = block_diagonal(ADAPTER_SCALE * dot(grad_ref[...], up_ref[...], NT))
    rg_ref[...] = rank_grad
    cut = terms_ref.shape[2]
    for s in range(terms_ref.shape[0]):
        terms_ref[s] = dot(rank_grad, tokens_ref[:, s * cut : (s + 1) * cut], TN).astype(BF16)


def up_terms_kernel(where_ref, tokens_ref, maps_ref, grad_ref, up_ref, at_ref, lora_ref, terms_ref, full_ref):
    shards, _, cut = maps_ref.shape
    devices, _, width = terms_ref.shape
    value = grad_ref.shape[1]
    wide = value * shards // devices
    here = where_ref[0]
    for s in range(shards):
        at_ref[:, s * cut : (s + 1) * cut] = maps_ref[s]
    rank_in = block_diagonal(dot(tokens_ref[...], at_ref[...], NT))
    lora_ref[...] = (ADAPTER_SCALE * dot(rank_in, up_ref[...])).astype(BF16).astype(F32)
    terms = (ADAPTER_SCALE * dot(rank_in, grad_ref[...], TN)).astype(BF16)
    for other in range(value // wide):
        full_ref[:, pl.ds(pl.multiple_of((here ^ other) * wide, wide), wide)] = terms[
            :, other * wide : (other + 1) * wide
        ]
    for d in range(devices):
        s = d % shards
        terms_ref[d] = full_ref[:, s * width : (s + 1) * width]


def base_tile(core, tokens_ref, own, near, far, last, at_ref, grad_ref, rg_ref, out_ref, acc_ref):
    one, two = jnp.where(core == 0, near, far), jnp.where(core == 0, far, near)
    weight = jnp.concatenate([own, one, two, last], axis=1)
    back = dot(rg_ref[...], at_ref[...]).astype(BF16).astype(F32)
    out_ref[...] = (back + dot(grad_ref[...], weight, NT)).astype(BF16)
    acc_ref[...] += dot(tokens_ref[...], weight)


def spread_kernel(tokens_ref, own_ref, others_ref, at_ref, grad_ref, rg_ref, sum_ref, out_ref, total_ref):
    i = pl.program_id(0)

    @pl.when(i == 0)
    def _():
        total_ref[...] = sum_ref[...]

    base_tile(
        i % 2, tokens_ref, own_ref[...], others_ref[0, 0], others_ref[0, 1], others_ref[0, 2],
        at_ref, grad_ref, rg_ref, out_ref, total_ref,
    )


def swap_kernel(
    steps, where_ref, fill_ref, tokens_ref, own_ref, near_ref, far_ref, mine_ref, theirs_ref,
    at_ref, grad_ref, rg_ref, sum_ref, _, out_ref, total_ref, acc_ref
):
    i = pl.program_id(0)
    here, core, first = where_ref[0], where_ref[1], where_ref[2]

    @pl.when(i == 0)
    def _():
        acc_ref[...] = sum_ref[...]

    last = jnp.where(i < steps // 2, mine_ref[...], theirs_ref[...])
    base_tile(
        core, tokens_ref, own_ref[...], near_ref[...], far_ref[...], last,
        at_ref, grad_ref, rg_ref, out_ref, acc_ref,
    )

    @pl.when(i == steps - 1)
    def _():
        wide = own_ref.shape[1]
        for n in range(total_ref.shape[0] // BLOCK):
            span = slice(n * BLOCK, (n + 1) * BLOCK)
            for other in range(total_ref.shape[1] // wide):
                part = acc_ref[span, other * wide : (other + 1) * wide]
                row = lax.broadcasted_iota(jnp.int32, part.shape, 0)
                total_ref[span, pl.ds(pl.multiple_of((here ^ other) * wide, wide), wide)] = jnp.where(
                    row < fill_ref[first + n], part, 0.0
                ).astype(BF16)


def fill_expand(tenant_ref, fill_ref, pick_ref, scale_ref, row, first, count, shard):
    columns = pick_ref.shape[1]

    @pl.loop(0, count)
    def _(n):
        start = pl.multiple_of(row + n * ADAPTER_RANK, ADAPTER_RANK)
        part = block_rows(tenant_ref, first + n, shard, columns)
        pick_ref[pl.ds(start, ADAPTER_RANK), :] = part.astype(BF16)
        scale_ref[...] += part * fill_ref[first + n].astype(F32)


def tenant_scale(scale_ref):
    return 1.0 / jnp.maximum(jnp.sum(scale_ref[...], axis=0, keepdims=True), 1.0)


def expand_down_kernel(
    group, where_ref, tenant_ref, fill_ref, r0_ref, r1_ref, r2_ref, r3_ref, down_ref, pick_ref, scale_ref
):
    here, core = where_ref[0], where_ref[1]
    rows = group * ADAPTER_RANK
    scale_ref[...] = jnp.zeros_like(scale_ref)
    for place, other in enumerate((0, 1 + core, 2 - core, 3)):
        fill_expand(
            tenant_ref, fill_ref, pick_ref, scale_ref, place * rows, (here ^ other) * group, group, here
        )
    scale = tenant_scale(scale_ref)
    cut = down_ref.shape[0]
    step = min(cut, 256)
    for lo in range(0, cut, step):
        terms = jnp.concatenate([ref[:, lo : lo + step] for ref in (r0_ref, r1_ref, r2_ref, r3_ref)], axis=0)
        down_ref[lo : lo + step, :] = dot(terms, pick_ref[...], TN) * scale


def expand_up_kernel(where_ref, tenant_ref, fill_ref, terms_ref, up_ref, pick_ref, scale_ref):
    scale_ref[...] = jnp.zeros_like(scale_ref)
    fill_expand(tenant_ref, fill_ref, pick_ref, scale_ref, 0, 0, tenant_ref.shape[0], where_ref[0])
    up_ref[...] = dot(terms_ref[...], pick_ref[...], TN) * tenant_scale(scale_ref)


def params(**extra):
    return pltpu.CompilerParams(vmem_limit_bytes=VMEM_LIMIT, **extra)


def shape(*dims, dtype=BF16):
    return jax.ShapeDtypeStruct(dims, dtype)


def local(tokens, weight, down_maps, up_maps, cotangent, tenants, fills):
    shards = lax.axis_size("tok")
    groups = lax.axis_size("fsdp")
    devices = groups * shards
    rows, model = tokens.shape
    value = cotangent.shape[1]
    wide = weight.shape[1]
    cut, columns = down_maps.shape
    width = up_maps.shape[0]
    dev_blocks = rows // BLOCK
    group = dev_blocks * shards
    rank = dev_blocks * ADAPTER_RANK
    group_rank = group * ADAPTER_RANK
    here = lax.axis_index("fsdp")
    tok_here = lax.axis_index("tok")
    core = tok_here % 2
    where = jnp.stack([here, core, (here * shards + tok_here) * dev_blocks, tok_here]).astype(jnp.int32)

    def on_core(a):
        return lax.ppermute(a, "tok", [(t, t ^ 1) for t in range(shards)])

    def split(first, second):
        pairs = [
            (f * shards + t, (f ^ (second if t % 2 else first)) * shards + t)
            for f in range(groups)
            for t in range(shards)
        ]
        return lambda a: lax.ppermute(a, ("fsdp", "tok"), pairs)

    first_way, second_way = split(1, 2), split(2, 1)

    def everywhere(a):
        return lax.all_to_all(a, ("fsdp", "tok"), split_axis=0, concat_axis=0)

    def along_tok(a):
        return lax.all_to_all(a, "tok", split_axis=0, concat_axis=0)

    def call(body, out_shape, in_specs, name, scratch=(), out_specs=None, **extra):
        return pl.pallas_call(
            body,
            out_shape=out_shape,
            in_specs=in_specs,
            out_specs=out_specs or jax.tree.map(lambda _: VMEM, out_shape),
            scratch_shapes=list(scratch),
            compiler_params=params(),
            name=name,
            **extra,
        )

    up_sent = call(
        up_select_kernel,
        shape(devices * rank, width),
        [SMEM, SMEM, VMEM],
        "select_up",
        [pltpu.VMEM((devices * rank, columns), BF16)],
    )(where, tenants, up_maps)
    up_came = everywhere(up_sent.reshape(devices, rank, width))

    spread = max(model // 8 * SPREAD, BLOCK * shards)
    swapped = model - spread
    pick = pltpu.VMEM((2 * group_rank, columns), BF16)
    sent, share = call(
        functools.partial(send_select_kernel, group),
        [shape(2 * group_rank, cut), shape(spread // shards, wide)],
        [SMEM, SMEM, ANY, VMEM],
        "select_sent",
        [pick, pltpu.SemaphoreType.DMA],
    )(where, tenants, weight, down_maps)
    came = first_way(sent)
    kept = call(
        functools.partial(keep_select_kernel, group),
        shape(2 * group_rank, cut),
        [SMEM, SMEM, VMEM],
        "select_kept",
        [pick],
    )(where, tenants, down_maps)
    keep, sent, piece = call(
        functools.partial(sum_kernel, spread),
        [shape(group_rank, cut), shape(group_rank, cut), shape(swapped, wide)],
        [VMEM, VMEM, ANY],
        "sum_and_cut",
        [pltpu.SemaphoreType.DMA],
    )(kept, came, weight)
    down_came = along_tok((keep + second_way(sent)).reshape(shards, rank, cut))

    grad, rank_grad, up, down_terms = call(
        down_terms_kernel,
        [shape(rows, value), shape(rows, rank), shape(rank, value), shape(shards, rank, cut)],
        [SMEM, SMEM, VMEM, VMEM, VMEM],
        "down_terms",
        [pltpu.VMEM((rank, value), BF16)],
    )(where, fills, tokens, cotangent, up_came)
    r0 = along_tok(down_terms).reshape(group_rank, cut)
    r1, r2 = first_way(r0), second_way(r0)
    r3 = second_way(r1)

    at, lora, up_terms = call(
        up_terms_kernel,
        [shape(rank, model), shape(rows, value, dtype=F32), shape(devices, rank, width)],
        [SMEM, VMEM, VMEM, VMEM, VMEM],
        "up_terms",
        [pltpu.VMEM((rank, value), BF16)],
    )(where, tokens, down_came, grad, up)
    r_up = everywhere(up_terms).reshape(devices * rank, width)

    first = first_way(share)
    others = lax.all_gather(jnp.stack([first, second_way(share), second_way(first)]), "tok")

    near = first_way(piece)
    far = on_core(near)
    mine = second_way(lax.dynamic_slice_in_dim(near, core * (swapped // 2), swapped // 2, axis=0))
    theirs = on_core(mine)

    expand_scratch = [
        pltpu.VMEM((devices * rank, columns), BF16),
        pltpu.VMEM((ADAPTER_RANK, columns), F32),
    ]
    grad_down = call(
        functools.partial(expand_down_kernel, group),
        shape(cut, columns, dtype=F32),
        [SMEM, SMEM, SMEM] + [VMEM] * 4,
        "expand_down",
        expand_scratch,
    )(where, tenants, fills, r0, r1, r2, r3)
    grad_up = call(
        expand_up_kernel,
        shape(width, columns, dtype=F32),
        [SMEM, SMEM, SMEM, VMEM],
        "expand_up",
        expand_scratch,
    )(where, tenants, fills, r_up)

    whole = lambda i, *refs: (0, 0)
    along = lambda spot, tile: pl.BlockSpec((rows, tile), lambda i, *refs: (0, spot(i, *refs)))
    down = lambda spot, tile: pl.BlockSpec((tile, wide), lambda i, *refs: (spot(i, *refs), 0))
    resident = [
        pl.BlockSpec((rows, value), whole),
        pl.BlockSpec((rows, rank), whole),
        pl.BlockSpec((rows, value), whole),
    ]

    def cost(count):
        return pl.CostEstimate(
            flops=4 * rows * count * value,
            bytes_accessed=2 * count * (2 * rows + value) + 8 * rows * value,
            transcendentals=0,
        )

    tile = spread // shards
    same = lambda i: i
    token_gradient, total = pl.pallas_call(
        spread_kernel,
        out_shape=[shape(rows, model), shape(rows, value, dtype=F32)],
        grid=(shards,),
        in_specs=[
            along(same, tile),
            down(same, tile),
            pl.BlockSpec((1, 3, tile, wide), lambda i: (i, 0, 0, 0)),
            pl.BlockSpec((rank, tile), lambda i: (0, i)),
        ]
        + resident,
        out_specs=[along(same, tile), pl.BlockSpec((rows, value), whole)],
        compiler_params=params(dimension_semantics=("arbitrary",)),
        cost_estimate=cost(spread),
        name="base_spread",
    )(tokens, weight, others, at, grad, rank_grad, lora)

    tile = 512
    steps = swapped // tile
    half = steps // 2
    turned = lambda i, w, f: (i + w[1] * half) % steps
    spot = lambda i, w, f: spread // tile + turned(i, w, f)
    token_gradient, values = pl.pallas_call(
        functools.partial(swap_kernel, steps),
        out_shape=[shape(rows, model), shape(rows, value)],
        grid_spec=pltpu.PrefetchScalarGridSpec(
            num_scalar_prefetch=2,
            grid=(steps,),
            in_specs=[
                along(spot, tile),
                down(spot, tile),
                down(turned, tile),
                down(turned, tile),
                down(lambda i, w, f: jnp.minimum(i, half - 1), tile),
                down(lambda i, w, f: jnp.maximum(i - half, 0), tile),
                pl.BlockSpec((rank, tile), lambda i, w, f: (0, spot(i, w, f))),
            ]
            + resident
            + [ANY],
            out_specs=[along(spot, tile), pl.BlockSpec((rows, value), whole)],
            scratch_shapes=[pltpu.VMEM((rows, value), F32)],
        ),
        input_output_aliases={12: 0},
        compiler_params=params(dimension_semantics=("arbitrary",)),
        cost_estimate=cost(swapped),
        name="base_swapped",
    )(where, fills, tokens, weight, near, far, mine, theirs, at, grad, rank_grad, total, token_gradient)
    return values, token_gradient, grad_down, grad_up


def solution(mesh):
    placed = (
        P(("fsdp", "tok"), None),
        P(None, "fsdp"),
        P("tok", "fsdp"),
        P("tok", "fsdp"),
        P(("fsdp", "tok"), None),
        P(),
        P(),
    )
    return jax.shard_map(
        local,
        mesh=mesh,
        in_specs=placed,
        out_specs=(
            P(("fsdp", "tok"), None),
            P(("fsdp", "tok"), None),
            P("tok", "fsdp"),
            P("tok", "fsdp"),
        ),
        check_vma=False,
    )
```

```python
import functools

import jax
import jax.numpy as jnp
from jax import lax
from jax.experimental import pallas as pl
from jax.experimental.pallas import tpu as pltpu
from jax.sharding import PartitionSpec as P

ADAPTER_RANK = 16
BLOCK = 128
ADAPTER_SCALE = 2.0
CHUNKS = (3, 3, 2)
VMEM_LIMIT = 48 * 1024 * 1024

F32 = jnp.float32
BF16 = jnp.bfloat16
NT = (((1,), (1,)), ((), ()))
TN = (((0,), (0,)), ((), ()))
SMEM = pl.BlockSpec(memory_space=pltpu.SMEM)
VMEM = pl.BlockSpec(memory_space=pltpu.VMEM)
ANY = pl.BlockSpec(memory_space=pl.ANY)


def dot(a, b, dims=(((1,), (0,)), ((), ()))):
    return lax.dot_general(a, b, dims, preferred_element_type=F32)


def block_rows(tenant_ref, block, shard, columns):
    base = tenant_ref[block] * ADAPTER_RANK - shard * columns
    lane = lax.broadcasted_iota(jnp.int32, (ADAPTER_RANK, columns), 1)
    row = lax.broadcasted_iota(jnp.int32, (ADAPTER_RANK, columns), 0)
    return jnp.where(lane - row == base, 1.0, 0.0)


def fill_pick(tenant_ref, pick_ref, row, first_block, count, shard):
    columns = pick_ref.shape[1]

    @pl.loop(0, count)
    def _(n):
        start = pl.multiple_of(row + n * ADAPTER_RANK, ADAPTER_RANK)
        rows = block_rows(tenant_ref, first_block + n, shard, columns)
        pick_ref[pl.ds(start, ADAPTER_RANK), :] = rows.astype(BF16)


def pick_two(group, tenant_ref, pick_ref, here, others):
    for place, other in enumerate(others):
        fill_pick(tenant_ref, pick_ref, place * group * ADAPTER_RANK, (here ^ other) * group, group, here)


def picked(pick_ref, down_ref, up_ref, out_ref):
    cut = down_ref.shape[0]
    out_ref[:, :cut] = dot(pick_ref[...], down_ref[...], NT).astype(BF16)
    out_ref[:, cut:] = dot(pick_ref[...], up_ref[...], NT).astype(BF16)


def send_select_kernel(group, where_ref, tenant_ref, down_ref, up_ref, out_ref, pick_ref):
    here, core = where_ref[0], where_ref[1]
    pick_two(group, tenant_ref, pick_ref, here, (1 + core, 3))
    picked(pick_ref, down_ref, up_ref, out_ref)


def keep_select_kernel(group, where_ref, tenant_ref, down_ref, up_ref, out_ref, pick_ref):
    here, core = where_ref[0], where_ref[1]
    pick_two(group, tenant_ref, pick_ref, here, (0, 2 - core))
    picked(pick_ref, down_ref, up_ref, out_ref)


def sum_kernel(start, keep_ref, came_ref, weight_ref, keep_out_ref, send_out_ref, piece_ref, sem):
    copy = pltpu.make_async_copy(weight_ref.at[pl.ds(start, piece_ref.shape[0]), :], piece_ref, sem)
    copy.start()
    rows = keep_out_ref.shape[0]
    send_out_ref[...] = keep_ref[rows:, :] + came_ref[rows:, :]
    keep_out_ref[...] = keep_ref[:rows, :] + came_ref[:rows, :]
    copy.wait()


def cut_kernel(start, where_ref, near_ref, weight_ref, half_ref, *refs):
    *piece_refs, sems = refs
    half = half_ref.shape[0]
    at = pl.multiple_of(where_ref[1] * half, half)
    copies = [pltpu.make_async_copy(near_ref.at[pl.ds(at, half), :], half_ref, sems.at[0])]
    for piece_ref in piece_refs:
        copies.append(
            pltpu.make_async_copy(weight_ref.at[pl.ds(start, piece_ref.shape[0]), :], piece_ref, sems.at[1])
        )
    for copy in copies:
        copy.start()
    for copy in copies:
        copy.wait()


def block_diagonal(a):
    own = (
        lax.broadcasted_iota(jnp.int32, a.shape, 0) // BLOCK
        == lax.broadcasted_iota(jnp.int32, a.shape, 1) // ADAPTER_RANK
    )
    return jnp.where(own, a, 0.0).astype(BF16)


def rank_kernel(
    where_ref, fill_ref, tokens_ref, cot_ref, maps_ref,
    grad_ref, rg_ref, at_ref, lora_ref, terms_ref, full_ref, up_ref
):
    rows, value = cot_ref.shape
    shards, _, both = maps_ref.shape
    cut = at_ref.shape[1] // shards
    width = both - cut
    wide = value // 4
    here, first = where_ref[0], where_ref[2]
    turned = [pl.ds(pl.multiple_of((here ^ n) * wide, wide), wide) for n in range(4)]
    for s in range(shards):
        full_ref[:, s * width : (s + 1) * width] = maps_ref[s, :, cut:]
        at_ref[:, s * cut : (s + 1) * cut] = maps_ref[s, :, :cut]
    for n, place in enumerate(turned):
        up_ref[:, n * wide : (n + 1) * wide] = full_ref[:, place]
        for block in range(rows // BLOCK):
            span = slice(block * BLOCK, (block + 1) * BLOCK)
            part = cot_ref[span, place]
            row = lax.broadcasted_iota(jnp.int32, part.shape, 0)
            grad_ref[span, n * wide : (n + 1) * wide] = jnp.where(
                row < fill_ref[first + block], part, jnp.zeros_like(part)
            )
    rank_grad = block_diagonal(ADAPTER_SCALE * dot(grad_ref[...], up_ref[...], NT))
    rg_ref[...] = rank_grad
    rank_in = block_diagonal(dot(tokens_ref[...], at_ref[...], NT))
    lora_ref[...] = (ADAPTER_SCALE * dot(rank_in, up_ref[...])).astype(BF16)
    up_terms = (ADAPTER_SCALE * dot(rank_in, grad_ref[...], TN)).astype(BF16)
    for n, place in enumerate(turned):
        full_ref[:, place] = up_terms[:, n * wide : (n + 1) * wide]
    for s in range(shards):
        terms_ref[s, :, :cut] = dot(rank_grad, tokens_ref[:, s * cut : (s + 1) * cut], TN).astype(BF16)
        terms_ref[s, :, cut:] = full_ref[:, s * width : (s + 1) * width]


def base_tile(core, tokens_ref, own, near, far, last, at_ref, grad_ref, rg_ref, out_ref, acc_ref):
    one, two = jnp.where(core == 0, near, far), jnp.where(core == 0, far, near)
    weight = jnp.concatenate([own, one, two, last], axis=1)
    back = dot(rg_ref[...], at_ref[...]).astype(BF16).astype(F32)
    out_ref[...] = (back + dot(grad_ref[...], weight, NT)).astype(BF16)
    acc_ref[...] += dot(tokens_ref[...], weight)


def base_kernel(
    steps, final, where_ref, fill_ref, tokens_ref, own_ref, near_ref, far_ref, mine_ref, theirs_ref,
    at_ref, grad_ref, rg_ref, sum_ref, *refs
):
    out_ref, total_ref = refs[-3:-1] if final else refs[-2:]
    acc_ref = refs[-1]
    i = pl.program_id(0)
    here, core, first = where_ref[0], where_ref[1], where_ref[2]

    @pl.when(i == 0)
    def _():
        acc_ref[...] = sum_ref[...].astype(F32)

    last = jnp.where(i < steps // 2, mine_ref[...], theirs_ref[...])
    base_tile(
        core, tokens_ref, own_ref[...], near_ref[...], far_ref[...], last,
        at_ref, grad_ref, rg_ref, out_ref, acc_ref,
    )

    if final:

        @pl.when(i == steps - 1)
        def _():
            wide = own_ref.shape[1]
            for n in range(total_ref.shape[0] // BLOCK):
                span = slice(n * BLOCK, (n + 1) * BLOCK)
                for other in range(total_ref.shape[1] // wide):
                    part = acc_ref[span, other * wide : (other + 1) * wide]
                    row = lax.broadcasted_iota(jnp.int32, part.shape, 0)
                    total_ref[span, pl.ds(pl.multiple_of((here ^ other) * wide, wide), wide)] = jnp.where(
                        row < fill_ref[first + n], part, 0.0
                    ).astype(BF16)


def fill_expand(tenant_ref, fill_ref, pick_ref, scale_ref, row, first, count, shard):
    columns = pick_ref.shape[1]

    @pl.loop(0, count)
    def _(n):
        start = pl.multiple_of(row + n * ADAPTER_RANK, ADAPTER_RANK)
        part = block_rows(tenant_ref, first + n, shard, columns)
        pick_ref[pl.ds(start, ADAPTER_RANK), :] = part.astype(BF16)
        scale_ref[...] += part * fill_ref[first + n].astype(F32)


def tenant_scale(scale_ref):
    return 1.0 / jnp.maximum(jnp.sum(scale_ref[...], axis=0, keepdims=True), 1.0)


def expand_kernel(
    group, where_ref, tenant_ref, fill_ref, r0_ref, r1_ref, r2_ref, r3_ref, down_ref, up_ref, pick_ref, scale_ref
):
    here, core = where_ref[0], where_ref[1]
    rows = group * ADAPTER_RANK
    scale_ref[...] = jnp.zeros_like(scale_ref)
    for place, other in enumerate((0, 1 + core, 2 - core, 3)):
        fill_expand(
            tenant_ref, fill_ref, pick_ref, scale_ref, place * rows, (here ^ other) * group, group, here
        )
    scale = tenant_scale(scale_ref)
    cut, both = down_ref.shape[0], r0_ref.shape[1]

    def means(lo, hi):
        terms = jnp.concatenate([ref[:, lo:hi] for ref in (r0_ref, r1_ref, r2_ref, r3_ref)], axis=0)
        return dot(terms, pick_ref[...], TN) * scale

    step = min(cut, 256)
    for lo in range(0, cut, step):
        down_ref[lo : lo + step, :] = means(lo, lo + step)
    up_ref[...] = means(cut, both)


def after(body, place, *tokens):
    return lambda *refs: body(*refs[:place], *refs[place + len(tokens) :])


def params(**extra):
    return pltpu.CompilerParams(vmem_limit_bytes=VMEM_LIMIT, **extra)


def shape(*dims, dtype=BF16):
    return jax.ShapeDtypeStruct(dims, dtype)


def local(tokens, weight, down_maps, up_maps, cotangent, tenants, fills):
    shards = lax.axis_size("tok")
    groups = lax.axis_size("fsdp")
    devices = groups * shards
    rows, model = tokens.shape
    value = cotangent.shape[1]
    wide = weight.shape[1]
    cut, columns = down_maps.shape
    width = up_maps.shape[0]
    dev_blocks = rows // BLOCK
    group = dev_blocks * shards
    rank = dev_blocks * ADAPTER_RANK
    group_rank = group * ADAPTER_RANK
    here = lax.axis_index("fsdp")
    tok_here = lax.axis_index("tok")
    core = tok_here % 2
    where = jnp.stack([here, core, (here * shards + tok_here) * dev_blocks, tok_here]).astype(jnp.int32)

    def on_core(a):
        return lax.ppermute(a, "tok", [(t, t ^ 1) for t in range(shards)])

    def split(first, second):
        pairs = [
            (f * shards + t, (f ^ (second if t % 2 else first)) * shards + t)
            for f in range(groups)
            for t in range(shards)
        ]
        return lambda a: lax.ppermute(a, ("fsdp", "tok"), pairs)

    first_way, second_way = split(1, 2), split(2, 1)

    def along_tok(a):
        return lax.all_to_all(a, "tok", split_axis=0, concat_axis=0)

    def call(body, out_shape, in_specs, name, scratch=(), out_specs=None, **extra):
        return pl.pallas_call(
            body,
            out_shape=out_shape,
            in_specs=in_specs,
            out_specs=out_specs or jax.tree.map(lambda _: VMEM, out_shape),
            scratch_shapes=list(scratch),
            compiler_params=params(),
            name=name,
            **extra,
        )

    parts = [(model // 8 * sum(CHUNKS[:k]), model // 8 * size) for k, size in enumerate(CHUNKS)]
    both = cut + width
    pick = pltpu.VMEM((2 * group_rank, columns), BF16)
    sent = call(
        functools.partial(send_select_kernel, group),
        shape(2 * group_rank, both),
        [SMEM, SMEM, VMEM, VMEM],
        "select_sent",
        [pick],
    )(where, tenants, down_maps, up_maps)
    came = first_way(sent)
    kept = call(
        after(functools.partial(keep_select_kernel, group), 4, sent),
        shape(2 * group_rank, both),
        [SMEM, SMEM, VMEM, VMEM, ANY],
        "select_kept",
        [pick],
    )(where, tenants, down_maps, up_maps, sent)
    keep, sent, piece = call(
        functools.partial(sum_kernel, parts[0][0]),
        [shape(group_rank, both), shape(group_rank, both), shape(parts[0][1], wide)],
        [VMEM, VMEM, ANY],
        "sum_and_cut",
        [pltpu.SemaphoreType.DMA],
    )(kept, came, weight)
    maps = along_tok((keep + second_way(sent)).reshape(shards, rank, both))

    arrived, pieces = [], []
    for k, (_, size) in enumerate(parts):
        near = first_way(piece)
        far = on_core(near)
        nexts = parts[k + 1 : k + 2]
        part, *cuts = call(
            functools.partial(cut_kernel, nexts[0][0] if nexts else 0),
            [shape(size // 2, wide)] + [shape(n, wide) for _, n in nexts],
            [SMEM, ANY, ANY],
            "cut_chunk",
            [pltpu.SemaphoreType.DMA((2,))],
        )(where, near, weight)
        mine = second_way(part)
        arrived.append((near, far, mine, on_core(mine)))
        pieces.append(part)
        if cuts:
            piece = cuts[0]

    grad, rank_grad, at, lora, terms = call(
        after(rank_kernel, 5, pieces[0]),
        [
            shape(rows, value),
            shape(rows, rank),
            shape(rank, model),
            shape(rows, value),
            shape(shards, rank, both),
        ],
        [SMEM, SMEM, VMEM, VMEM, VMEM, ANY],
        "rank_space",
        [pltpu.VMEM((rank, value), BF16)] * 2,
    )(where, fills, tokens, cotangent, maps, pieces[0])
    r0 = along_tok(terms).reshape(group_rank, both)
    r1, r2 = first_way(r0), second_way(r0)
    r3 = second_way(r1)

    whole = lambda i, *refs: (0, 0)
    along = lambda spot, tile: pl.BlockSpec((rows, tile), lambda i, *refs: (0, spot(i, *refs)))
    down = lambda spot, tile: pl.BlockSpec((tile, wide), lambda i, *refs: (spot(i, *refs), 0))
    resident = [
        pl.BlockSpec((rows, value), whole),
        pl.BlockSpec((rows, rank), whole),
        pl.BlockSpec((rows, value), whole),
    ]

    def cost(count):
        return pl.CostEstimate(
            flops=4 * rows * count * value,
            bytes_accessed=2 * count * (2 * rows + value) + 8 * rows * value,
            transcendentals=0,
        )

    tile = 512
    total, token_gradient, grad_down = lora, None, None
    for k, ((start, size), (near, far, mine, theirs)) in enumerate(zip(parts, arrived)):
        final = k == len(parts) - 1
        steps = size // tile
        half = steps // 2
        if final:
            grad_down, grad_up = call(
                after(functools.partial(expand_kernel, group), 7, total),
                [shape(cut, columns, dtype=F32), shape(width, columns, dtype=F32)],
                [SMEM, SMEM, SMEM] + [VMEM] * 4 + [ANY],
                "expand",
                [pltpu.VMEM((devices * rank, columns), BF16), pltpu.VMEM((ADAPTER_RANK, columns), F32)],
            )(where, tenants, fills, r0, r1, r2, r3, total)
        turned = lambda i, w, f, half=half, steps=steps: (i + w[1] * half) % steps
        spot = lambda i, w, f, start=start, turned=turned: start // tile + turned(i, w, f)
        extra = [a for a in (token_gradient, grad_down, pieces[1] if k == 0 else None) if a is not None]
        token_gradient, total = pl.pallas_call(
            functools.partial(base_kernel, steps, final),
            out_shape=[shape(rows, model), shape(rows, value, dtype=BF16 if final else F32)],
            grid_spec=pltpu.PrefetchScalarGridSpec(
                num_scalar_prefetch=2,
                grid=(steps,),
                in_specs=[
                    along(spot, tile),
                    down(spot, tile),
                    down(turned, tile),
                    down(turned, tile),
                    down(lambda i, w, f, half=half: jnp.minimum(i, half - 1), tile),
                    down(lambda i, w, f, half=half: jnp.maximum(i - half, 0), tile),
                    pl.BlockSpec((rank, tile), lambda i, w, f, spot=spot: (0, spot(i, w, f))),
                ]
                + resident
                + [ANY] * len(extra),
                out_specs=[along(spot, tile), pl.BlockSpec((rows, value), whole)],
                scratch_shapes=[pltpu.VMEM((rows, value), F32)] if final else [],
            ),
            input_output_aliases={12: 0} if k else {},
            compiler_params=params(dimension_semantics=("arbitrary",)),
            cost_estimate=cost(size),
            name="base_chunk",
        )(where, fills, tokens, weight, near, far, mine, theirs, at, grad, rank_grad, total, *extra)
    return total, token_gradient, grad_down, grad_up


def solution(mesh):
    placed = (
        P(("fsdp", "tok"), None),
        P(None, "fsdp"),
        P("tok", "fsdp"),
        P("tok", "fsdp"),
        P(("fsdp", "tok"), None),
        P(),
        P(),
    )
    return jax.shard_map(
        local,
        mesh=mesh,
        in_specs=placed,
        out_specs=(
            P(("fsdp", "tok"), None),
            P(("fsdp", "tok"), None),
            P("tok", "fsdp"),
            P("tok", "fsdp"),
        ),
        check_vma=False,
    )
```

```python
import functools

import jax
import jax.numpy as jnp
from jax import lax
from jax.experimental import pallas as pl
from jax.experimental.pallas import tpu as pltpu
from jax.sharding import PartitionSpec as P

ADAPTER_RANK = 16
BLOCK = 128
ADAPTER_SCALE = 2.0
CHUNKS = (3, 3, 2)
VMEM_LIMIT = 48 * 1024 * 1024

F32 = jnp.float32
BF16 = jnp.bfloat16
NT = (((1,), (1,)), ((), ()))
TN = (((0,), (0,)), ((), ()))
SMEM = pl.BlockSpec(memory_space=pltpu.SMEM)
VMEM = pl.BlockSpec(memory_space=pltpu.VMEM)
ANY = pl.BlockSpec(memory_space=pl.ANY)


def dot(a, b, dims=(((1,), (0,)), ((), ()))):
    return lax.dot_general(a, b, dims, preferred_element_type=F32)


def block_rows(tenant_ref, block, shard, columns):
    base = tenant_ref[block] * ADAPTER_RANK - shard * columns
    lane = lax.broadcasted_iota(jnp.int32, (ADAPTER_RANK, columns), 1)
    row = lax.broadcasted_iota(jnp.int32, (ADAPTER_RANK, columns), 0)
    return jnp.where(lane - row == base, 1.0, 0.0)


def fill_pick(tenant_ref, pick_ref, row, first_block, count, shard):
    columns = pick_ref.shape[1]

    @pl.loop(0, count)
    def _(n):
        start = pl.multiple_of(row + n * ADAPTER_RANK, ADAPTER_RANK)
        rows = block_rows(tenant_ref, first_block + n, shard, columns)
        pick_ref[pl.ds(start, ADAPTER_RANK), :] = rows.astype(BF16)


def pick_two(group, tenant_ref, pick_ref, here, others):
    for place, other in enumerate(others):
        fill_pick(tenant_ref, pick_ref, place * group * ADAPTER_RANK, (here ^ other) * group, group, here)


def picked(pick_ref, down_ref, up_ref, out_ref):
    cut = down_ref.shape[0]
    out_ref[:, :cut] = dot(pick_ref[...], down_ref[...], NT).astype(BF16)
    out_ref[:, cut:] = dot(pick_ref[...], up_ref[...], NT).astype(BF16)


def send_select_kernel(group, where_ref, tenant_ref, down_ref, up_ref, out_ref, pick_ref):
    here, core = where_ref[0], where_ref[1]
    pick_two(group, tenant_ref, pick_ref, here, (1 + core, 3))
    picked(pick_ref, down_ref, up_ref, out_ref)


def keep_select_kernel(group, where_ref, tenant_ref, down_ref, up_ref, weight_ref, out_ref, piece_ref, pick_ref, sem):
    copy = pltpu.make_async_copy(weight_ref.at[pl.ds(0, piece_ref.shape[0]), :], piece_ref, sem)
    copy.start()
    here, core = where_ref[0], where_ref[1]
    pick_two(group, tenant_ref, pick_ref, here, (0, 2 - core))
    picked(pick_ref, down_ref, up_ref, out_ref)
    copy.wait()


def sum_two_kernel(kept_ref, came_ref, keep_ref, send_ref):
    rows = keep_ref.shape[0]
    send_ref[...] = kept_ref[rows:, :] + came_ref[rows:, :]
    keep_ref[...] = kept_ref[:rows, :] + came_ref[:rows, :]


def sum_kernel(keep_ref, came_ref, out_ref):
    out_ref[...] = keep_ref[...] + came_ref[...]


def cut_kernel(start, where_ref, near_ref, weight_ref, half_ref, *refs):
    *piece_refs, sems = refs
    half = half_ref.shape[0]
    at = pl.multiple_of(where_ref[1] * half, half)
    copies = [pltpu.make_async_copy(near_ref.at[pl.ds(at, half), :], half_ref, sems.at[0])]
    for piece_ref in piece_refs:
        copies.append(
            pltpu.make_async_copy(weight_ref.at[pl.ds(start, piece_ref.shape[0]), :], piece_ref, sems.at[1])
        )
    for copy in copies:
        copy.start()
    for copy in copies:
        copy.wait()


def block_diagonal(a):
    own = (
        lax.broadcasted_iota(jnp.int32, a.shape, 0) // BLOCK
        == lax.broadcasted_iota(jnp.int32, a.shape, 1) // ADAPTER_RANK
    )
    return jnp.where(own, a, 0.0).astype(BF16)


def rank_kernel(
    where_ref, fill_ref, tokens_ref, cot_ref, maps_ref,
    grad_ref, rg_ref, at_ref, lora_ref, terms_ref, full_ref, up_ref
):
    rows, value = cot_ref.shape
    shards, _, both = maps_ref.shape
    cut = at_ref.shape[1] // shards
    width = both - cut
    wide = value // 4
    here, first = where_ref[0], where_ref[2]
    turned = [pl.ds(pl.multiple_of((here ^ n) * wide, wide), wide) for n in range(4)]
    for s in range(shards):
        full_ref[:, s * width : (s + 1) * width] = maps_ref[s, :, cut:]
        at_ref[:, s * cut : (s + 1) * cut] = maps_ref[s, :, :cut]
    for n, place in enumerate(turned):
        up_ref[:, n * wide : (n + 1) * wide] = full_ref[:, place]
        for block in range(rows // BLOCK):
            span = slice(block * BLOCK, (block + 1) * BLOCK)
            part = cot_ref[span, place]
            row = lax.broadcasted_iota(jnp.int32, part.shape, 0)
            grad_ref[span, n * wide : (n + 1) * wide] = jnp.where(
                row < fill_ref[first + block], part, jnp.zeros_like(part)
            )
    rank_grad = block_diagonal(ADAPTER_SCALE * dot(grad_ref[...], up_ref[...], NT))
    rg_ref[...] = rank_grad
    rank_in = block_diagonal(dot(tokens_ref[...], at_ref[...], NT))
    lora_ref[...] = (ADAPTER_SCALE * dot(rank_in, up_ref[...])).astype(BF16)
    up_terms = (ADAPTER_SCALE * dot(rank_in, grad_ref[...], TN)).astype(BF16)
    for n, place in enumerate(turned):
        full_ref[:, place] = up_terms[:, n * wide : (n + 1) * wide]
    for s in range(shards):
        terms_ref[s, :, :cut] = dot(rank_grad, tokens_ref[:, s * cut : (s + 1) * cut], TN).astype(BF16)
        terms_ref[s, :, cut:] = full_ref[:, s * width : (s + 1) * width]


def base_tile(core, tokens_ref, own, near, far, last, at_ref, grad_ref, rg_ref, out_ref, acc_ref):
    one, two = jnp.where(core == 0, near, far), jnp.where(core == 0, far, near)
    weight = jnp.concatenate([own, one, two, last], axis=1)
    back = dot(rg_ref[...], at_ref[...]).astype(BF16).astype(F32)
    out_ref[...] = (back + dot(grad_ref[...], weight, NT)).astype(BF16)
    acc_ref[...] += dot(tokens_ref[...], weight)


def base_kernel(
    steps, final, where_ref, fill_ref, tokens_ref, own_ref, near_ref, far_ref, mine_ref, theirs_ref,
    at_ref, grad_ref, rg_ref, sum_ref, *refs
):
    out_ref, total_ref = refs[-3:-1] if final else refs[-2:]
    acc_ref = refs[-1]
    i = pl.program_id(0)
    here, core, first = where_ref[0], where_ref[1], where_ref[2]

    @pl.when(i == 0)
    def _():
        acc_ref[...] = sum_ref[...].astype(F32)

    last = jnp.where(i < steps // 2, mine_ref[...], theirs_ref[...])
    base_tile(
        core, tokens_ref, own_ref[...], near_ref[...], far_ref[...], last,
        at_ref, grad_ref, rg_ref, out_ref, acc_ref,
    )

    if final:

        @pl.when(i == steps - 1)
        def _():
            wide = own_ref.shape[1]
            for n in range(total_ref.shape[0] // BLOCK):
                span = slice(n * BLOCK, (n + 1) * BLOCK)
                for other in range(total_ref.shape[1] // wide):
                    part = acc_ref[span, other * wide : (other + 1) * wide]
                    row = lax.broadcasted_iota(jnp.int32, part.shape, 0)
                    total_ref[span, pl.ds(pl.multiple_of((here ^ other) * wide, wide), wide)] = jnp.where(
                        row < fill_ref[first + n], part, 0.0
                    ).astype(BF16)


def fill_expand(tenant_ref, fill_ref, pick_ref, scale_ref, row, first, count, shard):
    columns = pick_ref.shape[1]

    @pl.loop(0, count)
    def _(n):
        start = pl.multiple_of(row + n * ADAPTER_RANK, ADAPTER_RANK)
        part = block_rows(tenant_ref, first + n, shard, columns)
        pick_ref[pl.ds(start, ADAPTER_RANK), :] = part.astype(BF16)
        scale_ref[...] += part * fill_ref[first + n].astype(F32)


def tenant_scale(scale_ref):
    return 1.0 / jnp.maximum(jnp.sum(scale_ref[...], axis=0, keepdims=True), 1.0)


def expand_kernel(
    group, where_ref, tenant_ref, fill_ref, r0_ref, r1_ref, r2_ref, r3_ref, down_ref, up_ref, pick_ref, scale_ref
):
    here, core = where_ref[0], where_ref[1]
    rows = group * ADAPTER_RANK
    scale_ref[...] = jnp.zeros_like(scale_ref)
    for place, other in enumerate((0, 1 + core, 2 - core, 3)):
        fill_expand(
            tenant_ref, fill_ref, pick_ref, scale_ref, place * rows, (here ^ other) * group, group, here
        )
    scale = tenant_scale(scale_ref)
    cut, both = down_ref.shape[0], r0_ref.shape[1]

    def means(lo, hi):
        terms = jnp.concatenate([ref[:, lo:hi] for ref in (r0_ref, r1_ref, r2_ref, r3_ref)], axis=0)
        return dot(terms, pick_ref[...], TN) * scale

    step = min(cut, 256)
    for lo in range(0, cut, step):
        down_ref[lo : lo + step, :] = means(lo, lo + step)
    up_ref[...] = means(cut, both)


def after(body, place, *tokens):
    return lambda *refs: body(*refs[:place], *refs[place + len(tokens) :])


def params(**extra):
    return pltpu.CompilerParams(vmem_limit_bytes=VMEM_LIMIT, **extra)


def shape(*dims, dtype=BF16):
    return jax.ShapeDtypeStruct(dims, dtype)


def local(tokens, weight, down_maps, up_maps, cotangent, tenants, fills):
    shards = lax.axis_size("tok")
    groups = lax.axis_size("fsdp")
    devices = groups * shards
    rows, model = tokens.shape
    value = cotangent.shape[1]
    wide = weight.shape[1]
    cut, columns = down_maps.shape
    width = up_maps.shape[0]
    dev_blocks = rows // BLOCK
    group = dev_blocks * shards
    rank = dev_blocks * ADAPTER_RANK
    group_rank = group * ADAPTER_RANK
    here = lax.axis_index("fsdp")
    tok_here = lax.axis_index("tok")
    core = tok_here % 2
    where = jnp.stack([here, core, (here * shards + tok_here) * dev_blocks, tok_here]).astype(jnp.int32)

    def on_core(a):
        return lax.ppermute(a, "tok", [(t, t ^ 1) for t in range(shards)])

    def split(first, second):
        pairs = [
            (f * shards + t, (f ^ (second if t % 2 else first)) * shards + t)
            for f in range(groups)
            for t in range(shards)
        ]
        return lambda a: lax.ppermute(a, ("fsdp", "tok"), pairs)

    first_way, second_way = split(1, 2), split(2, 1)

    def along_tok(a):
        return lax.all_to_all(a, "tok", split_axis=0, concat_axis=0)

    def call(body, out_shape, in_specs, name, scratch=(), out_specs=None, **extra):
        return pl.pallas_call(
            body,
            out_shape=out_shape,
            in_specs=in_specs,
            out_specs=out_specs or jax.tree.map(lambda _: VMEM, out_shape),
            scratch_shapes=list(scratch),
            compiler_params=params(),
            name=name,
            **extra,
        )

    parts = [(model // 8 * sum(CHUNKS[:k]), model // 8 * size) for k, size in enumerate(CHUNKS)]
    both = cut + width
    pick = pltpu.VMEM((2 * group_rank, columns), BF16)
    sent = call(
        functools.partial(send_select_kernel, group),
        shape(2 * group_rank, both),
        [SMEM, SMEM, VMEM, VMEM],
        "select_sent",
        [pick],
    )(where, tenants, down_maps, up_maps)
    came = first_way(sent)
    kept, piece = call(
        after(functools.partial(keep_select_kernel, group), 5, sent),
        [shape(2 * group_rank, both), shape(parts[0][1], wide)],
        [SMEM, SMEM, VMEM, VMEM, ANY, ANY],
        "select_kept",
        [pick, pltpu.SemaphoreType.DMA],
    )(where, tenants, down_maps, up_maps, weight, sent)
    keep, sent = call(sum_two_kernel, [shape(group_rank, both)] * 2, [VMEM] * 2, "sum_two")(kept, came)

    arrived = []

    def cut_chunk(*earlier):
        k = len(arrived)
        nexts = parts[k + 1 : k + 2]
        near = first_way(pieces[k])
        part, *cuts = call(
            after(functools.partial(cut_kernel, nexts[0][0] if nexts else 0), 3, *earlier),
            [shape(parts[k][1] // 2, wide)] + [shape(n, wide) for _, n in nexts],
            [SMEM, ANY, ANY] + [ANY] * len(earlier),
            "cut_chunk",
            [pltpu.SemaphoreType.DMA((2,))],
        )(where, near, weight, *earlier)
        mine = second_way(part)
        arrived.append((near, on_core(near), mine, on_core(mine)))
        pieces.extend(cuts)
        return part

    pieces = [piece]
    part = cut_chunk(sent)
    maps = call(after(sum_kernel, 2, part), shape(group_rank, both), [VMEM, VMEM, ANY], "sum")(
        keep, second_way(sent), part
    )
    maps = along_tok(maps.reshape(shards, rank, both))

    grad, rank_grad, at, lora, terms = call(
        rank_kernel,
        [
            shape(rows, value),
            shape(rows, rank),
            shape(rank, model),
            shape(rows, value),
            shape(shards, rank, both),
        ],
        [SMEM, SMEM, VMEM, VMEM, VMEM],
        "rank_space",
        [pltpu.VMEM((rank, value), BF16)] * 2,
    )(where, fills, tokens, cotangent, maps)
    r0 = along_tok(terms).reshape(group_rank, both)
    r1, r2 = first_way(r0), second_way(r0)
    r3 = second_way(r1)

    whole = lambda i, *refs: (0, 0)
    along = lambda spot, tile: pl.BlockSpec((rows, tile), lambda i, *refs: (0, spot(i, *refs)))
    down = lambda spot, tile: pl.BlockSpec((tile, wide), lambda i, *refs: (spot(i, *refs), 0))
    resident = [
        pl.BlockSpec((rows, value), whole),
        pl.BlockSpec((rows, rank), whole),
        pl.BlockSpec((rows, value), whole),
    ]

    def cost(count):
        return pl.CostEstimate(
            flops=4 * rows * count * value,
            bytes_accessed=2 * count * (2 * rows + value) + 8 * rows * value,
            transcendentals=0,
        )

    tile = 512
    total, token_gradient, early = lora, None, rank_grad
    for k, (start, size) in enumerate(parts):
        final = k == len(parts) - 1
        steps = size // tile
        half = steps // 2
        part = None if final else cut_chunk(early, arrived[k][1], arrived[k][3])
        near, far, mine, theirs = arrived[k]
        turned = lambda i, w, f, half=half, steps=steps: (i + w[1] * half) % steps
        spot = lambda i, w, f, start=start, turned=turned: start // tile + turned(i, w, f)
        extra = [a for a in (token_gradient, part, r0 if k == 0 else None) if a is not None]
        token_gradient, total = pl.pallas_call(
            functools.partial(base_kernel, steps, final),
            out_shape=[shape(rows, model), shape(rows, value, dtype=BF16 if final else F32)],
            grid_spec=pltpu.PrefetchScalarGridSpec(
                num_scalar_prefetch=2,
                grid=(steps,),
                in_specs=[
                    along(spot, tile),
                    down(spot, tile),
                    down(turned, tile),
                    down(turned, tile),
                    down(lambda i, w, f, half=half: jnp.minimum(i, half - 1), tile),
                    down(lambda i, w, f, half=half: jnp.maximum(i - half, 0), tile),
                    pl.BlockSpec((rank, tile), lambda i, w, f, spot=spot: (0, spot(i, w, f))),
                ]
                + resident
                + [ANY] * len(extra),
                out_specs=[along(spot, tile), pl.BlockSpec((rows, value), whole)],
                scratch_shapes=[pltpu.VMEM((rows, value), F32)] if final else [],
            ),
            input_output_aliases={12: 0} if k else {},
            compiler_params=params(dimension_semantics=("arbitrary",)),
            cost_estimate=cost(size),
            name="base_chunk",
        )(where, fills, tokens, weight, near, far, mine, theirs, at, grad, rank_grad, total, *extra)
        early = total

    grad_down, grad_up = call(
        after(functools.partial(expand_kernel, group), 7, total),
        [shape(cut, columns, dtype=F32), shape(width, columns, dtype=F32)],
        [SMEM, SMEM, SMEM] + [VMEM] * 4 + [ANY],
        "expand",
        [pltpu.VMEM((devices * rank, columns), BF16), pltpu.VMEM((ADAPTER_RANK, columns), F32)],
    )(where, tenants, fills, r0, r1, r2, r3, total)
    return total, token_gradient, grad_down, grad_up


def solution(mesh):
    placed = (
        P(("fsdp", "tok"), None),
        P(None, "fsdp"),
        P("tok", "fsdp"),
        P("tok", "fsdp"),
        P(("fsdp", "tok"), None),
        P(),
        P(),
    )
    return jax.shard_map(
        local,
        mesh=mesh,
        in_specs=placed,
        out_specs=(
            P(("fsdp", "tok"), None),
            P(("fsdp", "tok"), None),
            P("tok", "fsdp"),
            P("tok", "fsdp"),
        ),
        check_vma=False,
    )
```

```python
import functools

import jax
import jax.numpy as jnp
from jax import lax
from jax.experimental import pallas as pl
from jax.experimental.pallas import tpu as pltpu
from jax.sharding import PartitionSpec as P

ADAPTER_RANK = 16
BLOCK = 128
ADAPTER_SCALE = 2.0
SPREAD = 3
VMEM_LIMIT = 48 * 1024 * 1024

F32 = jnp.float32
BF16 = jnp.bfloat16
NT = (((1,), (1,)), ((), ()))
TN = (((0,), (0,)), ((), ()))
SMEM = pl.BlockSpec(memory_space=pltpu.SMEM)
VMEM = pl.BlockSpec(memory_space=pltpu.VMEM)
ANY = pl.BlockSpec(memory_space=pl.ANY)


def dot(a, b, dims=(((1,), (0,)), ((), ()))):
    return lax.dot_general(a, b, dims, preferred_element_type=F32)


def block_rows(tenant_ref, block, shard, columns):
    base = tenant_ref[block] * ADAPTER_RANK - shard * columns
    lane = lax.broadcasted_iota(jnp.int32, (ADAPTER_RANK, columns), 1)
    row = lax.broadcasted_iota(jnp.int32, (ADAPTER_RANK, columns), 0)
    return jnp.where(lane - row == base, 1.0, 0.0)


def fill_pick(tenant_ref, pick_ref, row, first_block, count, shard):
    columns = pick_ref.shape[1]

    @pl.loop(0, count)
    def _(n):
        start = pl.multiple_of(row + n * ADAPTER_RANK, ADAPTER_RANK)
        rows = block_rows(tenant_ref, first_block + n, shard, columns)
        pick_ref[pl.ds(start, ADAPTER_RANK), :] = rows.astype(BF16)


def pick_two(group, tenant_ref, pick_ref, here, others):
    for place, other in enumerate(others):
        fill_pick(tenant_ref, pick_ref, place * group * ADAPTER_RANK, (here ^ other) * group, group, here)


def picked(pick_ref, down_ref, up_ref, out_ref):
    cut = down_ref.shape[0]
    out_ref[:, :cut] = dot(pick_ref[...], down_ref[...], NT).astype(BF16)
    out_ref[:, cut:] = dot(pick_ref[...], up_ref[...], NT).astype(BF16)


def send_select_kernel(group, where_ref, tenant_ref, down_ref, up_ref, out_ref, pick_ref):
    here, core = where_ref[0], where_ref[1]
    pick_two(group, tenant_ref, pick_ref, here, (1 + core, 3))
    picked(pick_ref, down_ref, up_ref, out_ref)


def keep_select_kernel(group, where_ref, tenant_ref, down_ref, up_ref, weight_ref, out_ref, piece_ref, pick_ref, sem):
    size = piece_ref.shape[0]
    start = pl.multiple_of(where_ref[3] * size, size)
    copy = pltpu.make_async_copy(weight_ref.at[pl.ds(start, size), :], piece_ref, sem)
    copy.start()
    here, core = where_ref[0], where_ref[1]
    pick_two(group, tenant_ref, pick_ref, here, (0, 2 - core))
    picked(pick_ref, down_ref, up_ref, out_ref)
    copy.wait()


def sum_two_kernel(kept_ref, came_ref, keep_ref, send_ref):
    rows = keep_ref.shape[0]
    send_ref[...] = kept_ref[rows:, :] + came_ref[rows:, :]
    keep_ref[...] = kept_ref[:rows, :] + came_ref[:rows, :]


def sum_kernel(start, keep_ref, came_ref, weight_ref, out_ref, piece_ref, sem):
    copy = pltpu.make_async_copy(weight_ref.at[pl.ds(start, piece_ref.shape[0]), :], piece_ref, sem)
    copy.start()
    out_ref[...] = keep_ref[...] + came_ref[...]
    copy.wait()


def gate_kernel(in_ref, out_ref):
    out_ref[...] = in_ref[...]


def block_diagonal(a):
    own = (
        lax.broadcasted_iota(jnp.int32, a.shape, 0) // BLOCK
        == lax.broadcasted_iota(jnp.int32, a.shape, 1) // ADAPTER_RANK
    )
    return jnp.where(own, a, 0.0).astype(BF16)


def rank_kernel(
    where_ref, fill_ref, tokens_ref, cot_ref, maps_ref,
    grad_ref, rg_ref, at_ref, lora_ref, terms_ref, full_ref, up_ref
):
    rows, value = cot_ref.shape
    shards, _, both = maps_ref.shape
    cut = at_ref.shape[1] // shards
    width = both - cut
    wide = value // 4
    here, first = where_ref[0], where_ref[2]
    turned = [pl.ds(pl.multiple_of((here ^ n) * wide, wide), wide) for n in range(4)]
    for s in range(shards):
        full_ref[:, s * width : (s + 1) * width] = maps_ref[s, :, cut:]
        at_ref[:, s * cut : (s + 1) * cut] = maps_ref[s, :, :cut]
    for n, place in enumerate(turned):
        up_ref[:, n * wide : (n + 1) * wide] = full_ref[:, place]
        for block in range(rows // BLOCK):
            span = slice(block * BLOCK, (block + 1) * BLOCK)
            part = cot_ref[span, place]
            row = lax.broadcasted_iota(jnp.int32, part.shape, 0)
            grad_ref[span, n * wide : (n + 1) * wide] = jnp.where(
                row < fill_ref[first + block], part, jnp.zeros_like(part)
            )
    rank_grad = block_diagonal(ADAPTER_SCALE * dot(grad_ref[...], up_ref[...], NT))
    rg_ref[...] = rank_grad
    rank_in = block_diagonal(dot(tokens_ref[...], at_ref[...], NT))
    lora_ref[...] = (ADAPTER_SCALE * dot(rank_in, up_ref[...])).astype(BF16)
    up_terms = (ADAPTER_SCALE * dot(rank_in, grad_ref[...], TN)).astype(BF16)
    for n, place in enumerate(turned):
        full_ref[:, place] = up_terms[:, n * wide : (n + 1) * wide]
    for s in range(shards):
        terms_ref[s, :, :cut] = dot(rank_grad, tokens_ref[:, s * cut : (s + 1) * cut], TN).astype(BF16)
        terms_ref[s, :, cut:] = full_ref[:, s * width : (s + 1) * width]


def base_tile(core, tokens_ref, own, near, far, last, at_ref, grad_ref, rg_ref, out_ref, acc_ref):
    one, two = jnp.where(core == 0, near, far), jnp.where(core == 0, far, near)
    weight = jnp.concatenate([own, one, two, last], axis=1)
    back = dot(rg_ref[...], at_ref[...]).astype(BF16).astype(F32)
    out_ref[...] = (back + dot(grad_ref[...], weight, NT)).astype(BF16)
    acc_ref[...] += dot(tokens_ref[...], weight)


def spread_kernel(tokens_ref, own_ref, others_ref, at_ref, grad_ref, rg_ref, sum_ref, out_ref, total_ref):
    i = pl.program_id(0)

    @pl.when(i == 0)
    def _():
        total_ref[...] = sum_ref[...].astype(F32)

    base_tile(
        i % 2, tokens_ref, own_ref[...], others_ref[0, 0], others_ref[0, 1], others_ref[0, 2],
        at_ref, grad_ref, rg_ref, out_ref, total_ref,
    )


def swap_kernel(
    steps, where_ref, fill_ref, tokens_ref, own_ref, near_ref, far_ref, mine_ref, theirs_ref,
    at_ref, grad_ref, rg_ref, sum_ref, _, out_ref, total_ref, acc_ref
):
    i = pl.program_id(0)
    here, core, first = where_ref[0], where_ref[1], where_ref[2]

    @pl.when(i == 0)
    def _():
        acc_ref[...] = sum_ref[...]

    last = jnp.where(i < steps // 2, mine_ref[...], theirs_ref[...])
    base_tile(
        core, tokens_ref, own_ref[...], near_ref[...], far_ref[...], last,
        at_ref, grad_ref, rg_ref, out_ref, acc_ref,
    )

    @pl.when(i == steps - 1)
    def _():
        wide = own_ref.shape[1]
        for n in range(total_ref.shape[0] // BLOCK):
            span = slice(n * BLOCK, (n + 1) * BLOCK)
            for other in range(total_ref.shape[1] // wide):
                part = acc_ref[span, other * wide : (other + 1) * wide]
                row = lax.broadcasted_iota(jnp.int32, part.shape, 0)
                total_ref[span, pl.ds(pl.multiple_of((here ^ other) * wide, wide), wide)] = jnp.where(
                    row < fill_ref[first + n], part, 0.0
                ).astype(BF16)


def fill_expand(tenant_ref, fill_ref, pick_ref, scale_ref, row, first, count, shard):
    columns = pick_ref.shape[1]

    @pl.loop(0, count)
    def _(n):
        start = pl.multiple_of(row + n * ADAPTER_RANK, ADAPTER_RANK)
        part = block_rows(tenant_ref, first + n, shard, columns)
        pick_ref[pl.ds(start, ADAPTER_RANK), :] = part.astype(BF16)
        scale_ref[...] += part * fill_ref[first + n].astype(F32)


def tenant_scale(scale_ref):
    return 1.0 / jnp.maximum(jnp.sum(scale_ref[...], axis=0, keepdims=True), 1.0)


def expand_kernel(
    group, where_ref, tenant_ref, fill_ref, r0_ref, r1_ref, r2_ref, r3_ref, down_ref, up_ref, pick_ref, scale_ref
):
    here, core = where_ref[0], where_ref[1]
    rows = group * ADAPTER_RANK
    scale_ref[...] = jnp.zeros_like(scale_ref)
    for place, other in enumerate((0, 1 + core, 2 - core, 3)):
        fill_expand(
            tenant_ref, fill_ref, pick_ref, scale_ref, place * rows, (here ^ other) * group, group, here
        )
    scale = tenant_scale(scale_ref)
    cut, both = down_ref.shape[0], r0_ref.shape[1]

    def means(lo, hi):
        terms = jnp.concatenate([ref[:, lo:hi] for ref in (r0_ref, r1_ref, r2_ref, r3_ref)], axis=0)
        return dot(terms, pick_ref[...], TN) * scale

    step = min(cut, 256)
    for lo in range(0, cut, step):
        down_ref[lo : lo + step, :] = means(lo, lo + step)
    up_ref[...] = means(cut, both)


def after(body, place, *tokens):
    return lambda *refs: body(*refs[:place], *refs[place + len(tokens) :])


def params(**extra):
    return pltpu.CompilerParams(vmem_limit_bytes=VMEM_LIMIT, **extra)


def shape(*dims, dtype=BF16):
    return jax.ShapeDtypeStruct(dims, dtype)


def local(tokens, weight, down_maps, up_maps, cotangent, tenants, fills):
    shards = lax.axis_size("tok")
    groups = lax.axis_size("fsdp")
    devices = groups * shards
    rows, model = tokens.shape
    value = cotangent.shape[1]
    wide = weight.shape[1]
    cut, columns = down_maps.shape
    width = up_maps.shape[0]
    dev_blocks = rows // BLOCK
    group = dev_blocks * shards
    rank = dev_blocks * ADAPTER_RANK
    group_rank = group * ADAPTER_RANK
    here = lax.axis_index("fsdp")
    tok_here = lax.axis_index("tok")
    core = tok_here % 2
    where = jnp.stack([here, core, (here * shards + tok_here) * dev_blocks, tok_here]).astype(jnp.int32)

    def on_core(a):
        return lax.ppermute(a, "tok", [(t, t ^ 1) for t in range(shards)])

    def split(first, second):
        pairs = [
            (f * shards + t, (f ^ (second if t % 2 else first)) * shards + t)
            for f in range(groups)
            for t in range(shards)
        ]
        return lambda a: lax.ppermute(a, ("fsdp", "tok"), pairs)

    first_way, second_way = split(1, 2), split(2, 1)

    def along_tok(a):
        return lax.all_to_all(a, "tok", split_axis=0, concat_axis=0)

    def call(body, out_shape, in_specs, name, scratch=(), out_specs=None, **extra):
        return pl.pallas_call(
            body,
            out_shape=out_shape,
            in_specs=in_specs,
            out_specs=out_specs or jax.tree.map(lambda _: VMEM, out_shape),
            scratch_shapes=list(scratch),
            compiler_params=params(),
            name=name,
            **extra,
        )

    spread = max(model // 8 * SPREAD, BLOCK * shards)
    swapped = model - spread
    both = cut + width
    pick = pltpu.VMEM((2 * group_rank, columns), BF16)
    sent = call(
        functools.partial(send_select_kernel, group),
        shape(2 * group_rank, both),
        [SMEM, SMEM, VMEM, VMEM],
        "select_sent",
        [pick],
    )(where, tenants, down_maps, up_maps)
    came = first_way(sent)
    kept, share = call(
        after(functools.partial(keep_select_kernel, group), 5, sent),
        [shape(2 * group_rank, both), shape(spread // shards, wide)],
        [SMEM, SMEM, VMEM, VMEM, ANY, ANY],
        "select_kept",
        [pick, pltpu.SemaphoreType.DMA],
    )(where, tenants, down_maps, up_maps, weight, sent)
    first = first_way(share)
    shares = jnp.stack([first, second_way(share), second_way(first)])
    others = lax.all_gather(shares, "tok")

    keep, sent = call(after(sum_two_kernel, 2, shares), [shape(group_rank, both)] * 2, [VMEM, VMEM, ANY], "sum_two")(
        kept, came, shares
    )
    maps, piece = call(
        functools.partial(sum_kernel, spread),
        [shape(group_rank, both), shape(swapped, wide)],
        [VMEM, VMEM, ANY],
        "sum_and_cut",
        [pltpu.SemaphoreType.DMA],
    )(keep, second_way(sent), weight)
    maps = along_tok(maps.reshape(shards, rank, both))

    near = first_way(piece)
    far = on_core(near)
    mine = second_way(lax.dynamic_slice_in_dim(near, core * (swapped // 2), swapped // 2, axis=0))
    theirs = on_core(mine)

    grad, rank_grad, at, lora, terms = call(
        rank_kernel,
        [
            shape(rows, value),
            shape(rows, rank),
            shape(rank, model),
            shape(rows, value),
            shape(shards, rank, both),
        ],
        [SMEM, SMEM, VMEM, VMEM, VMEM],
        "rank_space",
        [pltpu.VMEM((rank, value), BF16)] * 2,
    )(where, fills, tokens, cotangent, maps)
    whole = lambda i, *refs: (0, 0)
    along = lambda spot, tile: pl.BlockSpec((rows, tile), lambda i, *refs: (0, spot(i, *refs)))
    down = lambda spot, tile: pl.BlockSpec((tile, wide), lambda i, *refs: (spot(i, *refs), 0))
    resident = [
        pl.BlockSpec((rows, value), whole),
        pl.BlockSpec((rows, rank), whole),
        pl.BlockSpec((rows, value), whole),
    ]

    def cost(count):
        return pl.CostEstimate(
            flops=4 * rows * count * value,
            bytes_accessed=2 * count * (2 * rows + value) + 8 * rows * value,
            transcendentals=0,
        )

    tile = spread // shards
    same = lambda i: i
    token_gradient, total = pl.pallas_call(
        spread_kernel,
        out_shape=[shape(rows, model), shape(rows, value, dtype=F32)],
        grid=(shards,),
        in_specs=[
            along(same, tile),
            down(same, tile),
            pl.BlockSpec((1, 3, tile, wide), lambda i: (i, 0, 0, 0)),
            pl.BlockSpec((rank, tile), lambda i: (0, i)),
        ]
        + resident,
        out_specs=[along(same, tile), pl.BlockSpec((rows, value), whole)],
        compiler_params=params(dimension_semantics=("arbitrary",)),
        cost_estimate=cost(spread),
        name="base_spread",
    )(tokens, weight, others, at, grad, rank_grad, lora)

    r0 = along_tok(terms).reshape(group_rank, both)
    r0 = call(after(gate_kernel, 1, total), shape(group_rank, both), [VMEM, ANY], "gate")(r0, total)
    r1, r2 = first_way(r0), second_way(r0)
    r3 = second_way(r1)

    tile = 512
    steps = swapped // tile
    half = steps // 2
    turned = lambda i, w, f: (i + w[1] * half) % steps
    spot = lambda i, w, f: spread // tile + turned(i, w, f)
    token_gradient, values = pl.pallas_call(
        functools.partial(swap_kernel, steps),
        out_shape=[shape(rows, model), shape(rows, value)],
        grid_spec=pltpu.PrefetchScalarGridSpec(
            num_scalar_prefetch=2,
            grid=(steps,),
            in_specs=[
                along(spot, tile),
                down(spot, tile),
                down(turned, tile),
                down(turned, tile),
                down(lambda i, w, f: jnp.minimum(i, half - 1), tile),
                down(lambda i, w, f: jnp.maximum(i - half, 0), tile),
                pl.BlockSpec((rank, tile), lambda i, w, f: (0, spot(i, w, f))),
            ]
            + resident
            + [ANY],
            out_specs=[along(spot, tile), pl.BlockSpec((rows, value), whole)],
            scratch_shapes=[pltpu.VMEM((rows, value), F32)],
        ),
        input_output_aliases={12: 0},
        compiler_params=params(dimension_semantics=("arbitrary",)),
        cost_estimate=cost(swapped),
        name="base_swapped",
    )(where, fills, tokens, weight, near, far, mine, theirs, at, grad, rank_grad, total, token_gradient)
    grad_down, grad_up = call(
        after(functools.partial(expand_kernel, group), 7, values),
        [shape(cut, columns, dtype=F32), shape(width, columns, dtype=F32)],
        [SMEM, SMEM, SMEM] + [VMEM] * 4 + [ANY],
        "expand",
        [pltpu.VMEM((devices * rank, columns), BF16), pltpu.VMEM((ADAPTER_RANK, columns), F32)],
    )(where, tenants, fills, r0, r1, r2, r3, values)
    return values, token_gradient, grad_down, grad_up


def solution(mesh):
    placed = (
        P(("fsdp", "tok"), None),
        P(None, "fsdp"),
        P("tok", "fsdp"),
        P("tok", "fsdp"),
        P(("fsdp", "tok"), None),
        P(),
        P(),
    )
    return jax.shard_map(
        local,
        mesh=mesh,
        in_specs=placed,
        out_specs=(
            P(("fsdp", "tok"), None),
            P(("fsdp", "tok"), None),
            P("tok", "fsdp"),
            P("tok", "fsdp"),
        ),
        check_vma=False,
    )
```

```python
import functools

import jax
import jax.numpy as jnp
from jax import lax
from jax.experimental import pallas as pl
from jax.experimental.pallas import tpu as pltpu
from jax.sharding import PartitionSpec as P

ADAPTER_RANK = 16
BLOCK = 128
ADAPTER_SCALE = 2.0
CHUNKS = (5, 3)
VMEM_LIMIT = 48 * 1024 * 1024

F32 = jnp.float32
BF16 = jnp.bfloat16
NT = (((1,), (1,)), ((), ()))
TN = (((0,), (0,)), ((), ()))
SMEM = pl.BlockSpec(memory_space=pltpu.SMEM)
VMEM = pl.BlockSpec(memory_space=pltpu.VMEM)
ANY = pl.BlockSpec(memory_space=pl.ANY)


def dot(a, b, dims=(((1,), (0,)), ((), ()))):
    return lax.dot_general(a, b, dims, preferred_element_type=F32)


def block_rows(tenant_ref, block, shard, columns):
    base = tenant_ref[block] * ADAPTER_RANK - shard * columns
    lane = lax.broadcasted_iota(jnp.int32, (ADAPTER_RANK, columns), 1)
    row = lax.broadcasted_iota(jnp.int32, (ADAPTER_RANK, columns), 0)
    return jnp.where(lane - row == base, 1.0, 0.0)


def fill_pick(tenant_ref, pick_ref, row, first_block, count, shard):
    columns = pick_ref.shape[1]

    @pl.loop(0, count)
    def _(n):
        start = pl.multiple_of(row + n * ADAPTER_RANK, ADAPTER_RANK)
        rows = block_rows(tenant_ref, first_block + n, shard, columns)
        pick_ref[pl.ds(start, ADAPTER_RANK), :] = rows.astype(BF16)


def pick_two(group, tenant_ref, pick_ref, here, others):
    for place, other in enumerate(others):
        fill_pick(tenant_ref, pick_ref, place * group * ADAPTER_RANK, (here ^ other) * group, group, here)


def picked(pick_ref, down_ref, up_ref, out_ref):
    cut = down_ref.shape[0]
    out_ref[:, :cut] = dot(pick_ref[...], down_ref[...], NT).astype(BF16)
    out_ref[:, cut:] = dot(pick_ref[...], up_ref[...], NT).astype(BF16)


def send_select_kernel(group, where_ref, tenant_ref, down_ref, up_ref, out_ref, pick_ref):
    here, core = where_ref[0], where_ref[1]
    pick_two(group, tenant_ref, pick_ref, here, (1 + core, 3))
    picked(pick_ref, down_ref, up_ref, out_ref)


def keep_select_kernel(group, where_ref, tenant_ref, down_ref, up_ref, out_ref, pick_ref):
    here, core = where_ref[0], where_ref[1]
    pick_two(group, tenant_ref, pick_ref, here, (0, 2 - core))
    picked(pick_ref, down_ref, up_ref, out_ref)


def sum_two_kernel(kept_ref, came_ref, weight_ref, keep_ref, send_ref, piece_ref, sem):
    copy = pltpu.make_async_copy(weight_ref.at[pl.ds(0, piece_ref.shape[0]), :], piece_ref, sem)
    copy.start()
    rows = keep_ref.shape[0]
    send_ref[...] = kept_ref[rows:, :] + came_ref[rows:, :]
    keep_ref[...] = kept_ref[:rows, :] + came_ref[:rows, :]
    copy.wait()


def cut_kernel(start, where_ref, near_ref, weight_ref, half_ref, *refs):
    *piece_refs, sems = refs
    half = half_ref.shape[0]
    at = pl.multiple_of(where_ref[1] * half, half)
    copies = [pltpu.make_async_copy(near_ref.at[pl.ds(at, half), :], half_ref, sems.at[0])]
    for piece_ref in piece_refs:
        copies.append(
            pltpu.make_async_copy(weight_ref.at[pl.ds(start, piece_ref.shape[0]), :], piece_ref, sems.at[1])
        )
    for copy in copies:
        copy.start()
    for copy in copies:
        copy.wait()


def block_diagonal(a):
    own = (
        lax.broadcasted_iota(jnp.int32, a.shape, 0) // BLOCK
        == lax.broadcasted_iota(jnp.int32, a.shape, 1) // ADAPTER_RANK
    )
    return jnp.where(own, a, 0.0).astype(BF16)


def rank_kernel(
    where_ref, fill_ref, tokens_ref, cot_ref, maps_ref,
    grad_ref, rg_ref, at_ref, lora_ref, terms_ref, full_ref, up_ref
):
    rows, value = cot_ref.shape
    shards, _, both = maps_ref.shape
    cut = at_ref.shape[1] // shards
    width = both - cut
    wide = value // 4
    here, first = where_ref[0], where_ref[2]
    turned = [pl.ds(pl.multiple_of((here ^ n) * wide, wide), wide) for n in range(4)]
    for s in range(shards):
        full_ref[:, s * width : (s + 1) * width] = maps_ref[s, :, cut:]
        at_ref[:, s * cut : (s + 1) * cut] = maps_ref[s, :, :cut]
    for n, place in enumerate(turned):
        up_ref[:, n * wide : (n + 1) * wide] = full_ref[:, place]
        for block in range(rows // BLOCK):
            span = slice(block * BLOCK, (block + 1) * BLOCK)
            part = cot_ref[span, place]
            row = lax.broadcasted_iota(jnp.int32, part.shape, 0)
            grad_ref[span, n * wide : (n + 1) * wide] = jnp.where(
                row < fill_ref[first + block], part, jnp.zeros_like(part)
            )
    rank_grad = block_diagonal(ADAPTER_SCALE * dot(grad_ref[...], up_ref[...], NT))
    rg_ref[...] = rank_grad
    rank_in = block_diagonal(dot(tokens_ref[...], at_ref[...], NT))
    lora_ref[...] = (ADAPTER_SCALE * dot(rank_in, up_ref[...])).astype(BF16)
    up_terms = (ADAPTER_SCALE * dot(rank_in, grad_ref[...], TN)).astype(BF16)
    for n, place in enumerate(turned):
        full_ref[:, place] = up_terms[:, n * wide : (n + 1) * wide]
    for s in range(shards):
        terms_ref[s, :, :cut] = dot(rank_grad, tokens_ref[:, s * cut : (s + 1) * cut], TN).astype(BF16)
        terms_ref[s, :, cut:] = full_ref[:, s * width : (s + 1) * width]


def base_tile(core, tokens_ref, own, near, far, last, at_ref, grad_ref, rg_ref, out_ref, acc_ref):
    one, two = jnp.where(core == 0, near, far), jnp.where(core == 0, far, near)
    weight = jnp.concatenate([own, one, two, last], axis=1)
    back = dot(rg_ref[...], at_ref[...]).astype(BF16).astype(F32)
    out_ref[...] = (back + dot(grad_ref[...], weight, NT)).astype(BF16)
    acc_ref[...] += dot(tokens_ref[...], weight)


def base_kernel(
    steps, final, where_ref, fill_ref, tokens_ref, own_ref, near_ref, far_ref, mine_ref, theirs_ref,
    at_ref, grad_ref, rg_ref, sum_ref, *refs
):
    out_ref, total_ref = refs[-3:-1] if final else refs[-2:]
    acc_ref = refs[-1]
    i = pl.program_id(0)
    here, core, first = where_ref[0], where_ref[1], where_ref[2]

    @pl.when(i == 0)
    def _():
        acc_ref[...] = sum_ref[...].astype(F32)

    last = jnp.where(i < steps // 2, mine_ref[...], theirs_ref[...])
    base_tile(
        core, tokens_ref, own_ref[...], near_ref[...], far_ref[...], last,
        at_ref, grad_ref, rg_ref, out_ref, acc_ref,
    )

    if final:

        @pl.when(i == steps - 1)
        def _():
            wide = own_ref.shape[1]
            for n in range(total_ref.shape[0] // BLOCK):
                span = slice(n * BLOCK, (n + 1) * BLOCK)
                for other in range(total_ref.shape[1] // wide):
                    part = acc_ref[span, other * wide : (other + 1) * wide]
                    row = lax.broadcasted_iota(jnp.int32, part.shape, 0)
                    total_ref[span, pl.ds(pl.multiple_of((here ^ other) * wide, wide), wide)] = jnp.where(
                        row < fill_ref[first + n], part, 0.0
                    ).astype(BF16)


def fill_expand(tenant_ref, fill_ref, pick_ref, scale_ref, row, first, count, shard):
    columns = pick_ref.shape[1]

    @pl.loop(0, count)
    def _(n):
        start = pl.multiple_of(row + n * ADAPTER_RANK, ADAPTER_RANK)
        part = block_rows(tenant_ref, first + n, shard, columns)
        pick_ref[pl.ds(start, ADAPTER_RANK), :] = part.astype(BF16)
        scale_ref[...] += part * fill_ref[first + n].astype(F32)


def tenant_scale(scale_ref):
    return 1.0 / jnp.maximum(jnp.sum(scale_ref[...], axis=0, keepdims=True), 1.0)


def expand_kernel(
    group, where_ref, tenant_ref, fill_ref, r0_ref, r1_ref, r2_ref, r3_ref, down_ref, up_ref, pick_ref, scale_ref
):
    here, core = where_ref[0], where_ref[1]
    rows = group * ADAPTER_RANK
    scale_ref[...] = jnp.zeros_like(scale_ref)
    for place, other in enumerate((0, 1 + core, 2 - core, 3)):
        fill_expand(
            tenant_ref, fill_ref, pick_ref, scale_ref, place * rows, (here ^ other) * group, group, here
        )
    scale = tenant_scale(scale_ref)
    cut, both = down_ref.shape[0], r0_ref.shape[1]

    def means(lo, hi):
        terms = jnp.concatenate([ref[:, lo:hi] for ref in (r0_ref, r1_ref, r2_ref, r3_ref)], axis=0)
        return dot(terms, pick_ref[...], TN) * scale

    step = min(cut, 256)
    for lo in range(0, cut, step):
        down_ref[lo : lo + step, :] = means(lo, lo + step)
    up_ref[...] = means(cut, both)


def after(body, place, *tokens):
    return lambda *refs: body(*refs[:place], *refs[place + len(tokens) :])


def params(**extra):
    return pltpu.CompilerParams(vmem_limit_bytes=VMEM_LIMIT, **extra)


def shape(*dims, dtype=BF16):
    return jax.ShapeDtypeStruct(dims, dtype)


def local(tokens, weight, down_maps, up_maps, cotangent, tenants, fills):
    shards = lax.axis_size("tok")
    groups = lax.axis_size("fsdp")
    devices = groups * shards
    rows, model = tokens.shape
    value = cotangent.shape[1]
    wide = weight.shape[1]
    cut, columns = down_maps.shape
    width = up_maps.shape[0]
    dev_blocks = rows // BLOCK
    group = dev_blocks * shards
    rank = dev_blocks * ADAPTER_RANK
    group_rank = group * ADAPTER_RANK
    here = lax.axis_index("fsdp")
    tok_here = lax.axis_index("tok")
    core = tok_here % 2
    where = jnp.stack([here, core, (here * shards + tok_here) * dev_blocks, tok_here]).astype(jnp.int32)

    def on_core(a):
        return lax.ppermute(a, "tok", [(t, t ^ 1) for t in range(shards)])

    def split(first, second):
        pairs = [
            (f * shards + t, (f ^ (second if t % 2 else first)) * shards + t)
            for f in range(groups)
            for t in range(shards)
        ]
        return lambda a: lax.ppermute(a, ("fsdp", "tok"), pairs)

    first_way, second_way = split(1, 2), split(2, 1)

    def along_tok(a):
        return lax.all_to_all(a, "tok", split_axis=0, concat_axis=0)

    def call(body, out_shape, in_specs, name, scratch=(), out_specs=None, **extra):
        return pl.pallas_call(
            body,
            out_shape=out_shape,
            in_specs=in_specs,
            out_specs=out_specs or jax.tree.map(lambda _: VMEM, out_shape),
            scratch_shapes=list(scratch),
            compiler_params=params(),
            name=name,
            **extra,
        )

    parts = [(model // 8 * sum(CHUNKS[:k]), model // 8 * size) for k, size in enumerate(CHUNKS)]
    both = cut + width
    pick = pltpu.VMEM((2 * group_rank, columns), BF16)
    sent = call(
        functools.partial(send_select_kernel, group),
        shape(2 * group_rank, both),
        [SMEM, SMEM, VMEM, VMEM],
        "select_sent",
        [pick],
    )(where, tenants, down_maps, up_maps)
    came = first_way(sent)
    kept = call(
        after(functools.partial(keep_select_kernel, group), 4, sent),
        shape(2 * group_rank, both),
        [SMEM, SMEM, VMEM, VMEM, ANY],
        "select_kept",
        [pick],
    )(where, tenants, down_maps, up_maps, sent)
    keep, sent, piece = call(
        sum_two_kernel,
        [shape(group_rank, both)] * 2 + [shape(parts[0][1], wide)],
        [VMEM, VMEM, ANY],
        "sum_and_cut",
        [pltpu.SemaphoreType.DMA],
    )(kept, came, weight)
    maps = along_tok((keep + second_way(sent)).reshape(shards, rank, both))

    arrived = []

    def pass_after(a, *earlier):
        return call(
            lambda *refs: None,
            shape(*a.shape),
            [ANY] * (1 + len(earlier)),
            "pass_after",
            out_specs=ANY,
            input_output_aliases={0: 0},
        )(a, *earlier)

    def cut_chunk(*earlier):
        k = len(arrived)
        nexts = parts[k + 1 : k + 2]
        near = first_way(pieces[k])
        part, *cuts = call(
            after(functools.partial(cut_kernel, nexts[0][0] if nexts else 0), 3, *earlier),
            [shape(parts[k][1] // 2, wide)] + [shape(n, wide) for _, n in nexts],
            [SMEM, ANY, ANY] + [ANY] * len(earlier),
            "cut_chunk",
            [pltpu.SemaphoreType.DMA((2,))],
        )(where, near, weight, *earlier)
        near = pass_after(near, part)
        arrived.append((near, on_core(near), second_way(part)))
        pieces.extend(cuts)
        return part

    pieces = [piece]
    part = cut_chunk(maps)

    grad, rank_grad, at, lora, terms = call(
        after(rank_kernel, 5, part),
        [
            shape(rows, value),
            shape(rows, rank),
            shape(rank, model),
            shape(rows, value),
            shape(shards, rank, both),
        ],
        [SMEM, SMEM, VMEM, VMEM, VMEM, ANY],
        "rank_space",
        [pltpu.VMEM((rank, value), BF16)] * 2,
    )(where, fills, tokens, cotangent, maps, part)
    r0 = along_tok(terms).reshape(group_rank, both)
    r1, r2 = first_way(r0), second_way(r0)
    r3 = second_way(r1)

    whole = lambda i, *refs: (0, 0)
    along = lambda spot, tile: pl.BlockSpec((rows, tile), lambda i, *refs: (0, spot(i, *refs)))
    down = lambda spot, tile: pl.BlockSpec((tile, wide), lambda i, *refs: (spot(i, *refs), 0))
    resident = [
        pl.BlockSpec((rows, value), whole),
        pl.BlockSpec((rows, rank), whole),
        pl.BlockSpec((rows, value), whole),
    ]

    def cost(count):
        return pl.CostEstimate(
            flops=4 * rows * count * value,
            bytes_accessed=2 * count * (2 * rows + value) + 8 * rows * value,
            transcendentals=0,
        )

    tile = 512
    total, token_gradient = lora, None
    for k, (start, size) in enumerate(parts):
        final = k == len(parts) - 1
        steps = size // tile
        half = steps // 2
        part = None if final else cut_chunk(r0, arrived[k][1])
        near, far, mine = arrived[k]
        mine = pass_after(mine, *((r1, r2, total) if final else (r0,)))
        theirs = on_core(mine)
        turned = lambda i, w, f, half=half, steps=steps: (i + w[1] * half) % steps
        spot = lambda i, w, f, start=start, turned=turned: start // tile + turned(i, w, f)
        extra = [a for a in (token_gradient, part) if a is not None]
        token_gradient, total = pl.pallas_call(
            functools.partial(base_kernel, steps, final),
            out_shape=[shape(rows, model), shape(rows, value, dtype=BF16 if final else F32)],
            grid_spec=pltpu.PrefetchScalarGridSpec(
                num_scalar_prefetch=2,
                grid=(steps,),
                in_specs=[
                    along(spot, tile),
                    down(spot, tile),
                    down(turned, tile),
                    down(turned, tile),
                    down(lambda i, w, f, half=half: jnp.minimum(i, half - 1), tile),
                    down(lambda i, w, f, half=half: jnp.maximum(i - half, 0), tile),
                    pl.BlockSpec((rank, tile), lambda i, w, f, spot=spot: (0, spot(i, w, f))),
                ]
                + resident
                + [ANY] * len(extra),
                out_specs=[along(spot, tile), pl.BlockSpec((rows, value), whole)],
                scratch_shapes=[pltpu.VMEM((rows, value), F32)] if final else [],
            ),
            input_output_aliases={12: 0} if k else {},
            compiler_params=params(dimension_semantics=("arbitrary",)),
            cost_estimate=cost(size),
            name="base_chunk",
        )(where, fills, tokens, weight, near, far, mine, theirs, at, grad, rank_grad, total, *extra)

    grad_down, grad_up = call(
        after(functools.partial(expand_kernel, group), 7, total),
        [shape(cut, columns, dtype=F32), shape(width, columns, dtype=F32)],
        [SMEM, SMEM, SMEM] + [VMEM] * 4 + [ANY],
        "expand",
        [pltpu.VMEM((devices * rank, columns), BF16), pltpu.VMEM((ADAPTER_RANK, columns), F32)],
    )(where, tenants, fills, r0, r1, r2, r3, total)
    return total, token_gradient, grad_down, grad_up


def solution(mesh):
    placed = (
        P(("fsdp", "tok"), None),
        P(None, "fsdp"),
        P("tok", "fsdp"),
        P("tok", "fsdp"),
        P(("fsdp", "tok"), None),
        P(),
        P(),
    )
    return jax.shard_map(
        local,
        mesh=mesh,
        in_specs=placed,
        out_specs=(
            P(("fsdp", "tok"), None),
            P(("fsdp", "tok"), None),
            P("tok", "fsdp"),
            P("tok", "fsdp"),
        ),
        check_vma=False,
    )
```

```python
import functools

import jax
import jax.numpy as jnp
from jax import lax
from jax.experimental import pallas as pl
from jax.experimental.pallas import tpu as pltpu
from jax.sharding import PartitionSpec as P

ADAPTER_RANK = 16
BLOCK = 128
ADAPTER_SCALE = 2.0
CHUNKS = (4, 4)
VMEM_LIMIT = 48 * 1024 * 1024

F32 = jnp.float32
BF16 = jnp.bfloat16
NT = (((1,), (1,)), ((), ()))
TN = (((0,), (0,)), ((), ()))
SMEM = pl.BlockSpec(memory_space=pltpu.SMEM)
VMEM = pl.BlockSpec(memory_space=pltpu.VMEM)
ANY = pl.BlockSpec(memory_space=pl.ANY)


def dot(a, b, dims=(((1,), (0,)), ((), ()))):
    return lax.dot_general(a, b, dims, preferred_element_type=F32)


def block_rows(tenant_ref, block, shard, columns):
    base = tenant_ref[block] * ADAPTER_RANK - shard * columns
    lane = lax.broadcasted_iota(jnp.int32, (ADAPTER_RANK, columns), 1)
    row = lax.broadcasted_iota(jnp.int32, (ADAPTER_RANK, columns), 0)
    return jnp.where(lane - row == base, 1.0, 0.0)


def fill_pick(tenant_ref, pick_ref, row, first_block, count, shard):
    columns = pick_ref.shape[1]

    @pl.loop(0, count)
    def _(n):
        start = pl.multiple_of(row + n * ADAPTER_RANK, ADAPTER_RANK)
        rows = block_rows(tenant_ref, first_block + n, shard, columns)
        pick_ref[pl.ds(start, ADAPTER_RANK), :] = rows.astype(BF16)


def pick_two(group, tenant_ref, pick_ref, here, others):
    for place, other in enumerate(others):
        fill_pick(tenant_ref, pick_ref, place * group * ADAPTER_RANK, (here ^ other) * group, group, here)


def picked(pick_ref, down_ref, up_ref, out_ref):
    cut = down_ref.shape[0]
    out_ref[:, :cut] = dot(pick_ref[...], down_ref[...], NT).astype(BF16)
    out_ref[:, cut:] = dot(pick_ref[...], up_ref[...], NT).astype(BF16)


def send_select_kernel(group, where_ref, tenant_ref, down_ref, up_ref, out_ref, pick_ref):
    here, core = where_ref[0], where_ref[1]
    pick_two(group, tenant_ref, pick_ref, here, (1 + core, 3))
    picked(pick_ref, down_ref, up_ref, out_ref)


def keep_select_kernel(group, where_ref, tenant_ref, down_ref, up_ref, out_ref, pick_ref):
    here, core = where_ref[0], where_ref[1]
    pick_two(group, tenant_ref, pick_ref, here, (0, 2 - core))
    picked(pick_ref, down_ref, up_ref, out_ref)


def sum_two_kernel(kept_ref, came_ref, weight_ref, keep_ref, send_ref, piece_ref, sem):
    copy = pltpu.make_async_copy(weight_ref.at[pl.ds(0, piece_ref.shape[0]), :], piece_ref, sem)
    copy.start()
    rows = keep_ref.shape[0]
    send_ref[...] = kept_ref[rows:, :] + came_ref[rows:, :]
    keep_ref[...] = kept_ref[:rows, :] + came_ref[:rows, :]
    copy.wait()


def sum_kernel(start, keep_ref, came_ref, weight_ref, out_ref, piece_ref, sem):
    copy = pltpu.make_async_copy(weight_ref.at[pl.ds(start, piece_ref.shape[0]), :], piece_ref, sem)
    copy.start()
    out_ref[...] = keep_ref[...] + came_ref[...]
    copy.wait()


def cut_kernel(where_ref, near_ref, half_ref, sem):
    half = half_ref.shape[0]
    at = pl.multiple_of(where_ref[1] * half, half)
    copy = pltpu.make_async_copy(near_ref.at[pl.ds(at, half), :], half_ref, sem)
    copy.start()
    copy.wait()


def block_diagonal(a):
    own = (
        lax.broadcasted_iota(jnp.int32, a.shape, 0) // BLOCK
        == lax.broadcasted_iota(jnp.int32, a.shape, 1) // ADAPTER_RANK
    )
    return jnp.where(own, a, 0.0).astype(BF16)


def rank_kernel(
    where_ref, fill_ref, tokens_ref, cot_ref, maps_ref,
    grad_ref, rg_ref, at_ref, lora_ref, terms_ref, full_ref, up_ref
):
    rows, value = cot_ref.shape
    shards, _, both = maps_ref.shape
    cut = at_ref.shape[1] // shards
    width = both - cut
    wide = value // 4
    here, first = where_ref[0], where_ref[2]
    turned = [pl.ds(pl.multiple_of((here ^ n) * wide, wide), wide) for n in range(4)]
    for s in range(shards):
        full_ref[:, s * width : (s + 1) * width] = maps_ref[s, :, cut:]
        at_ref[:, s * cut : (s + 1) * cut] = maps_ref[s, :, :cut]
    for n, place in enumerate(turned):
        up_ref[:, n * wide : (n + 1) * wide] = full_ref[:, place]
        for block in range(rows // BLOCK):
            span = slice(block * BLOCK, (block + 1) * BLOCK)
            part = cot_ref[span, place]
            row = lax.broadcasted_iota(jnp.int32, part.shape, 0)
            grad_ref[span, n * wide : (n + 1) * wide] = jnp.where(
                row < fill_ref[first + block], part, jnp.zeros_like(part)
            )
    rank_grad = block_diagonal(ADAPTER_SCALE * dot(grad_ref[...], up_ref[...], NT))
    rg_ref[...] = rank_grad
    rank_in = block_diagonal(dot(tokens_ref[...], at_ref[...], NT))
    lora_ref[...] = (ADAPTER_SCALE * dot(rank_in, up_ref[...])).astype(BF16)
    up_terms = (ADAPTER_SCALE * dot(rank_in, grad_ref[...], TN)).astype(BF16)
    for n, place in enumerate(turned):
        full_ref[:, place] = up_terms[:, n * wide : (n + 1) * wide]
    for s in range(shards):
        terms_ref[s, :, :cut] = dot(rank_grad, tokens_ref[:, s * cut : (s + 1) * cut], TN).astype(BF16)
        terms_ref[s, :, cut:] = full_ref[:, s * width : (s + 1) * width]


def base_tile(core, tokens_ref, own, near, far, last, at_ref, grad_ref, rg_ref, out_ref, acc_ref):
    one, two = jnp.where(core == 0, near, far), jnp.where(core == 0, far, near)
    weight = jnp.concatenate([own, one, two, last], axis=1)
    back = dot(rg_ref[...], at_ref[...]).astype(BF16).astype(F32)
    out_ref[...] = (back + dot(grad_ref[...], weight, NT)).astype(BF16)
    acc_ref[...] += dot(tokens_ref[...], weight)


def base_kernel(
    steps, final, where_ref, fill_ref, tokens_ref, own_ref, near_ref, far_ref, mine_ref, theirs_ref,
    at_ref, grad_ref, rg_ref, sum_ref, *refs
):
    out_ref, total_ref = refs[-3:-1] if final else refs[-2:]
    acc_ref = refs[-1]
    i = pl.program_id(0)
    here, core, first = where_ref[0], where_ref[1], where_ref[2]

    @pl.when(i == 0)
    def _():
        acc_ref[...] = sum_ref[...].astype(F32)

    last = jnp.where(i < steps // 2, mine_ref[...], theirs_ref[...])
    base_tile(
        core, tokens_ref, own_ref[...], near_ref[...], far_ref[...], last,
        at_ref, grad_ref, rg_ref, out_ref, acc_ref,
    )

    if final:

        @pl.when(i == steps - 1)
        def _():
            wide = own_ref.shape[1]
            for n in range(total_ref.shape[0] // BLOCK):
                span = slice(n * BLOCK, (n + 1) * BLOCK)
                for other in range(total_ref.shape[1] // wide):
                    part = acc_ref[span, other * wide : (other + 1) * wide]
                    row = lax.broadcasted_iota(jnp.int32, part.shape, 0)
                    total_ref[span, pl.ds(pl.multiple_of((here ^ other) * wide, wide), wide)] = jnp.where(
                        row < fill_ref[first + n], part, 0.0
                    ).astype(BF16)


def fill_expand(tenant_ref, fill_ref, pick_ref, scale_ref, row, first, count, shard):
    columns = pick_ref.shape[1]

    @pl.loop(0, count)
    def _(n):
        start = pl.multiple_of(row + n * ADAPTER_RANK, ADAPTER_RANK)
        part = block_rows(tenant_ref, first + n, shard, columns)
        pick_ref[pl.ds(start, ADAPTER_RANK), :] = part.astype(BF16)
        scale_ref[...] += part * fill_ref[first + n].astype(F32)


def tenant_scale(scale_ref):
    return 1.0 / jnp.maximum(jnp.sum(scale_ref[...], axis=0, keepdims=True), 1.0)


def expand_kernel(
    group, where_ref, tenant_ref, fill_ref, r0_ref, r1_ref, r2_ref, r3_ref, down_ref, up_ref, pick_ref, scale_ref
):
    here, core = where_ref[0], where_ref[1]
    rows = group * ADAPTER_RANK
    scale_ref[...] = jnp.zeros_like(scale_ref)
    for place, other in enumerate((0, 1 + core, 2 - core, 3)):
        fill_expand(
            tenant_ref, fill_ref, pick_ref, scale_ref, place * rows, (here ^ other) * group, group, here
        )
    scale = tenant_scale(scale_ref)
    cut, both = down_ref.shape[0], r0_ref.shape[1]

    def means(lo, hi):
        terms = jnp.concatenate([ref[:, lo:hi] for ref in (r0_ref, r1_ref, r2_ref, r3_ref)], axis=0)
        return dot(terms, pick_ref[...], TN) * scale

    step = min(cut, 256)
    for lo in range(0, cut, step):
        down_ref[lo : lo + step, :] = means(lo, lo + step)
    up_ref[...] = means(cut, both)


def after(body, place, *tokens):
    return lambda *refs: body(*refs[:place], *refs[place + len(tokens) :])


def params(**extra):
    return pltpu.CompilerParams(vmem_limit_bytes=VMEM_LIMIT, **extra)


def shape(*dims, dtype=BF16):
    return jax.ShapeDtypeStruct(dims, dtype)


def local(tokens, weight, down_maps, up_maps, cotangent, tenants, fills):
    shards = lax.axis_size("tok")
    groups = lax.axis_size("fsdp")
    devices = groups * shards
    rows, model = tokens.shape
    value = cotangent.shape[1]
    wide = weight.shape[1]
    cut, columns = down_maps.shape
    width = up_maps.shape[0]
    dev_blocks = rows // BLOCK
    group = dev_blocks * shards
    rank = dev_blocks * ADAPTER_RANK
    group_rank = group * ADAPTER_RANK
    here = lax.axis_index("fsdp")
    tok_here = lax.axis_index("tok")
    core = tok_here % 2
    where = jnp.stack([here, core, (here * shards + tok_here) * dev_blocks, tok_here]).astype(jnp.int32)

    def on_core(a):
        return lax.ppermute(a, "tok", [(t, t ^ 1) for t in range(shards)])

    def split(first, second):
        pairs = [
            (f * shards + t, (f ^ (second if t % 2 else first)) * shards + t)
            for f in range(groups)
            for t in range(shards)
        ]
        return lambda a: lax.ppermute(a, ("fsdp", "tok"), pairs)

    first_way, second_way = split(1, 2), split(2, 1)

    def along_tok(a):
        return lax.all_to_all(a, "tok", split_axis=0, concat_axis=0)

    def call(body, out_shape, in_specs, name, scratch=(), out_specs=None, **extra):
        return pl.pallas_call(
            body,
            out_shape=out_shape,
            in_specs=in_specs,
            out_specs=out_specs or jax.tree.map(lambda _: VMEM, out_shape),
            scratch_shapes=list(scratch),
            compiler_params=params(),
            name=name,
            **extra,
        )

    parts = [(model // 8 * sum(CHUNKS[:k]), model // 8 * size) for k, size in enumerate(CHUNKS)]
    both = cut + width
    pick = pltpu.VMEM((2 * group_rank, columns), BF16)
    sent = call(
        functools.partial(send_select_kernel, group),
        shape(2 * group_rank, both),
        [SMEM, SMEM, VMEM, VMEM],
        "select_sent",
        [pick],
    )(where, tenants, down_maps, up_maps)
    came = first_way(sent)
    kept = call(
        after(functools.partial(keep_select_kernel, group), 4, sent),
        shape(2 * group_rank, both),
        [SMEM, SMEM, VMEM, VMEM, ANY],
        "select_kept",
        [pick],
    )(where, tenants, down_maps, up_maps, sent)
    keep, sent, piece = call(
        sum_two_kernel,
        [shape(group_rank, both)] * 2 + [shape(parts[0][1], wide)],
        [VMEM, VMEM, ANY],
        "sum_and_cut",
        [pltpu.SemaphoreType.DMA],
    )(kept, came, weight)
    maps, later = call(
        functools.partial(sum_kernel, parts[1][0]),
        [shape(group_rank, both), shape(parts[1][1], wide)],
        [VMEM, VMEM, ANY],
        "sum_and_cut",
        [pltpu.SemaphoreType.DMA],
    )(keep, second_way(sent), weight)
    maps = along_tok(maps.reshape(shards, rank, both))

    arrived = []

    def pass_after(a, *earlier):
        return call(
            lambda *refs: None,
            shape(*a.shape),
            [ANY] * (1 + len(earlier)),
            "pass_after",
            out_specs=ANY,
            input_output_aliases={0: 0},
        )(a, *earlier)

    def cut_chunk(piece, *earlier):
        near = first_way(piece)
        part = call(
            after(cut_kernel, 2, *earlier),
            shape(piece.shape[0] // 2, wide),
            [SMEM, ANY] + [ANY] * len(earlier),
            "cut_chunk",
            [pltpu.SemaphoreType.DMA],
        )(where, near, *earlier)
        near = pass_after(near, part)
        arrived.append((near, on_core(near), second_way(part)))
        return part

    part = cut_chunk(piece, maps)

    grad, rank_grad, at, lora, terms = call(
        after(rank_kernel, 5, part),
        [
            shape(rows, value),
            shape(rows, rank),
            shape(rank, model),
            shape(rows, value),
            shape(shards, rank, both),
        ],
        [SMEM, SMEM, VMEM, VMEM, VMEM, ANY],
        "rank_space",
        [pltpu.VMEM((rank, value), BF16)] * 2,
    )(where, fills, tokens, cotangent, maps, part)
    r0 = along_tok(terms).reshape(group_rank, both)
    r1, r2 = first_way(r0), second_way(r0)

    whole = lambda i, *refs: (0, 0)
    along = lambda spot, tile: pl.BlockSpec((rows, tile), lambda i, *refs: (0, spot(i, *refs)))
    down = lambda spot, tile: pl.BlockSpec((tile, wide), lambda i, *refs: (spot(i, *refs), 0))
    resident = [
        pl.BlockSpec((rows, value), whole),
        pl.BlockSpec((rows, rank), whole),
        pl.BlockSpec((rows, value), whole),
    ]

    def cost(count):
        return pl.CostEstimate(
            flops=4 * rows * count * value,
            bytes_accessed=2 * count * (2 * rows + value) + 8 * rows * value,
            transcendentals=0,
        )

    tile = 512
    total, token_gradient = lora, None
    for k, (start, size) in enumerate(parts):
        final = k == len(parts) - 1
        steps = size // tile
        half = steps // 2
        part = None if final else cut_chunk(later, rank_grad, arrived[k][1])
        near, far, mine = arrived[k]
        mine = pass_after(mine, r0)
        theirs = on_core(mine)
        if final:
            r1 = pass_after(r1, total)
            r3 = second_way(r1)
        turned = lambda i, w, f, half=half, steps=steps: (i + w[1] * half) % steps
        spot = lambda i, w, f, start=start, turned=turned: start // tile + turned(i, w, f)
        extra = [a for a in (token_gradient, part, *((r1, r2) if final else ())) if a is not None]
        token_gradient, total = pl.pallas_call(
            functools.partial(base_kernel, steps, final),
            out_shape=[shape(rows, model), shape(rows, value, dtype=BF16 if final else F32)],
            grid_spec=pltpu.PrefetchScalarGridSpec(
                num_scalar_prefetch=2,
                grid=(steps,),
                in_specs=[
                    along(spot, tile),
                    down(spot, tile),
                    down(turned, tile),
                    down(turned, tile),
                    down(lambda i, w, f, half=half: jnp.minimum(i, half - 1), tile),
                    down(lambda i, w, f, half=half: jnp.maximum(i - half, 0), tile),
                    pl.BlockSpec((rank, tile), lambda i, w, f, spot=spot: (0, spot(i, w, f))),
                ]
                + resident
                + [ANY] * len(extra),
                out_specs=[along(spot, tile), pl.BlockSpec((rows, value), whole)],
                scratch_shapes=[pltpu.VMEM((rows, value), F32)] if final else [],
            ),
            input_output_aliases={12: 0} if k else {},
            compiler_params=params(dimension_semantics=("arbitrary",)),
            cost_estimate=cost(size),
            name="base_chunk",
        )(where, fills, tokens, weight, near, far, mine, theirs, at, grad, rank_grad, total, *extra)

    grad_down, grad_up = call(
        after(functools.partial(expand_kernel, group), 7, total),
        [shape(cut, columns, dtype=F32), shape(width, columns, dtype=F32)],
        [SMEM, SMEM, SMEM] + [VMEM] * 4 + [ANY],
        "expand",
        [pltpu.VMEM((devices * rank, columns), BF16), pltpu.VMEM((ADAPTER_RANK, columns), F32)],
    )(where, tenants, fills, r0, r1, r2, r3, total)
    return total, token_gradient, grad_down, grad_up


def solution(mesh):
    placed = (
        P(("fsdp", "tok"), None),
        P(None, "fsdp"),
        P("tok", "fsdp"),
        P("tok", "fsdp"),
        P(("fsdp", "tok"), None),
        P(),
        P(),
    )
    return jax.shard_map(
        local,
        mesh=mesh,
        in_specs=placed,
        out_specs=(
            P(("fsdp", "tok"), None),
            P(("fsdp", "tok"), None),
            P("tok", "fsdp"),
            P("tok", "fsdp"),
        ),
        check_vma=False,
    )
```

```python
import functools

import jax
import jax.numpy as jnp
from jax import lax
from jax.experimental import pallas as pl
from jax.experimental.pallas import tpu as pltpu
from jax.sharding import PartitionSpec as P

ADAPTER_RANK = 16
BLOCK = 128
ADAPTER_SCALE = 2.0
CHUNKS = (4, 4)
VMEM_LIMIT = 24 * 1024 * 1024

F32 = jnp.float32
BF16 = jnp.bfloat16
NT = (((1,), (1,)), ((), ()))
TN = (((0,), (0,)), ((), ()))
SMEM = pl.BlockSpec(memory_space=pltpu.SMEM)
VMEM = pl.BlockSpec(memory_space=pltpu.VMEM)
ANY = pl.BlockSpec(memory_space=pl.ANY)


def dot(a, b, dims=(((1,), (0,)), ((), ()))):
    return lax.dot_general(a, b, dims, preferred_element_type=F32)


def block_rows(tenant_ref, block, shard, columns):
    base = tenant_ref[block] * ADAPTER_RANK - shard * columns
    lane = lax.broadcasted_iota(jnp.int32, (ADAPTER_RANK, columns), 1)
    row = lax.broadcasted_iota(jnp.int32, (ADAPTER_RANK, columns), 0)
    return jnp.where(lane - row == base, 1.0, 0.0)


def fill_pick(tenant_ref, pick_ref, row, first_block, count, shard):
    columns = pick_ref.shape[1]

    @pl.loop(0, count)
    def _(n):
        start = pl.multiple_of(row + n * ADAPTER_RANK, ADAPTER_RANK)
        rows = block_rows(tenant_ref, first_block + n, shard, columns)
        pick_ref[pl.ds(start, ADAPTER_RANK), :] = rows.astype(BF16)


def pick_two(group, tenant_ref, pick_ref, here, others):
    for place, other in enumerate(others):
        fill_pick(tenant_ref, pick_ref, place * group * ADAPTER_RANK, (here ^ other) * group, group, here)


def picked(pick_ref, down_ref, up_ref, out_ref):
    cut = down_ref.shape[0]
    out_ref[:, :cut] = dot(pick_ref[...], down_ref[...], NT).astype(BF16)
    out_ref[:, cut:] = dot(pick_ref[...], up_ref[...], NT).astype(BF16)


def send_select_kernel(group, where_ref, tenant_ref, down_ref, up_ref, out_ref, pick_ref):
    here, core = where_ref[0], where_ref[1]
    pick_two(group, tenant_ref, pick_ref, here, (1 + core, 3))
    picked(pick_ref, down_ref, up_ref, out_ref)


def keep_select_kernel(group, where_ref, tenant_ref, down_ref, up_ref, out_ref, pick_ref):
    here, core = where_ref[0], where_ref[1]
    pick_two(group, tenant_ref, pick_ref, here, (0, 2 - core))
    picked(pick_ref, down_ref, up_ref, out_ref)


def sum_two_kernel(kept_ref, came_ref, weight_ref, keep_ref, send_ref, piece_ref, sem):
    copy = pltpu.make_async_copy(weight_ref.at[pl.ds(0, piece_ref.shape[0]), :], piece_ref, sem)
    copy.start()
    rows = keep_ref.shape[0]
    send_ref[...] = kept_ref[rows:, :] + came_ref[rows:, :]
    keep_ref[...] = kept_ref[:rows, :] + came_ref[:rows, :]
    copy.wait()


def sum_kernel(start, keep_ref, came_ref, weight_ref, out_ref, piece_ref, sem):
    copy = pltpu.make_async_copy(weight_ref.at[pl.ds(start, piece_ref.shape[0]), :], piece_ref, sem)
    copy.start()
    out_ref[...] = keep_ref[...] + came_ref[...]
    copy.wait()


def cut_kernel(where_ref, near_ref, half_ref, sem):
    half = half_ref.shape[0]
    at = pl.multiple_of(where_ref[1] * half, half)
    copy = pltpu.make_async_copy(near_ref.at[pl.ds(at, half), :], half_ref, sem)
    copy.start()
    copy.wait()


def block_diagonal(a):
    own = (
        lax.broadcasted_iota(jnp.int32, a.shape, 0) // BLOCK
        == lax.broadcasted_iota(jnp.int32, a.shape, 1) // ADAPTER_RANK
    )
    return jnp.where(own, a, 0.0).astype(BF16)


def rank_kernel(
    where_ref, fill_ref, tokens_ref, cot_ref, maps_ref,
    grad_ref, rg_ref, at_ref, lora_ref, terms_ref, full_ref, up_ref
):
    rows, value = cot_ref.shape
    shards, _, both = maps_ref.shape
    cut = at_ref.shape[1] // shards
    width = both - cut
    wide = value // 4
    here, first = where_ref[0], where_ref[2]
    turned = [pl.ds(pl.multiple_of((here ^ n) * wide, wide), wide) for n in range(4)]
    for s in range(shards):
        full_ref[:, s * width : (s + 1) * width] = maps_ref[s, :, cut:]
        at_ref[:, s * cut : (s + 1) * cut] = maps_ref[s, :, :cut]
    for n, place in enumerate(turned):
        up_ref[:, n * wide : (n + 1) * wide] = full_ref[:, place]
        for block in range(rows // BLOCK):
            span = slice(block * BLOCK, (block + 1) * BLOCK)
            part = cot_ref[span, place]
            row = lax.broadcasted_iota(jnp.int32, part.shape, 0)
            grad_ref[span, n * wide : (n + 1) * wide] = jnp.where(
                row < fill_ref[first + block], part, jnp.zeros_like(part)
            )
    rank_grad = block_diagonal(ADAPTER_SCALE * dot(grad_ref[...], up_ref[...], NT))
    rg_ref[...] = rank_grad
    rank_in = block_diagonal(dot(tokens_ref[...], at_ref[...], NT))
    lora_ref[...] = (ADAPTER_SCALE * dot(rank_in, up_ref[...])).astype(BF16)
    up_terms = (ADAPTER_SCALE * dot(rank_in, grad_ref[...], TN)).astype(BF16)
    for n, place in enumerate(turned):
        full_ref[:, place] = up_terms[:, n * wide : (n + 1) * wide]
    for s in range(shards):
        terms_ref[s, :, :cut] = dot(rank_grad, tokens_ref[:, s * cut : (s + 1) * cut], TN).astype(BF16)
        terms_ref[s, :, cut:] = full_ref[:, s * width : (s + 1) * width]


def base_tile(core, tokens_ref, own, near, far, last, at_ref, grad_ref, rg_ref, out_ref, acc_ref):
    one, two = jnp.where(core == 0, near, far), jnp.where(core == 0, far, near)
    weight = jnp.concatenate([own, one, two, last], axis=1)
    back = dot(rg_ref[...], at_ref[...]).astype(BF16).astype(F32)
    out_ref[...] = (back + dot(grad_ref[...], weight, NT)).astype(BF16)
    acc_ref[...] += dot(tokens_ref[...], weight)


def base_kernel(
    steps, final, where_ref, fill_ref, tokens_ref, own_ref, near_ref, far_ref, mine_ref, theirs_ref,
    at_ref, grad_ref, rg_ref, sum_ref, *refs
):
    out_ref, total_ref = refs[-3:-1] if final else refs[-2:]
    acc_ref = refs[-1]
    i = pl.program_id(0)
    here, core, first = where_ref[0], where_ref[1], where_ref[2]

    @pl.when(i == 0)
    def _():
        acc_ref[...] = sum_ref[...].astype(F32)

    last = jnp.where(i < steps // 2, mine_ref[...], theirs_ref[...])
    base_tile(
        core, tokens_ref, own_ref[...], near_ref[...], far_ref[...], last,
        at_ref, grad_ref, rg_ref, out_ref, acc_ref,
    )

    if final:

        @pl.when(i == steps - 1)
        def _():
            wide = own_ref.shape[1]
            for n in range(total_ref.shape[0] // BLOCK):
                span = slice(n * BLOCK, (n + 1) * BLOCK)
                for other in range(total_ref.shape[1] // wide):
                    part = acc_ref[span, other * wide : (other + 1) * wide]
                    row = lax.broadcasted_iota(jnp.int32, part.shape, 0)
                    total_ref[span, pl.ds(pl.multiple_of((here ^ other) * wide, wide), wide)] = jnp.where(
                        row < fill_ref[first + n], part, 0.0
                    ).astype(BF16)


def fill_expand(tenant_ref, fill_ref, pick_ref, scale_ref, row, first, count, shard):
    columns = pick_ref.shape[1]

    @pl.loop(0, count)
    def _(n):
        start = pl.multiple_of(row + n * ADAPTER_RANK, ADAPTER_RANK)
        part = block_rows(tenant_ref, first + n, shard, columns)
        pick_ref[pl.ds(start, ADAPTER_RANK), :] = part.astype(BF16)
        scale_ref[...] += part * fill_ref[first + n].astype(F32)


def tenant_scale(scale_ref):
    return 1.0 / jnp.maximum(jnp.sum(scale_ref[...], axis=0, keepdims=True), 1.0)


def expand_kernel(
    group, where_ref, tenant_ref, fill_ref, r0_ref, r1_ref, r2_ref, r3_ref, down_ref, up_ref, pick_ref, scale_ref
):
    here, core = where_ref[0], where_ref[1]
    rows = group * ADAPTER_RANK
    scale_ref[...] = jnp.zeros_like(scale_ref)
    for place, other in enumerate((0, 1 + core, 2 - core, 3)):
        fill_expand(
            tenant_ref, fill_ref, pick_ref, scale_ref, place * rows, (here ^ other) * group, group, here
        )
    scale = tenant_scale(scale_ref)
    cut, both = down_ref.shape[0], r0_ref.shape[1]

    def means(lo, hi):
        terms = jnp.concatenate([ref[:, lo:hi] for ref in (r0_ref, r1_ref, r2_ref, r3_ref)], axis=0)
        return dot(terms, pick_ref[...], TN) * scale

    step = min(cut, 256)
    for lo in range(0, cut, step):
        down_ref[lo : lo + step, :] = means(lo, lo + step)
    up_ref[...] = means(cut, both)


def after(body, place, *tokens):
    return lambda *refs: body(*refs[:place], *refs[place + len(tokens) :])


def params(**extra):
    return pltpu.CompilerParams(vmem_limit_bytes=VMEM_LIMIT, **extra)


def shape(*dims, dtype=BF16):
    return jax.ShapeDtypeStruct(dims, dtype)


def local(tokens, weight, down_maps, up_maps, cotangent, tenants, fills):
    shards = lax.axis_size("tok")
    groups = lax.axis_size("fsdp")
    devices = groups * shards
    rows, model = tokens.shape
    value = cotangent.shape[1]
    wide = weight.shape[1]
    cut, columns = down_maps.shape
    width = up_maps.shape[0]
    dev_blocks = rows // BLOCK
    group = dev_blocks * shards
    rank = dev_blocks * ADAPTER_RANK
    group_rank = group * ADAPTER_RANK
    here = lax.axis_index("fsdp")
    tok_here = lax.axis_index("tok")
    core = tok_here % 2
    where = jnp.stack([here, core, (here * shards + tok_here) * dev_blocks, tok_here]).astype(jnp.int32)

    def on_core(a):
        return lax.ppermute(a, "tok", [(t, t ^ 1) for t in range(shards)])

    def split(first, second):
        pairs = [
            (f * shards + t, (f ^ (second if t % 2 else first)) * shards + t)
            for f in range(groups)
            for t in range(shards)
        ]
        return lambda a: lax.ppermute(a, ("fsdp", "tok"), pairs)

    first_way, second_way = split(1, 2), split(2, 1)

    def along_tok(a):
        return lax.all_to_all(a, "tok", split_axis=0, concat_axis=0)

    def call(body, out_shape, in_specs, name, scratch=(), out_specs=None, **extra):
        return pl.pallas_call(
            body,
            out_shape=out_shape,
            in_specs=in_specs,
            out_specs=out_specs or jax.tree.map(lambda _: VMEM, out_shape),
            scratch_shapes=list(scratch),
            compiler_params=params(),
            name=name,
            **extra,
        )

    parts = [(model // 8 * sum(CHUNKS[:k]), model // 8 * size) for k, size in enumerate(CHUNKS)]
    both = cut + width
    pick = pltpu.VMEM((2 * group_rank, columns), BF16)
    sent = call(
        functools.partial(send_select_kernel, group),
        shape(2 * group_rank, both),
        [SMEM, SMEM, VMEM, VMEM],
        "select_sent",
        [pick],
    )(where, tenants, down_maps, up_maps)
    came = first_way(sent)
    kept = call(
        after(functools.partial(keep_select_kernel, group), 4, sent),
        shape(2 * group_rank, both),
        [SMEM, SMEM, VMEM, VMEM, ANY],
        "select_kept",
        [pick],
    )(where, tenants, down_maps, up_maps, sent)
    keep, sent, piece = call(
        sum_two_kernel,
        [shape(group_rank, both)] * 2 + [shape(parts[0][1], wide)],
        [VMEM, VMEM, ANY],
        "sum_and_cut",
        [pltpu.SemaphoreType.DMA],
    )(kept, came, weight)
    maps, later = call(
        functools.partial(sum_kernel, parts[1][0]),
        [shape(group_rank, both), shape(parts[1][1], wide)],
        [VMEM, VMEM, ANY],
        "sum_and_cut",
        [pltpu.SemaphoreType.DMA],
    )(keep, second_way(sent), weight)
    maps = along_tok(maps.reshape(shards, rank, both))

    arrived = []

    def pass_after(a, *earlier):
        return call(
            lambda *refs: None,
            shape(*a.shape),
            [ANY] * (1 + len(earlier)),
            "pass_after",
            out_specs=ANY,
            input_output_aliases={0: 0},
        )(a, *earlier)

    def cut_chunk(piece, *earlier):
        near = first_way(piece)
        part = call(
            after(cut_kernel, 2, *earlier),
            shape(piece.shape[0] // 2, wide),
            [SMEM, ANY] + [ANY] * len(earlier),
            "cut_chunk",
            [pltpu.SemaphoreType.DMA],
        )(where, near, *earlier)
        near = pass_after(near, part)
        arrived.append((near, on_core(near), second_way(part)))
        return part

    part = cut_chunk(piece, maps)

    grad, rank_grad, at, lora, terms = call(
        after(rank_kernel, 5, part),
        [
            shape(rows, value),
            shape(rows, rank),
            shape(rank, model),
            shape(rows, value),
            shape(shards, rank, both),
        ],
        [SMEM, SMEM, VMEM, VMEM, VMEM, ANY],
        "rank_space",
        [pltpu.VMEM((rank, value), BF16)] * 2,
    )(where, fills, tokens, cotangent, maps, part)
    r0 = along_tok(terms).reshape(group_rank, both)

    whole = lambda i, *refs: (0, 0)
    along = lambda spot, tile: pl.BlockSpec((rows, tile), lambda i, *refs: (0, spot(i, *refs)))
    down = lambda spot, tile: pl.BlockSpec((tile, wide), lambda i, *refs: (spot(i, *refs), 0))
    resident = [
        pl.BlockSpec((rows, value), whole),
        pl.BlockSpec((rows, rank), whole),
        pl.BlockSpec((rows, value), whole),
    ]

    def cost(count):
        return pl.CostEstimate(
            flops=4 * rows * count * value,
            bytes_accessed=2 * count * (2 * rows + value) + 8 * rows * value,
            transcendentals=0,
        )

    tile = 512
    total, token_gradient = lora, None
    for k, (start, size) in enumerate(parts):
        final = k == len(parts) - 1
        steps = size // tile
        half = steps // 2
        part = None if final else cut_chunk(later, rank_grad, arrived[k][1])
        near, far, mine = arrived[k]
        mine = pass_after(mine, r0 if final else part)
        theirs = on_core(mine)
        turned = lambda i, w, f, half=half, steps=steps: (i + w[1] * half) % steps
        spot = lambda i, w, f, start=start, turned=turned: start // tile + turned(i, w, f)
        extra = [a for a in (token_gradient, part) if a is not None]
        token_gradient, total = pl.pallas_call(
            functools.partial(base_kernel, steps, final),
            out_shape=[shape(rows, model), shape(rows, value, dtype=BF16 if final else F32)],
            grid_spec=pltpu.PrefetchScalarGridSpec(
                num_scalar_prefetch=2,
                grid=(steps,),
                in_specs=[
                    along(spot, tile),
                    down(spot, tile),
                    down(turned, tile),
                    down(turned, tile),
                    down(lambda i, w, f, half=half: jnp.minimum(i, half - 1), tile),
                    down(lambda i, w, f, half=half: jnp.maximum(i - half, 0), tile),
                    pl.BlockSpec((rank, tile), lambda i, w, f, spot=spot: (0, spot(i, w, f))),
                ]
                + resident
                + [ANY] * len(extra),
                out_specs=[along(spot, tile), pl.BlockSpec((rows, value), whole)],
                scratch_shapes=[pltpu.VMEM((rows, value), F32)] if final else [],
            ),
            input_output_aliases={12: 0} if k else {},
            compiler_params=params(dimension_semantics=("arbitrary",)),
            cost_estimate=cost(size),
            name="base_chunk",
        )(where, fills, tokens, weight, near, far, mine, theirs, at, grad, rank_grad, total, *extra)
        if final:
            r1 = pass_after(r1, total)
            r3 = second_way(r1)
        else:
            r0 = pass_after(r0, total)
            r1, r2 = first_way(r0), second_way(r0)

    grad_down, grad_up = call(
        after(functools.partial(expand_kernel, group), 7, total),
        [shape(cut, columns, dtype=F32), shape(width, columns, dtype=F32)],
        [SMEM, SMEM, SMEM] + [VMEM] * 4 + [ANY],
        "expand",
        [pltpu.VMEM((devices * rank, columns), BF16), pltpu.VMEM((ADAPTER_RANK, columns), F32)],
    )(where, tenants, fills, r0, r1, r2, r3, total)
    return total, token_gradient, grad_down, grad_up


def solution(mesh):
    placed = (
        P(("fsdp", "tok"), None),
        P(None, "fsdp"),
        P("tok", "fsdp"),
        P("tok", "fsdp"),
        P(("fsdp", "tok"), None),
        P(),
        P(),
    )
    return jax.shard_map(
        local,
        mesh=mesh,
        in_specs=placed,
        out_specs=(
            P(("fsdp", "tok"), None),
            P(("fsdp", "tok"), None),
            P("tok", "fsdp"),
            P("tok", "fsdp"),
        ),
        check_vma=False,
    )
```

```python
import functools

import jax
import jax.numpy as jnp
from jax import lax
from jax.experimental import pallas as pl
from jax.experimental.pallas import tpu as pltpu
from jax.sharding import PartitionSpec as P

ADAPTER_RANK = 16
BLOCK = 128
ADAPTER_SCALE = 2.0
CHUNKS = (4, 4)
BASE_MIB = 40
MIB = 1024 * 1024

F32 = jnp.float32
BF16 = jnp.bfloat16
NT = (((1,), (1,)), ((), ()))
TN = (((0,), (0,)), ((), ()))
SMEM = pl.BlockSpec(memory_space=pltpu.SMEM)
VMEM = pl.BlockSpec(memory_space=pltpu.VMEM)
ANY = pl.BlockSpec(memory_space=pl.ANY)


def dot(a, b, dims=(((1,), (0,)), ((), ()))):
    return lax.dot_general(a, b, dims, preferred_element_type=F32)


def block_rows(tenant_ref, block, shard, columns):
    base = tenant_ref[block] * ADAPTER_RANK - shard * columns
    lane = lax.broadcasted_iota(jnp.int32, (ADAPTER_RANK, columns), 1)
    row = lax.broadcasted_iota(jnp.int32, (ADAPTER_RANK, columns), 0)
    return jnp.where(lane - row == base, 1.0, 0.0)


def fill_pick(tenant_ref, pick_ref, row, first_block, count, shard):
    columns = pick_ref.shape[1]

    @pl.loop(0, count)
    def _(n):
        start = pl.multiple_of(row + n * ADAPTER_RANK, ADAPTER_RANK)
        rows = block_rows(tenant_ref, first_block + n, shard, columns)
        pick_ref[pl.ds(start, ADAPTER_RANK), :] = rows.astype(BF16)


def pick_two(group, tenant_ref, pick_ref, here, others):
    for place, other in enumerate(others):
        fill_pick(tenant_ref, pick_ref, place * group * ADAPTER_RANK, (here ^ other) * group, group, here)


def picked(pick_ref, down_ref, up_ref, out_ref):
    cut = down_ref.shape[0]
    out_ref[:, :cut] = dot(pick_ref[...], down_ref[...], NT).astype(BF16)
    out_ref[:, cut:] = dot(pick_ref[...], up_ref[...], NT).astype(BF16)


def send_select_kernel(group, where_ref, tenant_ref, down_ref, up_ref, out_ref, pick_ref):
    here, core = where_ref[0], where_ref[1]
    pick_two(group, tenant_ref, pick_ref, here, (1 + core, 3))
    picked(pick_ref, down_ref, up_ref, out_ref)


def keep_select_kernel(group, where_ref, tenant_ref, down_ref, up_ref, out_ref, pick_ref):
    here, core = where_ref[0], where_ref[1]
    pick_two(group, tenant_ref, pick_ref, here, (0, 2 - core))
    picked(pick_ref, down_ref, up_ref, out_ref)


def sum_two_kernel(kept_ref, came_ref, weight_ref, keep_ref, send_ref, piece_ref, sem):
    copy = pltpu.make_async_copy(weight_ref.at[pl.ds(0, piece_ref.shape[0]), :], piece_ref, sem)
    copy.start()
    rows = keep_ref.shape[0]
    send_ref[...] = kept_ref[rows:, :] + came_ref[rows:, :]
    keep_ref[...] = kept_ref[:rows, :] + came_ref[:rows, :]
    copy.wait()


def sum_kernel(start, keep_ref, came_ref, weight_ref, out_ref, piece_ref, sem):
    copy = pltpu.make_async_copy(weight_ref.at[pl.ds(start, piece_ref.shape[0]), :], piece_ref, sem)
    copy.start()
    out_ref[...] = keep_ref[...] + came_ref[...]
    copy.wait()


def cut_kernel(where_ref, near_ref, half_ref, sem):
    half = half_ref.shape[0]
    at = pl.multiple_of(where_ref[1] * half, half)
    copy = pltpu.make_async_copy(near_ref.at[pl.ds(at, half), :], half_ref, sem)
    copy.start()
    copy.wait()


def block_diagonal(a):
    own = (
        lax.broadcasted_iota(jnp.int32, a.shape, 0) // BLOCK
        == lax.broadcasted_iota(jnp.int32, a.shape, 1) // ADAPTER_RANK
    )
    return jnp.where(own, a, 0.0).astype(BF16)


def rank_kernel(
    where_ref, fill_ref, tokens_ref, cot_ref, maps_ref,
    grad_ref, rg_ref, at_ref, lora_ref, terms_ref, full_ref, up_ref
):
    rows, value = cot_ref.shape
    shards, _, both = maps_ref.shape
    cut = at_ref.shape[1] // shards
    width = both - cut
    wide = value // 4
    here, first = where_ref[0], where_ref[2]
    turned = [pl.ds(pl.multiple_of((here ^ n) * wide, wide), wide) for n in range(4)]
    for s in range(shards):
        full_ref[:, s * width : (s + 1) * width] = maps_ref[s, :, cut:]
        at_ref[:, s * cut : (s + 1) * cut] = maps_ref[s, :, :cut]
    for n, place in enumerate(turned):
        up_ref[:, n * wide : (n + 1) * wide] = full_ref[:, place]
        for block in range(rows // BLOCK):
            span = slice(block * BLOCK, (block + 1) * BLOCK)
            part = cot_ref[span, place]
            row = lax.broadcasted_iota(jnp.int32, part.shape, 0)
            grad_ref[span, n * wide : (n + 1) * wide] = jnp.where(
                row < fill_ref[first + block], part, jnp.zeros_like(part)
            )
    rank_grad = block_diagonal(ADAPTER_SCALE * dot(grad_ref[...], up_ref[...], NT))
    rg_ref[...] = rank_grad
    rank_in = block_diagonal(dot(tokens_ref[...], at_ref[...], NT))
    lora_ref[...] = (ADAPTER_SCALE * dot(rank_in, up_ref[...])).astype(BF16)
    up_terms = (ADAPTER_SCALE * dot(rank_in, grad_ref[...], TN)).astype(BF16)
    for n, place in enumerate(turned):
        full_ref[:, place] = up_terms[:, n * wide : (n + 1) * wide]
    for s in range(shards):
        terms_ref[s, :, :cut] = dot(rank_grad, tokens_ref[:, s * cut : (s + 1) * cut], TN).astype(BF16)
        terms_ref[s, :, cut:] = full_ref[:, s * width : (s + 1) * width]


def base_tile(core, tokens_ref, own, near, far, last, at_ref, grad_ref, rg_ref, out_ref, acc_ref):
    one, two = jnp.where(core == 0, near, far), jnp.where(core == 0, far, near)
    weight = jnp.concatenate([own, one, two, last], axis=1)
    back = dot(rg_ref[...], at_ref[...]).astype(BF16).astype(F32)
    out_ref[...] = (back + dot(grad_ref[...], weight, NT)).astype(BF16)
    acc_ref[...] += dot(tokens_ref[...], weight)


def base_kernel(
    steps, final, where_ref, fill_ref, tokens_ref, own_ref, near_ref, far_ref, mine_ref, theirs_ref,
    at_ref, grad_ref, rg_ref, sum_ref, *refs
):
    out_ref, total_ref = refs[-3:-1] if final else refs[-2:]
    acc_ref = refs[-1]
    i = pl.program_id(0)
    here, core, first = where_ref[0], where_ref[1], where_ref[2]

    @pl.when(i == 0)
    def _():
        acc_ref[...] = sum_ref[...].astype(F32)

    last = jnp.where(i < steps // 2, mine_ref[...], theirs_ref[...])
    base_tile(
        core, tokens_ref, own_ref[...], near_ref[...], far_ref[...], last,
        at_ref, grad_ref, rg_ref, out_ref, acc_ref,
    )

    if final:

        @pl.when(i == steps - 1)
        def _():
            wide = own_ref.shape[1]
            for n in range(total_ref.shape[0] // BLOCK):
                span = slice(n * BLOCK, (n + 1) * BLOCK)
                for other in range(total_ref.shape[1] // wide):
                    part = acc_ref[span, other * wide : (other + 1) * wide]
                    row = lax.broadcasted_iota(jnp.int32, part.shape, 0)
                    total_ref[span, pl.ds(pl.multiple_of((here ^ other) * wide, wide), wide)] = jnp.where(
                        row < fill_ref[first + n], part, 0.0
                    ).astype(BF16)


def fill_expand(tenant_ref, fill_ref, pick_ref, scale_ref, row, first, count, shard):
    columns = pick_ref.shape[1]

    @pl.loop(0, count)
    def _(n):
        start = pl.multiple_of(row + n * ADAPTER_RANK, ADAPTER_RANK)
        part = block_rows(tenant_ref, first + n, shard, columns)
        pick_ref[pl.ds(start, ADAPTER_RANK), :] = part.astype(BF16)
        scale_ref[...] += part * fill_ref[first + n].astype(F32)


def tenant_scale(scale_ref):
    return 1.0 / jnp.maximum(jnp.sum(scale_ref[...], axis=0, keepdims=True), 1.0)


def expand_kernel(
    group, where_ref, tenant_ref, fill_ref, r0_ref, r1_ref, r2_ref, r3_ref, down_ref, up_ref, pick_ref, scale_ref
):
    here, core = where_ref[0], where_ref[1]
    rows = group * ADAPTER_RANK
    scale_ref[...] = jnp.zeros_like(scale_ref)
    for place, other in enumerate((0, 1 + core, 2 - core, 3)):
        fill_expand(
            tenant_ref, fill_ref, pick_ref, scale_ref, place * rows, (here ^ other) * group, group, here
        )
    scale = tenant_scale(scale_ref)
    cut, both = down_ref.shape[0], r0_ref.shape[1]

    def means(lo, hi):
        terms = jnp.concatenate([ref[:, lo:hi] for ref in (r0_ref, r1_ref, r2_ref, r3_ref)], axis=0)
        return dot(terms, pick_ref[...], TN) * scale

    step = min(cut, 256)
    for lo in range(0, cut, step):
        down_ref[lo : lo + step, :] = means(lo, lo + step)
    up_ref[...] = means(cut, both)


def after(body, place, *tokens):
    return lambda *refs: body(*refs[:place], *refs[place + len(tokens) :])


def params(mib, **extra):
    return pltpu.CompilerParams(vmem_limit_bytes=mib * MIB, **extra)


def shape(*dims, dtype=BF16):
    return jax.ShapeDtypeStruct(dims, dtype)


def local(tokens, weight, down_maps, up_maps, cotangent, tenants, fills):
    shards = lax.axis_size("tok")
    groups = lax.axis_size("fsdp")
    devices = groups * shards
    rows, model = tokens.shape
    value = cotangent.shape[1]
    wide = weight.shape[1]
    cut, columns = down_maps.shape
    width = up_maps.shape[0]
    dev_blocks = rows // BLOCK
    group = dev_blocks * shards
    rank = dev_blocks * ADAPTER_RANK
    group_rank = group * ADAPTER_RANK
    here = lax.axis_index("fsdp")
    tok_here = lax.axis_index("tok")
    core = tok_here % 2
    where = jnp.stack([here, core, (here * shards + tok_here) * dev_blocks, tok_here]).astype(jnp.int32)

    def on_core(a):
        return lax.ppermute(a, "tok", [(t, t ^ 1) for t in range(shards)])

    def split(first, second):
        pairs = [
            (f * shards + t, (f ^ (second if t % 2 else first)) * shards + t)
            for f in range(groups)
            for t in range(shards)
        ]
        return lambda a: lax.ppermute(a, ("fsdp", "tok"), pairs)

    first_way, second_way = split(1, 2), split(2, 1)

    def along_tok(a):
        return lax.all_to_all(a, "tok", split_axis=0, concat_axis=0)

    def call(body, out_shape, in_specs, name, scratch=(), out_specs=None, mib=24, **extra):
        return pl.pallas_call(
            body,
            out_shape=out_shape,
            in_specs=in_specs,
            out_specs=out_specs or jax.tree.map(lambda _: VMEM, out_shape),
            scratch_shapes=list(scratch),
            compiler_params=params(mib),
            name=name,
            **extra,
        )

    parts = [(model // 8 * sum(CHUNKS[:k]), model // 8 * size) for k, size in enumerate(CHUNKS)]
    both = cut + width
    pick = pltpu.VMEM((2 * group_rank, columns), BF16)
    sent = call(
        functools.partial(send_select_kernel, group),
        shape(2 * group_rank, both),
        [SMEM, SMEM, VMEM, VMEM],
        "select_sent",
        [pick],
    )(where, tenants, down_maps, up_maps)
    came = first_way(sent)
    kept = call(
        after(functools.partial(keep_select_kernel, group), 4, sent),
        shape(2 * group_rank, both),
        [SMEM, SMEM, VMEM, VMEM, ANY],
        "select_kept",
        [pick],
    )(where, tenants, down_maps, up_maps, sent)
    keep, sent, piece = call(
        sum_two_kernel,
        [shape(group_rank, both)] * 2 + [shape(parts[0][1], wide)],
        [VMEM, VMEM, ANY],
        "sum_and_cut",
        [pltpu.SemaphoreType.DMA],
        mib=12,
    )(kept, came, weight)
    maps, later = call(
        functools.partial(sum_kernel, parts[1][0]),
        [shape(group_rank, both), shape(parts[1][1], wide)],
        [VMEM, VMEM, ANY],
        "sum_and_cut",
        [pltpu.SemaphoreType.DMA],
        mib=12,
    )(keep, second_way(sent), weight)
    maps = along_tok(maps.reshape(shards, rank, both))

    arrived = []

    def pass_after(a, *earlier):
        return call(
            lambda *refs: None,
            shape(*a.shape),
            [ANY] * (1 + len(earlier)),
            "pass_after",
            out_specs=ANY,
            input_output_aliases={0: 0},
            mib=8,
        )(a, *earlier)

    def cut_chunk(piece, *earlier):
        near = first_way(piece)
        part = call(
            after(cut_kernel, 2, *earlier),
            shape(piece.shape[0] // 2, wide),
            [SMEM, ANY] + [ANY] * len(earlier),
            "cut_chunk",
            [pltpu.SemaphoreType.DMA],
            mib=8,
        )(where, near, *earlier)
        near = pass_after(near, part)
        arrived.append((near, on_core(near), second_way(part)))
        return part

    part = cut_chunk(piece, maps)

    grad, rank_grad, at, lora, terms = call(
        after(rank_kernel, 5, part),
        [
            shape(rows, value),
            shape(rows, rank),
            shape(rank, model),
            shape(rows, value),
            shape(shards, rank, both),
        ],
        [SMEM, SMEM, VMEM, VMEM, VMEM, ANY],
        "rank_space",
        mib=24,
        scratch=[pltpu.VMEM((rank, value), BF16)] * 2,
    )(where, fills, tokens, cotangent, maps, part)
    r0 = along_tok(terms).reshape(group_rank, both)
    r1, r2 = first_way(r0), second_way(r0)

    whole = lambda i, *refs: (0, 0)
    along = lambda spot, tile: pl.BlockSpec((rows, tile), lambda i, *refs: (0, spot(i, *refs)))
    down = lambda spot, tile: pl.BlockSpec((tile, wide), lambda i, *refs: (spot(i, *refs), 0))
    resident = [
        pl.BlockSpec((rows, value), whole),
        pl.BlockSpec((rows, rank), whole),
        pl.BlockSpec((rows, value), whole),
    ]

    def cost(count):
        return pl.CostEstimate(
            flops=4 * rows * count * value,
            bytes_accessed=2 * count * (2 * rows + value) + 8 * rows * value,
            transcendentals=0,
        )

    tile = 512
    total, token_gradient = lora, None
    for k, (start, size) in enumerate(parts):
        final = k == len(parts) - 1
        steps = size // tile
        half = steps // 2
        part = None if final else cut_chunk(later, rank_grad, arrived[k][1])
        near, far, mine = arrived[k]
        mine = pass_after(mine, r0)
        theirs = on_core(mine)
        if final:
            r1 = pass_after(r1, total)
            r3 = second_way(r1)
        turned = lambda i, w, f, half=half, steps=steps: (i + w[1] * half) % steps
        spot = lambda i, w, f, start=start, turned=turned: start // tile + turned(i, w, f)
        extra = [a for a in (token_gradient, part, *((r1, r2) if final else ())) if a is not None]
        token_gradient, total = pl.pallas_call(
            functools.partial(base_kernel, steps, final),
            out_shape=[shape(rows, model), shape(rows, value, dtype=BF16 if final else F32)],
            grid_spec=pltpu.PrefetchScalarGridSpec(
                num_scalar_prefetch=2,
                grid=(steps,),
                in_specs=[
                    along(spot, tile),
                    down(spot, tile),
                    down(turned, tile),
                    down(turned, tile),
                    down(lambda i, w, f, half=half: jnp.minimum(i, half - 1), tile),
                    down(lambda i, w, f, half=half: jnp.maximum(i - half, 0), tile),
                    pl.BlockSpec((rank, tile), lambda i, w, f, spot=spot: (0, spot(i, w, f))),
                ]
                + resident
                + [ANY] * len(extra),
                out_specs=[along(spot, tile), pl.BlockSpec((rows, value), whole)],
                scratch_shapes=[pltpu.VMEM((rows, value), F32)] if final else [],
            ),
            input_output_aliases={12: 0} if k else {},
            compiler_params=params(BASE_MIB, dimension_semantics=("arbitrary",)),
            cost_estimate=cost(size),
            name="base_chunk",
        )(where, fills, tokens, weight, near, far, mine, theirs, at, grad, rank_grad, total, *extra)

    grad_down, grad_up = call(
        after(functools.partial(expand_kernel, group), 7, total),
        [shape(cut, columns, dtype=F32), shape(width, columns, dtype=F32)],
        [SMEM, SMEM, SMEM] + [VMEM] * 4 + [ANY],
        "expand",
        [pltpu.VMEM((devices * rank, columns), BF16), pltpu.VMEM((ADAPTER_RANK, columns), F32)],
    )(where, tenants, fills, r0, r1, r2, r3, total)
    return total, token_gradient, grad_down, grad_up


def solution(mesh):
    placed = (
        P(("fsdp", "tok"), None),
        P(None, "fsdp"),
        P("tok", "fsdp"),
        P("tok", "fsdp"),
        P(("fsdp", "tok"), None),
        P(),
        P(),
    )
    return jax.shard_map(
        local,
        mesh=mesh,
        in_specs=placed,
        out_specs=(
            P(("fsdp", "tok"), None),
            P(("fsdp", "tok"), None),
            P("tok", "fsdp"),
            P("tok", "fsdp"),
        ),
        check_vma=False,
    )
```
